32 devices in a mesh: dp: 8 (over z, x), seq: 4 (over y, core).
Axes of the slice: x: 2, y: 2, z: 4, core: 2. Of those that a mesh axis runs over, the one named last changes fastest.
Arguments:
- inputs: bfloat16 [64, 512, 768], P('dp', 'seq'), may hold values from -6 to 6
- lengths: int32 [64], P('dp'), may hold values from 1 to 512, as said below
- query_key_value_weight: bfloat16 [768, 2304], P(('dp', 'seq')), may hold values from -0.21875 to 0.21875
- query_bias: bfloat16 [768], P(('dp', 'seq')), may hold values from -3 to 3
- value_bias: bfloat16 [768], P(('dp', 'seq')), may hold values from -0.29882812 to 0.29882812
- output_weight: bfloat16 [768, 768], P(('dp', 'seq')), may hold values from -1.75 to 1.75
- output_bias: bfloat16 [768], P(('dp', 'seq')), may hold values from -1.1953125 to 1.1953125
- norm1_gain: bfloat16 [768], P(('dp', 'seq')), may hold values from 0.5 to 1.5
- norm1_shift: bfloat16 [768], P(('dp', 'seq')), may hold values from -1.1953125 to 1.1953125
- in_weight: bfloat16 [768, 3072], P(('dp', 'seq')), may hold values from -0.21875 to 0.21875
- in_bias: bfloat16 [3072], P(('dp', 'seq')), may hold values from -1.1953125 to 1.1953125
- down_weight: bfloat16 [3072, 768], P(('dp', 'seq')), may hold values from -0.109375 to 0.109375
- down_bias: bfloat16 [768], P(('dp', 'seq')), may hold values from -1.1953125 to 1.1953125
- norm2_gain: bfloat16 [768], P(('dp', 'seq')), may hold values from 0.5 to 1.5
- norm2_shift: bfloat16 [768], P(('dp', 'seq')), may hold values from -1.1953125 to 1.1953125
- cotangent: bfloat16 [64, 512, 768], P('dp', 'seq'), may hold values from -6 to 6
Outputs:
- outputs: bfloat16 [64, 512, 768], P('dp', 'seq')
- grad_inputs: bfloat16 [64, 512, 768], P('dp', 'seq')
- grad_qkv_weight: float32 [768, 2304], P(('dp', 'seq'))
- grad_query_bias: float32 [768], P(('dp', 'seq'))
- grad_value_bias: float32 [768], P(('dp', 'seq'))
- grad_out_weight: float32 [768, 768], P(('dp', 'seq'))
- grad_out_bias: float32 [768], P(('dp', 'seq'))
- grad_norm1_gain: float32 [768], P(('dp', 'seq'))
- grad_norm1_shift: float32 [768], P(('dp', 'seq'))
- grad_in_weight: float32 [768, 3072], P(('dp', 'seq'))
- grad_in_bias: float32 [3072], P(('dp', 'seq'))
- grad_down_weight: float32 [3072, 768], P(('dp', 'seq'))
- grad_down_bias: float32 [768], P(('dp', 'seq'))
- grad_norm2_gain: float32 [768], P(('dp', 'seq'))
- grad_norm2_shift: float32 [768], P(('dp', 'seq'))
The draws below stay inside these ranges and needn't reach their ends.
Inputs may be any that keep to these rules, and one draw needn't show every extreme that they name: `lengths`: in each aligned block of 8 sequences, one drawn from the seed has length 512.
All inputs are finite; a program needn't handle non-finite values.
Results may differ from the reference program's by a relative error of at most 0.017.
Values may be sent and summed in bfloat16 or wider, within the bound.
No kernel may reach another device: no remote copies, remote signals or barrier semaphores. Data moves between devices by JAX's collectives and lax.ppermute only.
A program may use at most 192 MiB of HBM per device.

```python
import jax
import jax.numpy as jnp
from jax import lax

D = 768
HEADS = 12
HD = 64
FF = 3072
SEQ_GRP = 8
LEN = 512
SEQS = 64


def draw_lengths(key, part):
    key = jax.random.fold_in(key, 7)
    first, second = jax.random.split(key)
    sizes = jax.random.randint(first, (SEQS,), 1, LEN + 1)
    picked = jax.random.randint(second, (SEQS // SEQ_GRP,), 0, SEQ_GRP)
    places = jnp.arange(SEQS, dtype=jnp.int32) % SEQ_GRP
    full = places == jnp.repeat(picked, SEQ_GRP, total_repeat_length=SEQS)
    return jnp.where(full, LEN, sizes).astype(jnp.int32)


def raised(drawn, stream_key, source, target, parts, factor):
    def block_of(position):
        return (jnp.arange(drawn.shape[position]) // (drawn.shape[position] // parts)).reshape((-1,) + (1,) * (drawn.ndim - 1 - position))

    first = jax.random.permutation(stream_key, parts)[block_of(target)]
    far = (block_of(target) + parts // 2) % parts
    return jnp.where((block_of(source) == first) | (block_of(source) == far), factor * drawn, drawn)


def level_of(stream_key, dims, cuts, smallest, high):
    factor_of = 1.0
    for position, blocks in cuts:
        heights = jax.random.uniform(jax.random.fold_in(jax.random.fold_in(stream_key, 6), position), (blocks,), jnp.float32, smallest / len(cuts), high / len(cuts))
        factor_of = factor_of * jnp.repeat(jnp.exp(heights), dims[position] // blocks).reshape((-1,) + (1,) * (len(dims) - 1 - position))
    return factor_of


def scatter_about(stream_key, extent, scale, reach, shards=(), held_as=jnp.bfloat16):
    values = scale * jax.random.normal(stream_key, extent, jnp.float32)
    if shards:
        values = values * level_of(stream_key, extent, shards, -0.22, 0.18)
    return jnp.clip(values, -reach, reach).astype(held_as)


def heavy_noise(stream_key, dims, deviation, most, cuts, heavy, held_as=jnp.bfloat16):
    entries = deviation * jax.random.normal(stream_key, dims, jnp.float32)
    if cuts:
        entries = entries * level_of(stream_key, dims, cuts, -0.22, 0.18)
    return jnp.clip(raised(entries, jax.random.fold_in(stream_key, 3), *heavy), -most, most).astype(held_as)


def setup_inputs(seed: int = 0) -> dict:
    streams_of = jax.random.split(jax.random.key(seed), 17)
    return {
        "inputs": heavy_noise(streams_of[0], (SEQS, LEN, D), 1.0, 6.0, ((0, 8), (1, 4)), (0, 2, 8, 2.0)),
        "lengths": draw_lengths(jax.random.fold_in(streams_of[16], 71), 0),
        "query_key_value_weight": scatter_about(streams_of[2], (D, 3 * D), D ** -0.5, 0.21875, ((0, 32),)),
        "query_bias": scatter_about(streams_of[3], (D,), 0.5, 3.0, ((0, 32),)),
        "value_bias": scatter_about(streams_of[4], (D,), 0.05, 0.29882812, ((0, 32),)),
        "output_weight": scatter_about(streams_of[5], (D, D), (D // 64) ** -0.5, 1.75, ((0, 32),)),
        "output_bias": scatter_about(streams_of[6], (D,), 0.2, 1.1953125, ((0, 32),)),
        "norm1_gain": jnp.clip(0.5 + 1.0 * jax.random.uniform(streams_of[7], (D,), jnp.float32) ** level_of(streams_of[7], (D,), ((0, 32),), -0.2, 0.2), 0.5, 1.5).astype(jnp.bfloat16),
        "norm1_shift": scatter_about(streams_of[8], (D,), 0.2, 1.1953125, ((0, 32),)),
        "in_weight": scatter_about(streams_of[9], (D, FF), D ** -0.5, 0.21875, ((0, 32),)),
        "in_bias": scatter_about(streams_of[10], (FF,), 0.2, 1.1953125, ((0, 32),)),
        "down_weight": scatter_about(streams_of[11], (FF, D), FF ** -0.5, 0.109375, ((0, 32),)),
        "down_bias": scatter_about(streams_of[12], (D,), 0.2, 1.1953125, ((0, 32),)),
        "norm2_gain": jnp.clip(0.5 + 1.0 * jax.random.uniform(streams_of[13], (D,), jnp.float32) ** level_of(streams_of[13], (D,), ((0, 32),), -0.2, 0.2), 0.5, 1.5).astype(jnp.bfloat16),
        "norm2_shift": scatter_about(streams_of[14], (D,), 0.2, 1.1953125, ((0, 32),)),
        "cotangent": scatter_about(streams_of[15], (SEQS, LEN, D), 1.0, 6.0, ((0, 8), (1, 4))),
    }


@jax.custom_vjp
def low(v):
    return lax.optimization_barrier(v.astype(jnp.bfloat16)).astype(jnp.float32)

@jax.custom_vjp
def reduced_backward(v):
    return v

def low_keep(v):
    return (low(v), None)

def low_pass(kept, grad):
    return (grad,)

def back_keep(v):
    return (v, None)

def back_low(kept, grad):
    return (low(grad),)
low.defvjp(low_keep, low_pass)
reduced_backward.defvjp(back_keep, back_low)
highest_precision = lax.Precision.HIGHEST
epsilon = 1e-12

def layer_norm(value, gain, shift):
    center = lax.optimization_barrier(jnp.mean(value, -1, keepdims=True))
    centered = value - center
    spread = lax.optimization_barrier(jnp.mean(centered * centered, -1, keepdims=True))
    return centered * lax.rsqrt(spread + epsilon) * gain + shift

def attend(item):
    queries, keys, values, limit = item
    query_heads = queries.reshape(LEN, HEADS, HD)
    key_heads = keys.reshape(LEN, HEADS, HD)
    value_heads = values.reshape(LEN, HEADS, HD)
    scores = reduced_backward(jnp.einsum('qhd,khd->hqk', query_heads, key_heads, precision=highest_precision) * 0.125)
    valid = jnp.arange(LEN, dtype=jnp.int32) < limit
    scores = jnp.where(valid[None, None, :], scores, -1e+30)
    probs = low(jax.nn.softmax(scores, axis=-1))
    return jnp.einsum('hqk,khd->qhd', probs, value_heads, precision=highest_precision).reshape(LEN, D)

def layer(params, inputs, lengths):
    query_key_value_weight, query_bias, value_bias, output_weight, output_bias, norm1_gain, norm1_shift, in_weight, in_bias, down_weight, down_bias, norm2_gain, norm2_shift = params
    bias_vector = jnp.concatenate([query_bias, jnp.zeros_like(query_bias), value_bias])
    packed_tokens = jnp.einsum('cfu,ut->cft', inputs, query_key_value_weight, precision=highest_precision) + bias_vector
    packed_tokens = reduced_backward(low(packed_tokens))
    queries = packed_tokens[..., :D]
    keys = packed_tokens[..., D:2 * D]
    values = packed_tokens[..., 2 * D:]
    mixed_heads = lax.map(jax.checkpoint(attend), (queries, keys, values, lengths))
    mixed_heads = reduced_backward(low(mixed_heads))
    attention_branch = reduced_backward(jnp.einsum('cfu,ut->cft', mixed_heads, output_weight, precision=highest_precision) + output_bias)
    first = low(layer_norm(inputs + attention_branch, norm1_gain, norm1_shift))
    hidden = reduced_backward(jnp.einsum('snd,df->snf', first, in_weight, precision=highest_precision) + in_bias)
    active = low(jax.nn.gelu(hidden, approximate=False))
    branch_two = reduced_backward(jnp.einsum('snf,fd->snd', active, down_weight, precision=highest_precision) + down_bias)
    return layer_norm(first + branch_two, norm2_gain, norm2_shift)

def reference(inputs, lengths, query_key_value_weight, query_bias, value_bias, output_weight, output_bias, norm1_gain, norm1_shift, in_weight, in_bias, down_weight, down_bias, norm2_gain, norm2_shift, cotangent):
    params = tuple((weight.astype(jnp.float32) for weight in (query_key_value_weight, query_bias, value_bias, output_weight, output_bias, norm1_gain, norm1_shift, in_weight, in_bias, down_weight, down_bias, norm2_gain, norm2_shift)))
    blocks = SEQS // SEQ_GRP

    def step(totals, item):
        block_in, block_len, block_cot = item

        def forward(weights, values):
            return layer(weights, values, block_len)
        result, pull = jax.vjp(forward, params, block_in.astype(jnp.float32))
        grad_params, grad_in = pull(block_cot.astype(jnp.float32))
        totals = jax.tree.map(jnp.add, totals, grad_params)
        return (totals, (result.astype(jnp.bfloat16), grad_in.astype(jnp.bfloat16)))
    zeros = jax.tree.map(jnp.zeros_like, params)
    totals, (results, grads) = lax.scan(step, zeros, (inputs.reshape(blocks, SEQ_GRP, LEN, D), lengths.reshape(blocks, SEQ_GRP).astype(jnp.int32), cotangent.reshape(blocks, SEQ_GRP, LEN, D)))
    return (results.reshape(SEQS, LEN, D), grads.reshape(SEQS, LEN, D), totals[0], totals[1], totals[2], totals[3], totals[4], totals[5], totals[6], totals[7], totals[8], totals[9], totals[10], totals[11], totals[12])
```

```python
import functools

import jax
import jax.numpy as jnp
from jax import lax
from jax.experimental import pallas as pl
from jax.experimental.pallas import tpu as pltpu
from jax.sharding import PartitionSpec as P

BF = jnp.bfloat16
F32 = jnp.float32
HD = 64
BOTH = ("dp", "seq")

def layer_norm(value, gain, shift):
    center = jnp.mean(value, -1, keepdims=True)
    centered = value - center
    spread = jnp.mean(centered * centered, -1, keepdims=True)
    return centered * lax.rsqrt(spread + 1e-12) * gain + shift


def gelu_exact(value):
    return jax.nn.gelu(value, approximate=False)


def over_rows(left, right):
    return lax.dot_general(
        left, right, (((0,), (0,)), ((), ())), preferred_element_type=jnp.float32
    )


def times_transposed(left, right):
    return lax.dot_general(
        left, right, (((1,), (1,)), ((), ())), preferred_element_type=jnp.float32
    )


def nt(a,b): return lax.dot_general(a,b,(((1,),(1,)),((),())),preferred_element_type=F32)
def tn(a,b): return lax.dot_general(a,b,(((0,),(0,)),((),())),preferred_element_type=F32)
def nn(a,b): return lax.dot_general(a,b,(((1,),(0,)),((),())),preferred_element_type=F32)

def masked_pair(q, k, bias, head, lane):
    mine = (lane >= head*HD) & (lane < (head+1)*HD)
    spare = lane == (HD if head==0 else 0)
    zero=jnp.zeros((),BF)
    qh = jnp.where(mine, q*BF(0.125), jnp.where(spare, jnp.ones((),BF), zero))
    kh = jnp.where(mine, k, jnp.where(spare, bias, zero))
    return qh, kh

def fwd_kernel(cq, q_ref,k_ref,v_ref,b_ref,o_ref,lse_ref):
    n=q_ref.shape[0]
    lane=lax.broadcasted_iota(jnp.int32,(n,128),1)
    q=q_ref[...]; k=k_ref[...]; v=v_ref[...]; bias=b_ref[0]
    pairs=[masked_pair(q,k,bias,h,lane) for h in range(2)]
    for c in range(n//cq):
        sl=slice(c*cq,(c+1)*cq)
        halves=[]
        for h in range(2):
            qh,kh=pairs[h]
            s=nt(kh,qh[sl])
            m=jnp.max(s,0,keepdims=True)
            e=jnp.exp(s-m)
            l=jnp.sum(e,0,keepdims=True)
            ot=tn(v[:,h*HD:(h+1)*HD],e.astype(BF))
            halves.append(ot*(1.0/l))
            lse_ref[0,h:h+1,sl]=m+jnp.log(l)
        o_ref[sl,:]=jnp.concatenate(halves,0).T.astype(BF)

def bwd_kernel(cq, q_ref,k_ref,v_ref,b_ref,lse_ref,g_ref,dq_ref,dk_ref,dv_ref):
    n=q_ref.shape[0]
    lane=lax.broadcasted_iota(jnp.int32,(n,128),1)
    q=q_ref[...]; k=k_ref[...]; v=v_ref[...]; bias=b_ref[0]; g=g_ref[...]
    qs=q*BF(0.125); ks=k*BF(0.125)
    zero=jnp.zeros((),BF)
    dks=[];dvs=[]
    dq=[[None,None] for _ in range(n//cq)]
    for h in range(2):
        qh,kh=masked_pair(q,k,bias,h,lane)
        mine = (lane >= h*HD) & (lane < (h+1)*HD)
        vh=jnp.where(mine,v,zero)
        kth=ks[:,h*HD:(h+1)*HD]
        dk=dv=None
        for c in range(n//cq):
            sl=slice(c*cq,(c+1)*cq)
            s=nt(kh,qh[sl])
            p=jnp.exp(s-lse_ref[0,h:h+1,sl])
            gp=nt(vh,g[sl])
            inner=jnp.sum(p*gp,0,keepdims=True)
            ds=(p*(gp-inner)).astype(BF)
            a=nn(p.astype(BF),g[sl]); b=nn(ds,qs[sl])
            dv=a if dv is None else dv+a
            dk=b if dk is None else dk+b
            dq[c][h]=tn(kth,ds)
        dks.append(dk);dvs.append(dv)
    for c in range(n//cq):
        sl=slice(c*cq,(c+1)*cq)
        dq_ref[sl,:]=jnp.concatenate(dq[c],0).T.astype(BF)
    first=lane<HD
    dk_ref[...]=jnp.where(first,dks[0],dks[1]).astype(BF)
    dv_ref[...]=jnp.where(first,dvs[0],dvs[1]).astype(BF)

def attention_forward(packed,bias,length,cq=512):
    rows,wide=packed.shape; width=wide//3; pairs=width//128; seqs=rows//length
    blk=lambda off: pl.BlockSpec((length,128),lambda s,p:(s,off*pairs+p))
    return pl.pallas_call(functools.partial(fwd_kernel,cq),grid=(seqs,pairs),
      in_specs=[blk(0),blk(1),blk(2),pl.BlockSpec((1,length,128),lambda s,p:(s,0,0))],
      out_specs=[blk(0),pl.BlockSpec((1,2,length),lambda s,p:(s*pairs+p,0,0))],
      out_shape=[jax.ShapeDtypeStruct((rows,width),BF),jax.ShapeDtypeStruct((seqs*pairs,2,length),F32)],
      compiler_params=pltpu.CompilerParams(vmem_limit_bytes=48*2**20),name="attention_forward",
      cost_estimate=pl.CostEstimate(flops=4*rows*length*width,bytes_accessed=rows*width*8,transcendentals=rows*length*width//HD))(packed,packed,packed,bias)

def attention_backward(packed,bias,lse,grad,length,cq=512):
    rows,wide=packed.shape; width=wide//3; pairs=width//128; seqs=rows//length
    blk=lambda off: pl.BlockSpec((length,128),lambda s,p:(s,off*pairs+p))
    o=jax.ShapeDtypeStruct((rows,width),BF)
    return pl.pallas_call(functools.partial(bwd_kernel,cq),grid=(seqs,pairs),
      in_specs=[blk(0),blk(1),blk(2),pl.BlockSpec((1,length,128),lambda s,p:(s,0,0)),pl.BlockSpec((1,2,length),lambda s,p:(s*pairs+p,0,0)),blk(0)],
      out_specs=[blk(0)]*3,out_shape=[o,o,o],
      compiler_params=pltpu.CompilerParams(vmem_limit_bytes=48*2**20),name="attention_backward",
      cost_estimate=pl.CostEstimate(flops=10*rows*length*width,bytes_accessed=rows*width*14,transcendentals=rows*length*width//HD))(packed,packed,packed,bias,lse,grad)

def to_sequences(block):
    return lax.all_to_all(block, "seq", 0, 1, tiled=True)


def to_positions(block):
    return lax.all_to_all(block, "seq", 1, 0, tiled=True)


def gather_rows(block):
    return lax.all_gather(block, BOTH, axis=0, tiled=True)


def on_device(
    inputs,
    lengths,
    query_key_value_weight,
    query_bias,
    value_bias,
    output_weight,
    output_bias,
    norm1_gain,
    norm1_shift,
    in_weight,
    in_bias,
    down_weight,
    down_bias,
    norm2_gain,
    norm2_shift,
    cotangent,
):
    groups, local_len, width = inputs.shape
    rows = groups * local_len
    members = lax.axis_size("seq")
    devices = lax.axis_size("dp") * members
    kept = groups // members
    length = local_len * members
    flat = to_sequences(inputs).reshape(rows, width)
    wide_qkv = gather_rows(query_key_value_weight)
    vectors = (
        query_bias,
        value_bias,
        output_bias,
        norm1_gain,
        norm1_shift,
        in_bias,
        down_bias,
        norm2_gain,
        norm2_shift,
    )
    sizes = [v.shape[0] for v in vectors]
    gathered = gather_rows(jnp.concatenate(vectors)[None])
    full = []
    at = 0
    for size in sizes:
        full.append(gathered[:, at : at + size].reshape(-1).astype(F32))
        at += size
    (
        full_query_bias,
        full_value_bias,
        full_out_bias,
        gain_one,
        shift_one,
        full_in_bias,
        full_down_bias,
        gain_two,
        shift_two,
    ) = full
    wide_out = gather_rows(output_weight)
    wide_in = gather_rows(in_weight)
    wide_down = gather_rows(down_weight)
    cot = to_sequences(cotangent).reshape(rows, width)
    bias_vector = jnp.concatenate([full_query_bias, jnp.zeros((width,), F32), full_value_bias])
    packed = (jnp.dot(flat, wide_qkv, preferred_element_type=F32) + bias_vector).astype(BF)
    mine = lax.dynamic_slice(lengths, (lax.axis_index("seq") * kept,), (kept,))
    positions = jnp.arange(length, dtype=jnp.int32)
    mask = jnp.where(positions[None, :] < mine[:, None], 0.0, -1e30).astype(BF)
    mask = jnp.broadcast_to(mask[:, :, None], (kept, length, 128))
    mixed, logsum = attention_forward(packed, mask, length)
    attention_branch = jnp.dot(mixed, wide_out, preferred_element_type=F32) + full_out_bias
    first, norm_one_pull = jax.vjp(
        layer_norm, flat.astype(F32) + attention_branch, gain_one, shift_one
    )
    first_low = first.astype(BF)
    hidden = jnp.dot(first_low, wide_in, preferred_element_type=F32) + full_in_bias
    active, gelu_pull = jax.vjp(gelu_exact, hidden)
    active_low = active.astype(BF)
    branch_two = jnp.dot(active_low, wide_down, preferred_element_type=F32) + full_down_bias
    result, norm_two_pull = jax.vjp(
        layer_norm, first_low.astype(F32) + branch_two, gain_two, shift_two
    )
    outputs = to_positions(result.astype(BF).reshape(kept, length, width))
    grad_second, grad_gain_two, grad_shift_two = norm_two_pull(cot.astype(F32))
    grad_branch_two = grad_second.astype(BF)
    grad_down = over_rows(active_low, grad_branch_two)
    grad_down_bias = jnp.sum(grad_branch_two.astype(F32), 0)
    (grad_hidden,) = gelu_pull(times_transposed(grad_branch_two, wide_down))
    grad_hidden_low = grad_hidden.astype(BF)
    grad_in = over_rows(first_low, grad_hidden_low)
    grad_in_bias = jnp.sum(grad_hidden_low.astype(F32), 0)
    grad_first = times_transposed(grad_hidden_low, wide_in) + grad_second
    grad_residual, grad_gain_one, grad_shift_one = norm_one_pull(grad_first)
    grad_branch_one = grad_residual.astype(BF)
    grad_out = over_rows(mixed, grad_branch_one)
    grad_out_bias = jnp.sum(grad_branch_one.astype(F32), 0)
    grad_mixed = times_transposed(grad_branch_one, wide_out).astype(BF)
    grad_queries, grad_keys, grad_values = attention_backward(
        packed, mask, logsum, grad_mixed, length
    )
    grad_packed = jnp.concatenate([grad_queries, grad_keys, grad_values], -1)
    grad_inputs = times_transposed(grad_packed, wide_qkv) + grad_residual
    grad_inputs = to_positions(grad_inputs.astype(BF).reshape(kept, length, width))
    grad_qkv = over_rows(flat, grad_packed)
    column_sums = jnp.sum(grad_packed.astype(F32), 0)

    def scatter(total):
        return lax.psum_scatter(total.astype(BF), BOTH, scatter_dimension=0, tiled=True).astype(F32)

    sums = (
        column_sums[:width],
        column_sums[2 * width :],
        grad_out_bias,
        grad_gain_one,
        grad_shift_one,
        grad_in_bias,
        grad_down_bias,
        grad_gain_two,
        grad_shift_two,
    )
    joined = jnp.concatenate([v.reshape(devices, -1) for v in sums], 1)
    joined = lax.psum_scatter(joined, BOTH, scatter_dimension=0, tiled=True)[0]
    parts = []
    at = 0
    for size in sizes:
        parts.append(joined[at : at + size])
        at += size
    return (
        outputs,
        grad_inputs,
        scatter(grad_qkv),
        parts[0],
        parts[1],
        scatter(grad_out),
        parts[2],
        parts[3],
        parts[4],
        scatter(grad_in),
        parts[5],
        scatter(grad_down),
        parts[6],
        parts[7],
        parts[8],
    )


def solution(mesh):
    placed = (
        P("dp", "seq", None),
        P("dp"),
        P(("dp", "seq"), None),
        P(("dp", "seq")),
        P(("dp", "seq")),
        P(("dp", "seq"), None),
        P(("dp", "seq")),
        P(("dp", "seq")),
        P(("dp", "seq")),
        P(("dp", "seq"), None),
        P(("dp", "seq")),
        P(("dp", "seq"), None),
        P(("dp", "seq")),
        P(("dp", "seq")),
        P(("dp", "seq")),
        P("dp", "seq", None),
    )
    return jax.shard_map(
        on_device,
        mesh=mesh,
        in_specs=placed,
        out_specs=(
            P("dp", "seq", None),
            P("dp", "seq", None),
            P(("dp", "seq"), None),
            P(("dp", "seq")),
            P(("dp", "seq")),
            P(("dp", "seq"), None),
            P(("dp", "seq")),
            P(("dp", "seq")),
            P(("dp", "seq")),
            P(("dp", "seq"), None),
            P(("dp", "seq")),
            P(("dp", "seq"), None),
            P(("dp", "seq")),
            P(("dp", "seq")),
            P(("dp", "seq")),
        ),
        check_vma=False,
    )
```

```python
import functools

import jax
import jax.numpy as jnp
from jax import lax
from jax.experimental import pallas as pl
from jax.experimental.pallas import tpu as pltpu
from jax.sharding import PartitionSpec as P

BF = jnp.bfloat16
F32 = jnp.float32
HD = 64
BOTH = ("dp", "seq")

def layer_norm(value, gain, shift):
    center = jnp.mean(value, -1, keepdims=True)
    centered = value - center
    spread = jnp.mean(centered * centered, -1, keepdims=True)
    return centered * lax.rsqrt(spread + 1e-12) * gain + shift


def gelu_exact(value):
    return jax.nn.gelu(value, approximate=False)


def over_rows(left, right):
    return lax.dot_general(
        left, right, (((0,), (0,)), ((), ())), preferred_element_type=jnp.float32
    )


def times_transposed(left, right):
    return lax.dot_general(
        left, right, (((1,), (1,)), ((), ())), preferred_element_type=jnp.float32
    )


def nt(a,b): return lax.dot_general(a,b,(((1,),(1,)),((),())),preferred_element_type=F32)
def tn(a,b): return lax.dot_general(a,b,(((0,),(0,)),((),())),preferred_element_type=F32)
def nn(a,b): return lax.dot_general(a,b,(((1,),(0,)),((),())),preferred_element_type=F32)

def masked_pair(q, k, bias, head, lane):
    mine = (lane >= head*HD) & (lane < (head+1)*HD)
    spare = lane == (HD if head==0 else 0)
    zero=jnp.zeros((),BF)
    qh = jnp.where(mine, q*BF(0.125), jnp.where(spare, jnp.ones((),BF), zero))
    kh = jnp.where(mine, k, jnp.where(spare, bias, zero))
    return qh, kh

def fwd_kernel(cq, q_ref,k_ref,v_ref,b_ref,o_ref,lse_ref):
    n=q_ref.shape[0]
    lane=lax.broadcasted_iota(jnp.int32,(n,128),1)
    q=q_ref[...]; k=k_ref[...]; v=v_ref[...]; bias=b_ref[0]
    pairs=[masked_pair(q,k,bias,h,lane) for h in range(2)]
    for c in range(n//cq):
        sl=slice(c*cq,(c+1)*cq)
        halves=[]
        for h in range(2):
            qh,kh=pairs[h]
            s=nt(kh,qh[sl])
            m=jnp.max(s,0,keepdims=True)
            e=jnp.exp(s-m)
            l=jnp.sum(e,0,keepdims=True)
            ot=tn(v[:,h*HD:(h+1)*HD],e.astype(BF))
            halves.append(ot*(1.0/l))
            lse_ref[0,h:h+1,sl]=m+jnp.log(l)
        o_ref[sl,:]=jnp.concatenate(halves,0).T.astype(BF)

def bwd_kernel(cq, q_ref,k_ref,v_ref,b_ref,lse_ref,g_ref,dq_ref,dk_ref,dv_ref):
    n=q_ref.shape[0]
    lane=lax.broadcasted_iota(jnp.int32,(n,128),1)
    q=q_ref[...]; k=k_ref[...]; v=v_ref[...]; bias=b_ref[0]; g=g_ref[...]
    qs=q*BF(0.125); ks=k*BF(0.125)
    zero=jnp.zeros((),BF)
    dks=[];dvs=[]
    dq=[[None,None] for _ in range(n//cq)]
    for h in range(2):
        qh,kh=masked_pair(q,k,bias,h,lane)
        mine = (lane >= h*HD) & (lane < (h+1)*HD)
        vh=jnp.where(mine,v,zero)
        kth=ks[:,h*HD:(h+1)*HD]
        dk=dv=None
        for c in range(n//cq):
            sl=slice(c*cq,(c+1)*cq)
            s=nt(kh,qh[sl])
            p=jnp.exp(s-lse_ref[0,h:h+1,sl])
            gp=nt(vh,g[sl])
            inner=jnp.sum(p*gp,0,keepdims=True)
            ds=(p*(gp-inner)).astype(BF)
            a=nn(p.astype(BF),g[sl]); b=nn(ds,qs[sl])
            dv=a if dv is None else dv+a
            dk=b if dk is None else dk+b
            dq[c][h]=tn(kth,ds)
        dks.append(dk);dvs.append(dv)
    for c in range(n//cq):
        sl=slice(c*cq,(c+1)*cq)
        dq_ref[sl,:]=jnp.concatenate(dq[c],0).T.astype(BF)
    first=lane<HD
    dk_ref[...]=jnp.where(first,dks[0],dks[1]).astype(BF)
    dv_ref[...]=jnp.where(first,dvs[0],dvs[1]).astype(BF)

def attention_forward(packed,bias,length,cq=512):
    rows,wide=packed.shape; width=wide//3; pairs=width//128; seqs=rows//length
    blk=lambda off: pl.BlockSpec((length,128),lambda s,p:(s,off*pairs+p))
    return pl.pallas_call(functools.partial(fwd_kernel,cq),grid=(seqs,pairs),
      in_specs=[blk(0),blk(1),blk(2),pl.BlockSpec((1,length,128),lambda s,p:(s,0,0))],
      out_specs=[blk(0),pl.BlockSpec((1,2,length),lambda s,p:(s*pairs+p,0,0))],
      out_shape=[jax.ShapeDtypeStruct((rows,width),BF),jax.ShapeDtypeStruct((seqs*pairs,2,length),F32)],
      compiler_params=pltpu.CompilerParams(vmem_limit_bytes=48*2**20),name="attention_forward",
      cost_estimate=pl.CostEstimate(flops=4*rows*length*width,bytes_accessed=rows*width*8,transcendentals=rows*length*width//HD))(packed,packed,packed,bias)

def attention_backward(packed,bias,lse,grad,length,cq=512):
    rows,wide=packed.shape; width=wide//3; pairs=width//128; seqs=rows//length
    blk=lambda off: pl.BlockSpec((length,128),lambda s,p:(s,off*pairs+p))
    o=jax.ShapeDtypeStruct((rows,width),BF)
    return pl.pallas_call(functools.partial(bwd_kernel,cq),grid=(seqs,pairs),
      in_specs=[blk(0),blk(1),blk(2),pl.BlockSpec((1,length,128),lambda s,p:(s,0,0)),pl.BlockSpec((1,2,length),lambda s,p:(s*pairs+p,0,0)),blk(0)],
      out_specs=[blk(0)]*3,out_shape=[o,o,o],
      compiler_params=pltpu.CompilerParams(vmem_limit_bytes=48*2**20),name="attention_backward",
      cost_estimate=pl.CostEstimate(flops=10*rows*length*width,bytes_accessed=rows*width*14,transcendentals=rows*length*width//HD))(packed,packed,packed,bias,lse,grad)
def swap(block, distance, devices):
    return lax.ppermute(block, BOTH, [(i, i ^ distance) for i in range(devices)])


def place_kernel(ids, counts, spans, me_ref, *refs):
    pieces, rest = refs[: len(counts)], refs[len(counts) :]
    outs, sems = rest[: len(spans)], rest[len(spans)]
    me = me_ref[0]
    copies = []
    at = 0
    for piece, count in zip(pieces, counts):
        for j in range(count):
            spot = me ^ ids[at]
            for out, (start, size) in zip(outs, spans):
                source = piece.at[j] if len(spans) == 1 else piece.at[j, :, pl.ds(start, size)]
                copy = pltpu.make_async_copy(source, out.at[spot], sems.at[len(copies)])
                copy.start()
                copies.append(copy)
            at += 1
    for copy in copies:
        copy.wait()


def place(pieces, ids, me, spans=None):
    counts = [p.shape[0] for p in pieces]
    total = sum(counts)
    tail = pieces[0].shape[1:]
    spans = spans or [(0, tail[-1])]
    any_space = pl.BlockSpec(memory_space=pl.ANY)
    return pl.pallas_call(
        functools.partial(place_kernel, ids, counts, spans),
        in_specs=[pl.BlockSpec(memory_space=pltpu.SMEM)] + [any_space] * len(pieces),
        out_specs=[any_space] * len(spans),
        out_shape=[
            jax.ShapeDtypeStruct((total,) + tail[:-1] + (size,), pieces[0].dtype)
            for _, size in spans
        ],
        scratch_shapes=[pltpu.SemaphoreType.DMA((total * len(spans),))],
        name="place_blocks",
    )(me.reshape(1), *pieces)


def gather_blocks(block, me, devices, plan, spans=None):
    swapped = lambda b, distance: swap(b, distance, devices)
    own, own_ids = block[None], [0]
    distance = 32
    while distance < devices:
        own = jnp.concatenate([own, swapped(own, distance)])
        own_ids = own_ids + [i ^ distance for i in own_ids]
        distance *= 2
    far = [own] + [swapped(own, 8 * k) for k in (1, 2, 3)]
    far_ids = [[i ^ (8 * k) for i in own_ids] for k in range(4)]
    if plan == "split":
        parts = [((0, 1), (4, 2)), ((2, 3), (2, 4))]
    else:
        parts = [((0, 1, 2, 3), (4, 2) if plan == "xy" else (2, 4))]
    pieces, ids = [], []
    for which, order in parts:
        held = jnp.concatenate([far[k] for k in which])
        held_ids = [i for k in which for i in far_ids[k]]
        got = swapped(held, order[0])
        got_ids = [i ^ order[0] for i in held_ids]
        both = jnp.concatenate([held, got])
        both_ids = held_ids + got_ids
        last = swapped(both, order[1])
        last_ids = [i ^ order[1] for i in both_ids]
        for b, b_ids in ((both, both_ids), (last, last_ids)):
            pieces += [b, swapped(b, 1)]
            ids += b_ids + [i ^ 1 for i in b_ids]
    return place(pieces, ids, me, spans)


def pick(block, axis, index):
    return lax.dynamic_index_in_dim(block, index, axis, keepdims=False)


def fold(block, axis, me, distance, devices):
    digit = (me // distance) % 2
    got = swap(pick(block, axis, 1 - digit), distance, devices)
    return (pick(block, axis, digit).astype(F32) + got.astype(F32)).astype(BF)


def scatter_blocks(total, me, devices, plan):
    tail = total.shape[1:]
    distance = devices // 2
    while distance >= 32:
        total = fold(total.reshape((2, distance) + tail), 0, me, distance, devices)
        distance //= 2
    total = fold(total.reshape((16, 2) + tail), 1, me, 1, devices)
    total = total.reshape((4, 2, 2) + tail)
    z = (me // 8) % 4
    if plan == "split":
        upper = [pick(total.reshape((2, 2, 2, 2) + tail), 0, i) for i in (z // 2, 1 - z // 2)]
        near = fold(fold(upper[0], 1, me, 4, devices), 1, me, 2, devices)
        away = fold(fold(upper[1], 2, me, 2, devices), 1, me, 4, devices)
        odd = z % 2
        mine = [pick(near, 0, odd), pick(near, 0, 1 - odd), pick(away, 0, odd), pick(away, 0, 1 - odd)]
    else:
        if plan == "xy":
            total = fold(fold(total, 1, me, 4, devices), 1, me, 2, devices)
        else:
            total = fold(fold(total, 2, me, 2, devices), 1, me, 4, devices)
        mine = [pick(total, 0, z ^ k) for k in range(4)]
    got = [swap(mine[k], 8 * k, devices).astype(F32) for k in (1, 2, 3)]
    return mine[0].astype(F32) + got[0] + got[1] + got[2]


def to_sequences(block, seat, members, devices):
    groups, count, width = block.shape
    parts = block.reshape(members, groups // members, count, width)
    pieces = [pick(parts, 0, seat)]
    pieces += [swap(pick(parts, 0, seat ^ k), k, devices) for k in range(1, members)]
    return jnp.stack(pieces, 1).reshape(groups * count, width)


def to_positions(block, seat, members, devices):
    pieces = [block[:, 0][None]]
    pieces += [swap(block[:, k][None], k, devices) for k in range(1, members)]
    (placed,) = place(pieces, list(range(members)), seat)
    return placed.reshape((-1,) + placed.shape[2:])


def on_device(
    inputs,
    lengths,
    query_key_value_weight,
    query_bias,
    value_bias,
    output_weight,
    output_bias,
    norm1_gain,
    norm1_shift,
    in_weight,
    in_bias,
    down_weight,
    down_bias,
    norm2_gain,
    norm2_shift,
    cotangent,
):
    groups, local_len, width = inputs.shape
    rows = groups * local_len
    members = lax.axis_size("seq")
    devices = lax.axis_size("dp") * members
    kept = groups // members
    length = local_len * members
    seat = lax.axis_index("seq")
    me = lax.axis_index("dp") * members + seat
    flat = to_sequences(inputs, seat, members, devices)
    vectors = (
        query_bias,
        value_bias,
        output_bias,
        norm1_gain,
        norm1_shift,
        in_bias,
        down_bias,
        norm2_gain,
        norm2_shift,
    )
    sizes = [v.shape[0] for v in vectors]
    share = query_key_value_weight.shape[0]
    vector_block = jnp.concatenate(vectors).reshape(share, -1)
    used = vector_block.shape[1]
    vector_block = jnp.pad(vector_block, ((0, 0), (0, 128 - used)))
    wide_qkv, gathered = gather_blocks(
        jnp.concatenate([query_key_value_weight, vector_block], 1),
        me,
        devices,
        "split",
        [(0, 3 * width), (3 * width, 128)],
    )
    wide_qkv = wide_qkv.reshape(width, 3 * width)
    gathered = gathered[:, :, :used].reshape(devices, -1)
    full = []
    at = 0
    for size in sizes:
        full.append(gathered[:, at : at + size].reshape(-1).astype(F32))
        at += size
    (
        full_query_bias,
        full_value_bias,
        full_out_bias,
        gain_one,
        shift_one,
        full_in_bias,
        full_down_bias,
        gain_two,
        shift_two,
    ) = full
    inner_width = in_weight.shape[1]
    wide_in, wide_out = gather_blocks(
        jnp.concatenate([in_weight, output_weight], 1),
        me,
        devices,
        "yx",
        [(0, inner_width), (inner_width, width)],
    )
    wide_in = wide_in.reshape(width, inner_width)
    wide_out = wide_out.reshape(width, width)
    (wide_down,) = gather_blocks(down_weight, me, devices, "xy")
    wide_down = wide_down.reshape(inner_width, width)
    cot = to_sequences(cotangent, seat, members, devices)
    bias_vector = jnp.concatenate([full_query_bias, jnp.zeros((width,), F32), full_value_bias])
    packed = (jnp.dot(flat, wide_qkv, preferred_element_type=F32) + bias_vector).astype(BF)
    mine = lax.dynamic_slice(lengths, (seat * kept,), (kept,))
    slots = jnp.arange(length, dtype=jnp.int32)
    positions = ((slots // local_len) ^ seat) * local_len + slots % local_len
    mask = jnp.where(positions[None, :] < mine[:, None], 0.0, -1e30).astype(BF)
    mask = jnp.broadcast_to(mask[:, :, None], (kept, length, 128))
    mixed, logsum = attention_forward(packed, mask, length)
    attention_branch = jnp.dot(mixed, wide_out, preferred_element_type=F32) + full_out_bias
    first, norm_one_pull = jax.vjp(
        layer_norm, flat.astype(F32) + attention_branch, gain_one, shift_one
    )
    first_low = first.astype(BF)
    hidden = jnp.dot(first_low, wide_in, preferred_element_type=F32) + full_in_bias
    active, gelu_pull = jax.vjp(gelu_exact, hidden)
    active_low = active.astype(BF)
    branch_two = jnp.dot(active_low, wide_down, preferred_element_type=F32) + full_down_bias
    result, norm_two_pull = jax.vjp(
        layer_norm, first_low.astype(F32) + branch_two, gain_two, shift_two
    )
    outputs = to_positions(
        result.astype(BF).reshape(kept, members, local_len, width), seat, members, devices
    )
    grad_second, grad_gain_two, grad_shift_two = norm_two_pull(cot.astype(F32))
    grad_branch_two = grad_second.astype(BF)
    grad_down = over_rows(active_low, grad_branch_two)
    grad_down_bias = jnp.sum(grad_branch_two.astype(F32), 0)
    (grad_hidden,) = gelu_pull(times_transposed(grad_branch_two, wide_down))
    grad_hidden_low = grad_hidden.astype(BF)
    grad_in = over_rows(first_low, grad_hidden_low)
    grad_in_bias = jnp.sum(grad_hidden_low.astype(F32), 0)
    grad_first = times_transposed(grad_hidden_low, wide_in) + grad_second
    grad_residual, grad_gain_one, grad_shift_one = norm_one_pull(grad_first)
    grad_branch_one = grad_residual.astype(BF)
    grad_out = over_rows(mixed, grad_branch_one)
    grad_out_bias = jnp.sum(grad_branch_one.astype(F32), 0)
    grad_mixed = times_transposed(grad_branch_one, wide_out).astype(BF)
    grad_queries, grad_keys, grad_values = attention_backward(
        packed, mask, logsum, grad_mixed, length
    )
    grad_packed = jnp.concatenate([grad_queries, grad_keys, grad_values], -1)
    grad_inputs = times_transposed(grad_packed, wide_qkv) + grad_residual
    grad_inputs = to_positions(
        grad_inputs.astype(BF).reshape(kept, members, local_len, width), seat, members, devices
    )
    grad_qkv = over_rows(flat, grad_packed)
    column_sums = jnp.sum(grad_packed.astype(F32), 0)

    sums = (
        column_sums[:width],
        column_sums[2 * width :],
        grad_out_bias,
        grad_gain_one,
        grad_shift_one,
        grad_in_bias,
        grad_down_bias,
        grad_gain_two,
        grad_shift_two,
    )
    joined = jnp.concatenate([v.reshape(devices, -1) for v in sums], 1)
    joined = jnp.pad(joined.reshape(devices, share, used), ((0, 0), (0, 0), (0, 128 - used)))
    down_part = scatter_blocks(
        grad_down.astype(BF).reshape(devices, -1, width), me, devices, "xy"
    )
    in_part = scatter_blocks(
        jnp.concatenate([grad_in.astype(BF), grad_out.astype(BF)], 1).reshape(
            devices, share, inner_width + width
        ),
        me,
        devices,
        "yx",
    )
    qkv_part = scatter_blocks(
        jnp.concatenate(
            [grad_qkv.astype(BF).reshape(devices, share, 3 * width), joined.astype(BF)], 2
        ),
        me,
        devices,
        "split",
    )
    joined = qkv_part[:, 3 * width : 3 * width + used].reshape(-1)
    parts = []
    at = 0
    for size in sizes:
        parts.append(joined[at : at + size])
        at += size
    return (
        outputs,
        grad_inputs,
        qkv_part[:, : 3 * width],
        parts[0],
        parts[1],
        in_part[:, inner_width:],
        parts[2],
        parts[3],
        parts[4],
        in_part[:, :inner_width],
        parts[5],
        down_part,
        parts[6],
        parts[7],
        parts[8],
    )


def solution(mesh):
    placed = (
        P("dp", "seq", None),
        P("dp"),
        P(("dp", "seq"), None),
        P(("dp", "seq")),
        P(("dp", "seq")),
        P(("dp", "seq"), None),
        P(("dp", "seq")),
        P(("dp", "seq")),
        P(("dp", "seq")),
        P(("dp", "seq"), None),
        P(("dp", "seq")),
        P(("dp", "seq"), None),
        P(("dp", "seq")),
        P(("dp", "seq")),
        P(("dp", "seq")),
        P("dp", "seq", None),
    )
    return jax.shard_map(
        on_device,
        mesh=mesh,
        in_specs=placed,
        out_specs=(
            P("dp", "seq", None),
            P("dp", "seq", None),
            P(("dp", "seq"), None),
            P(("dp", "seq")),
            P(("dp", "seq")),
            P(("dp", "seq"), None),
            P(("dp", "seq")),
            P(("dp", "seq")),
            P(("dp", "seq")),
            P(("dp", "seq"), None),
            P(("dp", "seq")),
            P(("dp", "seq"), None),
            P(("dp", "seq")),
            P(("dp", "seq")),
            P(("dp", "seq")),
        ),
        check_vma=False,
    )
```

```python
import functools

import jax
import jax.numpy as jnp
from jax import lax
from jax.experimental import pallas as pl
from jax.experimental.pallas import tpu as pltpu
from jax.sharding import PartitionSpec as P

BF = jnp.bfloat16
F32 = jnp.float32
HD = 64
BOTH = ("dp", "seq")

def layer_norm(value, gain, shift):
    center = jnp.mean(value, -1, keepdims=True)
    centered = value - center
    spread = jnp.mean(centered * centered, -1, keepdims=True)
    return centered * lax.rsqrt(spread + 1e-12) * gain + shift


def gelu_exact(value):
    return jax.nn.gelu(value, approximate=False)


def over_rows(left, right):
    return lax.dot_general(
        left, right, (((0,), (0,)), ((), ())), preferred_element_type=jnp.float32
    )


def times_transposed(left, right):
    return lax.dot_general(
        left, right, (((1,), (1,)), ((), ())), preferred_element_type=jnp.float32
    )


def nt(a,b): return lax.dot_general(a,b,(((1,),(1,)),((),())),preferred_element_type=F32)
def tn(a,b): return lax.dot_general(a,b,(((0,),(0,)),((),())),preferred_element_type=F32)
def nn(a,b): return lax.dot_general(a,b,(((1,),(0,)),((),())),preferred_element_type=F32)

def masked_pair(q, k, bias, head, lane):
    mine = (lane >= head*HD) & (lane < (head+1)*HD)
    spare = lane == (HD if head==0 else 0)
    zero=jnp.zeros((),BF)
    qh = jnp.where(mine, q*BF(0.125), jnp.where(spare, jnp.ones((),BF), zero))
    kh = jnp.where(mine, k, jnp.where(spare, bias, zero))
    return qh, kh

def fwd_kernel(cq, q_ref,k_ref,v_ref,b_ref,o_ref,lse_ref):
    n=q_ref.shape[0]
    lane=lax.broadcasted_iota(jnp.int32,(n,128),1)
    q=q_ref[...]; k=k_ref[...]; v=v_ref[...]; bias=b_ref[0]
    pairs=[masked_pair(q,k,bias,h,lane) for h in range(2)]
    for c in range(n//cq):
        sl=slice(c*cq,(c+1)*cq)
        halves=[]
        for h in range(2):
            qh,kh=pairs[h]
            s=nt(kh,qh[sl])
            m=jnp.max(s,0,keepdims=True)
            e=jnp.exp(s-m)
            l=jnp.sum(e,0,keepdims=True)
            ot=tn(v[:,h*HD:(h+1)*HD],e.astype(BF))
            halves.append(ot*(1.0/l))
            lse_ref[0,h:h+1,sl]=m+jnp.log(l)
        o_ref[sl,:]=jnp.concatenate(halves,0).T.astype(BF)

def bwd_kernel(cq, q_ref,k_ref,v_ref,b_ref,lse_ref,g_ref,dq_ref,dk_ref,dv_ref):
    n=q_ref.shape[0]
    lane=lax.broadcasted_iota(jnp.int32,(n,128),1)
    q=q_ref[...]; k=k_ref[...]; v=v_ref[...]; bias=b_ref[0]; g=g_ref[...]
    qs=q*BF(0.125); ks=k*BF(0.125)
    zero=jnp.zeros((),BF)
    dks=[];dvs=[]
    dq=[[None,None] for _ in range(n//cq)]
    for h in range(2):
        qh,kh=masked_pair(q,k,bias,h,lane)
        mine = (lane >= h*HD) & (lane < (h+1)*HD)
        vh=jnp.where(mine,v,zero)
        kth=ks[:,h*HD:(h+1)*HD]
        dk=dv=None
        for c in range(n//cq):
            sl=slice(c*cq,(c+1)*cq)
            s=nt(kh,qh[sl])
            p=jnp.exp(s-lse_ref[0,h:h+1,sl])
            gp=nt(vh,g[sl])
            inner=jnp.sum(p*gp,0,keepdims=True)
            ds=(p*(gp-inner)).astype(BF)
            a=nn(p.astype(BF),g[sl]); b=nn(ds,qs[sl])
            dv=a if dv is None else dv+a
            dk=b if dk is None else dk+b
            dq[c][h]=tn(kth,ds)
        dks.append(dk);dvs.append(dv)
    for c in range(n//cq):
        sl=slice(c*cq,(c+1)*cq)
        dq_ref[sl,:]=jnp.concatenate(dq[c],0).T.astype(BF)
    first=lane<HD
    dk_ref[...]=jnp.where(first,dks[0],dks[1]).astype(BF)
    dv_ref[...]=jnp.where(first,dvs[0],dvs[1]).astype(BF)

def attention_forward(packed,bias,length,cq=512):
    rows,wide=packed.shape; width=wide//3; pairs=width//128; seqs=rows//length
    blk=lambda off: pl.BlockSpec((length,128),lambda s,p:(s,off*pairs+p))
    return pl.pallas_call(functools.partial(fwd_kernel,cq),grid=(seqs,pairs),
      in_specs=[blk(0),blk(1),blk(2),pl.BlockSpec((1,length,128),lambda s,p:(s,0,0))],
      out_specs=[blk(0),pl.BlockSpec((1,2,length),lambda s,p:(s*pairs+p,0,0))],
      out_shape=[jax.ShapeDtypeStruct((rows,width),BF),jax.ShapeDtypeStruct((seqs*pairs,2,length),F32)],
      compiler_params=pltpu.CompilerParams(vmem_limit_bytes=48*2**20),name="attention_forward",
      cost_estimate=pl.CostEstimate(flops=4*rows*length*width,bytes_accessed=rows*width*8,transcendentals=rows*length*width//HD))(packed,packed,packed,bias)

def attention_backward(packed,bias,lse,grad,length,cq=512):
    rows,wide=packed.shape; width=wide//3; pairs=width//128; seqs=rows//length
    blk=lambda off: pl.BlockSpec((length,128),lambda s,p:(s,off*pairs+p))
    o=jax.ShapeDtypeStruct((rows,width),BF)
    return pl.pallas_call(functools.partial(bwd_kernel,cq),grid=(seqs,pairs),
      in_specs=[blk(0),blk(1),blk(2),pl.BlockSpec((1,length,128),lambda s,p:(s,0,0)),pl.BlockSpec((1,2,length),lambda s,p:(s*pairs+p,0,0)),blk(0)],
      out_specs=[blk(0)]*3,out_shape=[o,o,o],
      compiler_params=pltpu.CompilerParams(vmem_limit_bytes=48*2**20),name="attention_backward",
      cost_estimate=pl.CostEstimate(flops=10*rows*length*width,bytes_accessed=rows*width*14,transcendentals=rows*length*width//HD))(packed,packed,packed,bias,lse,grad)
def swap(block, distance, devices):
    return lax.ppermute(block, BOTH, [(i, i ^ distance) for i in range(devices)])


def place_kernel(ids, counts, spans, me_ref, *refs):
    pieces, rest = refs[: len(counts)], refs[len(counts) :]
    outs, sems = rest[: len(spans)], rest[len(spans)]
    me = me_ref[0]
    copies = []
    at = 0
    for piece, count in zip(pieces, counts):
        for j in range(count):
            spot = me ^ ids[at]
            for out, (start, size) in zip(outs, spans):
                source = piece.at[j] if len(spans) == 1 else piece.at[j, :, pl.ds(start, size)]
                copy = pltpu.make_async_copy(source, out.at[spot], sems.at[len(copies)])
                copy.start()
                copies.append(copy)
            at += 1
    for copy in copies:
        copy.wait()


def place(pieces, ids, me, spans=None):
    counts = [p.shape[0] for p in pieces]
    total = sum(counts)
    tail = pieces[0].shape[1:]
    spans = spans or [(0, tail[-1])]
    any_space = pl.BlockSpec(memory_space=pl.ANY)
    return pl.pallas_call(
        functools.partial(place_kernel, ids, counts, spans),
        in_specs=[pl.BlockSpec(memory_space=pltpu.SMEM)] + [any_space] * len(pieces),
        out_specs=[pl.BlockSpec(memory_space=pltpu.VMEM)] * len(spans),
        out_shape=[
            jax.ShapeDtypeStruct((total,) + tail[:-1] + (size,), pieces[0].dtype)
            for _, size in spans
        ],
        scratch_shapes=[pltpu.SemaphoreType.DMA((total * len(spans),))],
        compiler_params=pltpu.CompilerParams(vmem_limit_bytes=32 * 2**20),
        name="place_blocks",
    )(me.reshape(1), *pieces)


def gather_blocks(block, me, devices, plan, spans=None):
    swapped = lambda b, distance: swap(b, distance, devices)
    own, own_ids = block[None], [0]
    distance = 32
    while distance < devices:
        own = jnp.concatenate([own, swapped(own, distance)])
        own_ids = own_ids + [i ^ distance for i in own_ids]
        distance *= 2
    far = [own] + [swapped(own, 8 * k) for k in (1, 2, 3)]
    far_ids = [[i ^ (8 * k) for i in own_ids] for k in range(4)]
    if plan == "split":
        parts = [((0, 1), (4, 2)), ((2, 3), (2, 4))]
    else:
        parts = [((0, 1, 2, 3), (4, 2) if plan == "xy" else (2, 4))]
    pieces, ids = [], []
    for which, order in parts:
        held = jnp.concatenate([far[k] for k in which])
        held_ids = [i for k in which for i in far_ids[k]]
        got = swapped(held, order[0])
        got_ids = [i ^ order[0] for i in held_ids]
        both = jnp.concatenate([held, got])
        both_ids = held_ids + got_ids
        last = swapped(both, order[1])
        last_ids = [i ^ order[1] for i in both_ids]
        for b, b_ids in ((both, both_ids), (last, last_ids)):
            pieces += [b, swapped(b, 1)]
            ids += b_ids + [i ^ 1 for i in b_ids]
    return place(pieces, ids, me, spans)


def pick(block, axis, index):
    return lax.dynamic_index_in_dim(block, index, axis, keepdims=False)


def fold(block, axis, me, distance, devices):
    digit = (me // distance) % 2
    got = swap(pick(block, axis, 1 - digit), distance, devices)
    return (pick(block, axis, digit).astype(F32) + got.astype(F32)).astype(BF)


def scatter_blocks(total, me, devices, plan):
    tail = total.shape[1:]
    distance = devices // 2
    while distance >= 32:
        total = fold(total.reshape((2, distance) + tail), 0, me, distance, devices)
        distance //= 2
    total = fold(total.reshape((16, 2) + tail), 1, me, 1, devices)
    total = total.reshape((4, 2, 2) + tail)
    z = (me // 8) % 4
    if plan == "split":
        upper = [pick(total.reshape((2, 2, 2, 2) + tail), 0, i) for i in (z // 2, 1 - z // 2)]
        near = fold(fold(upper[0], 1, me, 4, devices), 1, me, 2, devices)
        away = fold(fold(upper[1], 2, me, 2, devices), 1, me, 4, devices)
        odd = z % 2
        mine = [pick(near, 0, odd), pick(near, 0, 1 - odd), pick(away, 0, odd), pick(away, 0, 1 - odd)]
    else:
        if plan == "xy":
            total = fold(fold(total, 1, me, 4, devices), 1, me, 2, devices)
        else:
            total = fold(fold(total, 2, me, 2, devices), 1, me, 4, devices)
        mine = [pick(total, 0, z ^ k) for k in range(4)]
    got = [swap(mine[k], 8 * k, devices).astype(F32) for k in (1, 2, 3)]
    return mine[0].astype(F32) + got[0] + got[1] + got[2]


def to_sequences(block, seat, members, devices):
    groups, count, width = block.shape
    parts = block.reshape(members, groups // members, count, width)
    pieces = [pick(parts, 0, seat)]
    pieces += [swap(pick(parts, 0, seat ^ k), k, devices) for k in range(1, members)]
    return jnp.stack(pieces, 1).reshape(groups * count, width)


def to_positions(block, seat, members, devices):
    pieces = [block[:, 0][None]]
    pieces += [swap(block[:, k][None], k, devices) for k in range(1, members)]
    (placed,) = place(pieces, list(range(members)), seat)
    return placed.reshape((-1,) + placed.shape[2:])


def on_device(
    inputs,
    lengths,
    query_key_value_weight,
    query_bias,
    value_bias,
    output_weight,
    output_bias,
    norm1_gain,
    norm1_shift,
    in_weight,
    in_bias,
    down_weight,
    down_bias,
    norm2_gain,
    norm2_shift,
    cotangent,
):
    groups, local_len, width = inputs.shape
    rows = groups * local_len
    members = lax.axis_size("seq")
    devices = lax.axis_size("dp") * members
    kept = groups // members
    length = local_len * members
    seat = lax.axis_index("seq")
    me = lax.axis_index("dp") * members + seat
    flat = to_sequences(inputs, seat, members, devices)
    vectors = (
        query_bias,
        value_bias,
        output_bias,
        norm1_gain,
        norm1_shift,
        in_bias,
        down_bias,
        norm2_gain,
        norm2_shift,
    )
    sizes = [v.shape[0] for v in vectors]
    share = query_key_value_weight.shape[0]
    vector_block = jnp.concatenate(vectors).reshape(share, -1)
    used = vector_block.shape[1]
    vector_block = jnp.pad(vector_block, ((0, 0), (0, 128 - used)))
    wide_qkv, gathered = gather_blocks(
        jnp.concatenate([query_key_value_weight, vector_block], 1),
        me,
        devices,
        "split",
        [(0, 3 * width), (3 * width, 128)],
    )
    wide_qkv = wide_qkv.reshape(width, 3 * width)
    gathered = gathered[:, :, :used].reshape(devices, -1)
    full = []
    at = 0
    for size in sizes:
        full.append(gathered[:, at : at + size].reshape(-1).astype(F32))
        at += size
    (
        full_query_bias,
        full_value_bias,
        full_out_bias,
        gain_one,
        shift_one,
        full_in_bias,
        full_down_bias,
        gain_two,
        shift_two,
    ) = full
    inner_width = in_weight.shape[1]
    wide_in, wide_out = gather_blocks(
        jnp.concatenate([in_weight, output_weight], 1),
        me,
        devices,
        "yx",
        [(0, inner_width), (inner_width, width)],
    )
    wide_in = wide_in.reshape(width, inner_width)
    wide_out = wide_out.reshape(width, width)
    (wide_down,) = gather_blocks(down_weight, me, devices, "xy")
    wide_down = wide_down.reshape(inner_width, width)
    cot = to_sequences(cotangent, seat, members, devices)
    bias_vector = jnp.concatenate([full_query_bias, jnp.zeros((width,), F32), full_value_bias])
    packed = (jnp.dot(flat, wide_qkv, preferred_element_type=F32) + bias_vector).astype(BF)
    mine = lax.dynamic_slice(lengths, (seat * kept,), (kept,))
    slots = jnp.arange(length, dtype=jnp.int32)
    positions = ((slots // local_len) ^ seat) * local_len + slots % local_len
    mask = jnp.where(positions[None, :] < mine[:, None], 0.0, -1e30).astype(BF)
    mask = jnp.broadcast_to(mask[:, :, None], (kept, length, 128))
    mixed, logsum = attention_forward(packed, mask, length)
    attention_branch = jnp.dot(mixed, wide_out, preferred_element_type=F32) + full_out_bias
    first, norm_one_pull = jax.vjp(
        layer_norm, flat.astype(F32) + attention_branch, gain_one, shift_one
    )
    first_low = first.astype(BF)
    hidden = jnp.dot(first_low, wide_in, preferred_element_type=F32) + full_in_bias
    active, gelu_pull = jax.vjp(gelu_exact, hidden)
    active_low = active.astype(BF)
    branch_two = jnp.dot(active_low, wide_down, preferred_element_type=F32) + full_down_bias
    result, norm_two_pull = jax.vjp(
        layer_norm, first_low.astype(F32) + branch_two, gain_two, shift_two
    )
    outputs = to_positions(
        result.astype(BF).reshape(kept, members, local_len, width), seat, members, devices
    )
    grad_second, grad_gain_two, grad_shift_two = norm_two_pull(cot.astype(F32))
    grad_branch_two = grad_second.astype(BF)
    grad_down = over_rows(active_low, grad_branch_two)
    grad_down_bias = jnp.sum(grad_branch_two.astype(F32), 0)
    (grad_hidden,) = gelu_pull(times_transposed(grad_branch_two, wide_down))
    grad_hidden_low = grad_hidden.astype(BF)
    grad_in = over_rows(first_low, grad_hidden_low)
    grad_in_bias = jnp.sum(grad_hidden_low.astype(F32), 0)
    grad_first = times_transposed(grad_hidden_low, wide_in) + grad_second
    grad_residual, grad_gain_one, grad_shift_one = norm_one_pull(grad_first)
    grad_branch_one = grad_residual.astype(BF)
    grad_out = over_rows(mixed, grad_branch_one)
    grad_out_bias = jnp.sum(grad_branch_one.astype(F32), 0)
    grad_mixed = times_transposed(grad_branch_one, wide_out).astype(BF)
    grad_queries, grad_keys, grad_values = attention_backward(
        packed, mask, logsum, grad_mixed, length
    )
    grad_packed = jnp.concatenate([grad_queries, grad_keys, grad_values], -1)
    grad_inputs = times_transposed(grad_packed, wide_qkv) + grad_residual
    grad_inputs = to_positions(
        grad_inputs.astype(BF).reshape(kept, members, local_len, width), seat, members, devices
    )
    grad_qkv = over_rows(flat, grad_packed)
    column_sums = jnp.sum(grad_packed.astype(F32), 0)

    sums = (
        column_sums[:width],
        column_sums[2 * width :],
        grad_out_bias,
        grad_gain_one,
        grad_shift_one,
        grad_in_bias,
        grad_down_bias,
        grad_gain_two,
        grad_shift_two,
    )
    joined = jnp.concatenate([v.reshape(devices, -1) for v in sums], 1)
    joined = jnp.pad(joined.reshape(devices, share, used), ((0, 0), (0, 0), (0, 128 - used)))
    down_part = scatter_blocks(
        grad_down.astype(BF).reshape(devices, -1, width), me, devices, "xy"
    )
    in_part = scatter_blocks(
        jnp.concatenate([grad_in.astype(BF), grad_out.astype(BF)], 1).reshape(
            devices, share, inner_width + width
        ),
        me,
        devices,
        "yx",
    )
    qkv_part = scatter_blocks(
        jnp.concatenate(
            [grad_qkv.astype(BF).reshape(devices, share, 3 * width), joined.astype(BF)], 2
        ),
        me,
        devices,
        "split",
    )
    joined = qkv_part[:, 3 * width : 3 * width + used].reshape(-1)
    parts = []
    at = 0
    for size in sizes:
        parts.append(joined[at : at + size])
        at += size
    return (
        outputs,
        grad_inputs,
        qkv_part[:, : 3 * width],
        parts[0],
        parts[1],
        in_part[:, inner_width:],
        parts[2],
        parts[3],
        parts[4],
        in_part[:, :inner_width],
        parts[5],
        down_part,
        parts[6],
        parts[7],
        parts[8],
    )


def solution(mesh):
    placed = (
        P("dp", "seq", None),
        P("dp"),
        P(("dp", "seq"), None),
        P(("dp", "seq")),
        P(("dp", "seq")),
        P(("dp", "seq"), None),
        P(("dp", "seq")),
        P(("dp", "seq")),
        P(("dp", "seq")),
        P(("dp", "seq"), None),
        P(("dp", "seq")),
        P(("dp", "seq"), None),
        P(("dp", "seq")),
        P(("dp", "seq")),
        P(("dp", "seq")),
        P("dp", "seq", None),
    )
    return jax.shard_map(
        on_device,
        mesh=mesh,
        in_specs=placed,
        out_specs=(
            P("dp", "seq", None),
            P("dp", "seq", None),
            P(("dp", "seq"), None),
            P(("dp", "seq")),
            P(("dp", "seq")),
            P(("dp", "seq"), None),
            P(("dp", "seq")),
            P(("dp", "seq")),
            P(("dp", "seq")),
            P(("dp", "seq"), None),
            P(("dp", "seq")),
            P(("dp", "seq"), None),
            P(("dp", "seq")),
            P(("dp", "seq")),
            P(("dp", "seq")),
        ),
        check_vma=False,
    )
```

```python
import functools

import jax
import jax.numpy as jnp
from jax import lax
from jax.experimental import pallas as pl
from jax.experimental.pallas import tpu as pltpu
from jax.sharding import PartitionSpec as P

BF = jnp.bfloat16
F32 = jnp.float32
HD = 64
BOTH = ("dp", "seq")

def layer_norm(value, gain, shift):
    center = jnp.mean(value, -1, keepdims=True)
    centered = value - center
    spread = jnp.mean(centered * centered, -1, keepdims=True)
    return centered * lax.rsqrt(spread + 1e-12) * gain + shift


def gelu_exact(value):
    return jax.nn.gelu(value, approximate=False)


def over_rows(left, right):
    return lax.dot_general(
        left, right, (((0,), (0,)), ((), ())), preferred_element_type=jnp.float32
    )


def times_transposed(left, right):
    return lax.dot_general(
        left, right, (((1,), (1,)), ((), ())), preferred_element_type=jnp.float32
    )


def nt(a,b): return lax.dot_general(a,b,(((1,),(1,)),((),())),preferred_element_type=F32)
def tn(a,b): return lax.dot_general(a,b,(((0,),(0,)),((),())),preferred_element_type=F32)
def nn(a,b): return lax.dot_general(a,b,(((1,),(0,)),((),())),preferred_element_type=F32)

def masked_pair(q, k, bias, head, lane):
    mine = (lane >= head*HD) & (lane < (head+1)*HD)
    spare = lane == (HD if head==0 else 0)
    zero=jnp.zeros((),BF)
    qh = jnp.where(mine, q*BF(0.125), jnp.where(spare, jnp.ones((),BF), zero))
    kh = jnp.where(mine, k, jnp.where(spare, bias, zero))
    return qh, kh

def fwd_kernel(cq, q_ref,k_ref,v_ref,b_ref,o_ref,lse_ref):
    n=q_ref.shape[0]
    lane=lax.broadcasted_iota(jnp.int32,(n,128),1)
    q=q_ref[...]; k=k_ref[...]; v=v_ref[...]; bias=b_ref[0]
    pairs=[masked_pair(q,k,bias,h,lane) for h in range(2)]
    for c in range(n//cq):
        sl=slice(c*cq,(c+1)*cq)
        halves=[]
        for h in range(2):
            qh,kh=pairs[h]
            s=nt(kh,qh[sl])
            m=jnp.max(s,0,keepdims=True)
            e=jnp.exp(s-m)
            l=jnp.sum(e,0,keepdims=True)
            ot=tn(v[:,h*HD:(h+1)*HD],e.astype(BF))
            halves.append(ot*(1.0/l))
            lse_ref[0,h:h+1,sl]=m+jnp.log(l)
        o_ref[sl,:]=jnp.concatenate(halves,0).T.astype(BF)

def bwd_kernel(cq, q_ref,k_ref,v_ref,b_ref,lse_ref,g_ref,dq_ref,dk_ref,dv_ref):
    n=q_ref.shape[0]
    lane=lax.broadcasted_iota(jnp.int32,(n,128),1)
    q=q_ref[...]; k=k_ref[...]; v=v_ref[...]; bias=b_ref[0]; g=g_ref[...]
    qs=q*BF(0.125); ks=k*BF(0.125)
    zero=jnp.zeros((),BF)
    dks=[];dvs=[]
    dq=[[None,None] for _ in range(n//cq)]
    for h in range(2):
        qh,kh=masked_pair(q,k,bias,h,lane)
        mine = (lane >= h*HD) & (lane < (h+1)*HD)
        vh=jnp.where(mine,v,zero)
        kth=ks[:,h*HD:(h+1)*HD]
        dk=dv=None
        for c in range(n//cq):
            sl=slice(c*cq,(c+1)*cq)
            s=nt(kh,qh[sl])
            p=jnp.exp(s-lse_ref[0,h:h+1,sl])
            gp=nt(vh,g[sl])
            inner=jnp.sum(p*gp,0,keepdims=True)
            ds=(p*(gp-inner)).astype(BF)
            a=nn(p.astype(BF),g[sl]); b=nn(ds,qs[sl])
            dv=a if dv is None else dv+a
            dk=b if dk is None else dk+b
            dq[c][h]=tn(kth,ds)
        dks.append(dk);dvs.append(dv)
    for c in range(n//cq):
        sl=slice(c*cq,(c+1)*cq)
        dq_ref[sl,:]=jnp.concatenate(dq[c],0).T.astype(BF)
    first=lane<HD
    dk_ref[...]=jnp.where(first,dks[0],dks[1]).astype(BF)
    dv_ref[...]=jnp.where(first,dvs[0],dvs[1]).astype(BF)

def attention_forward(packed,bias,length,cq=512):
    rows,wide=packed.shape; width=wide//3; pairs=width//128; seqs=rows//length
    blk=lambda off: pl.BlockSpec((length,128),lambda s,p:(s,off*pairs+p))
    return pl.pallas_call(functools.partial(fwd_kernel,cq),grid=(seqs,pairs),
      in_specs=[blk(0),blk(1),blk(2),pl.BlockSpec((1,length,128),lambda s,p:(s,0,0))],
      out_specs=[blk(0),pl.BlockSpec((1,2,length),lambda s,p:(s*pairs+p,0,0))],
      out_shape=[jax.ShapeDtypeStruct((rows,width),BF),jax.ShapeDtypeStruct((seqs*pairs,2,length),F32)],
      compiler_params=pltpu.CompilerParams(vmem_limit_bytes=48*2**20),name="attention_forward",
      cost_estimate=pl.CostEstimate(flops=4*rows*length*width,bytes_accessed=rows*width*8,transcendentals=rows*length*width//HD))(packed,packed,packed,bias)

def attention_backward(packed,bias,lse,grad,length,cq=512):
    rows,wide=packed.shape; width=wide//3; pairs=width//128; seqs=rows//length
    blk=lambda off: pl.BlockSpec((length,128),lambda s,p:(s,off*pairs+p))
    o=jax.ShapeDtypeStruct((rows,width),BF)
    return pl.pallas_call(functools.partial(bwd_kernel,cq),grid=(seqs,pairs),
      in_specs=[blk(0),blk(1),blk(2),pl.BlockSpec((1,length,128),lambda s,p:(s,0,0)),pl.BlockSpec((1,2,length),lambda s,p:(s*pairs+p,0,0)),blk(0)],
      out_specs=[blk(0)]*3,out_shape=[o,o,o],
      compiler_params=pltpu.CompilerParams(vmem_limit_bytes=48*2**20),name="attention_backward",
      cost_estimate=pl.CostEstimate(flops=10*rows*length*width,bytes_accessed=rows*width*14,transcendentals=rows*length*width//HD))(packed,packed,packed,bias,lse,grad)
def swap(block, distance, devices):
    return lax.ppermute(block, BOTH, [(i, i ^ distance) for i in range(devices)])


def after(value, *done):
    return lax.optimization_barrier((value,) + done)[0]


def place_kernel(ids, counts, spans, me_ref, *refs):
    pieces, rest = refs[: len(counts)], refs[len(counts) :]
    outs, sems = rest[: len(spans)], rest[len(spans)]
    me = me_ref[0]
    copies = []
    at = 0
    for piece, count in zip(pieces, counts):
        for j in range(count):
            spot = me ^ ids[at]
            for out, (start, size) in zip(outs, spans):
                source = piece.at[j] if len(spans) == 1 else piece.at[j, :, pl.ds(start, size)]
                copy = pltpu.make_async_copy(source, out.at[spot], sems.at[len(copies)])
                copy.start()
                copies.append(copy)
            at += 1
    for copy in copies:
        copy.wait()


def place(pieces, ids, me, spans=None):
    counts = [p.shape[0] for p in pieces]
    total = sum(counts)
    tail = pieces[0].shape[1:]
    spans = spans or [(0, tail[-1])]
    any_space = pl.BlockSpec(memory_space=pl.ANY)
    moved = 2 * sum(p.size * p.dtype.itemsize for p in pieces)
    return pl.pallas_call(
        functools.partial(place_kernel, ids, counts, spans),
        in_specs=[pl.BlockSpec(memory_space=pltpu.SMEM)] + [any_space] * len(pieces),
        out_specs=[pl.BlockSpec(memory_space=pltpu.VMEM)] * len(spans),
        out_shape=[
            jax.ShapeDtypeStruct((total,) + tail[:-1] + (size,), pieces[0].dtype)
            for _, size in spans
        ],
        scratch_shapes=[pltpu.SemaphoreType.DMA((total * len(spans),))],
        compiler_params=pltpu.CompilerParams(vmem_limit_bytes=32 * 2**20),
        cost_estimate=pl.CostEstimate(flops=0, bytes_accessed=moved, transcendentals=0),
        name="place_blocks",
    )(me.reshape(1), *pieces)


def pack_rows(vectors, share):
    lead = vectors[0].shape[:-1]
    columns = []
    for at in range(0, len(vectors), share):
        rows = []
        for v in vectors[at : at + share]:
            rows.append(jnp.pad(v, [(0, 0)] * len(lead) + [(0, 128 - v.shape[-1])]))
        block = jnp.stack(rows, -2)
        columns.append(
            jnp.pad(block, [(0, 0)] * len(lead) + [(0, share - len(rows)), (0, 0)])
        )
    return columns[0] if len(columns) == 1 else jnp.concatenate(columns, -1)


def unpack_rows(block, sizes):
    share = block.shape[-2]
    out = []
    for i, size in enumerate(sizes):
        start = i // share * 128
        out.append(block[..., i % share, start : start + size])
    return out


class Gather:
    def __init__(self, block, me, devices, plan):
        self.me, self.devices, self.plan = me, devices, plan
        self.own, self.own_ids = block[None], [0]

    def swapped(self, block, distance):
        return swap(block, distance, self.devices)

    def along_z(self, *done):
        own, own_ids = self.own, self.own_ids
        if done:
            own = after(own, *done)
        distance = 32
        while distance < self.devices:
            own = jnp.concatenate([own, self.swapped(own, distance)])
            own_ids = own_ids + [i ^ distance for i in own_ids]
            distance *= 2
        far = [own] + [self.swapped(own, 8 * k) for k in (1, 2, 3)]
        far_ids = [[i ^ (8 * k) for i in own_ids] for k in range(4)]
        if self.plan == "split":
            parts = [((0, 1), (4, 2)), ((2, 3), (2, 4))]
        else:
            parts = [((0, 1, 2, 3), (4, 2) if self.plan == "xy" else (2, 4))]
        self.parts = []
        for which, order in parts:
            held = jnp.concatenate([far[k] for k in which])
            self.parts.append((held, [i for k in which for i in far_ids[k]], order))
        return far[1]

    def first(self, *done):
        grown = []
        for held, ids, order in self.parts:
            if done:
                held = after(held, *done)
            got = self.swapped(held, order[0])
            grown.append(
                (jnp.concatenate([held, got]), ids + [i ^ order[0] for i in ids], order)
            )
        self.parts = grown
        return grown[0][0]

    def second(self, spans=None, *done):
        pieces, piece_ids = [], []
        for held, ids, order in self.parts:
            if done:
                held = after(held, *done)
            last = self.swapped(held, order[1])
            last_ids = [i ^ order[1] for i in ids]
            for b, b_ids in ((held, ids), (last, last_ids)):
                pieces += [b, self.swapped(b, 1)]
                piece_ids += b_ids + [i ^ 1 for i in b_ids]
        return place(pieces, piece_ids, self.me, spans)


def pick(block, axis, index):
    return lax.dynamic_index_in_dim(block, index, axis, keepdims=False)


def fold(block, axis, me, distance, devices):
    digit = (me // distance) % 2
    got = swap(pick(block, axis, 1 - digit), distance, devices)
    return (pick(block, axis, digit).astype(F32) + got.astype(F32)).astype(BF)


class Scatter:
    def __init__(self, total, me, devices, plan):
        self.me, self.devices, self.plan = me, devices, plan
        self.tail = total.shape[1:]
        distance = devices // 2
        while distance >= 32:
            total = self.fold(total.reshape((2, distance) + self.tail), 0, distance)
            distance //= 2
        self.total = self.fold(total.reshape((16, 2) + self.tail), 1, 1)

    def fold(self, block, axis, distance):
        return fold(block, axis, self.me, distance, self.devices)

    def first(self):
        total = self.total.reshape((4, 2, 2) + self.tail)
        if self.plan == "split":
            z = (self.me // 8) % 4
            halves = total.reshape((2, 2, 2, 2) + self.tail)
            self.parts = [
                self.fold(pick(halves, 0, z // 2), 1, 4),
                self.fold(pick(halves, 0, 1 - z // 2), 2, 2),
            ]
        elif self.plan == "xy":
            self.parts = [self.fold(total, 1, 4)]
        else:
            self.parts = [self.fold(total, 2, 2)]
        return self.parts

    def second(self):
        z = (self.me // 8) % 4
        if self.plan == "split":
            near = self.fold(self.parts[0], 1, 2)
            away = self.fold(self.parts[1], 1, 4)
            odd = z % 2
            self.mine = [
                pick(near, 0, odd),
                pick(near, 0, 1 - odd),
                pick(away, 0, odd),
                pick(away, 0, 1 - odd),
            ]
        else:
            total = self.fold(self.parts[0], 1, 2 if self.plan == "xy" else 4)
            self.mine = [pick(total, 0, z ^ k) for k in range(4)]
        return self.mine

    def along_z(self):
        got = [swap(self.mine[k], 8 * k, self.devices).astype(F32) for k in (1, 2, 3)]
        return self.mine[0].astype(F32) + got[0] + got[1] + got[2]


def to_sequences(block, seat, members, devices):
    groups, count, width = block.shape
    parts = block.reshape(members, groups // members, count, width)
    pieces = [pick(parts, 0, seat)]
    pieces += [swap(pick(parts, 0, seat ^ k), k, devices) for k in range(1, members)]
    return jnp.stack(pieces, 1).reshape(groups * count, width)


def to_positions(block, seat, members, devices):
    pieces = [block[:, 0][None]]
    pieces += [swap(block[:, k][None], k, devices) for k in range(1, members)]
    (placed,) = place(pieces, list(range(members)), seat)
    return placed.reshape((-1,) + placed.shape[2:])


def on_device(
    inputs,
    lengths,
    query_key_value_weight,
    query_bias,
    value_bias,
    output_weight,
    output_bias,
    norm1_gain,
    norm1_shift,
    in_weight,
    in_bias,
    down_weight,
    down_bias,
    norm2_gain,
    norm2_shift,
    cotangent,
):
    groups, local_len, width = inputs.shape
    rows = groups * local_len
    members = lax.axis_size("seq")
    devices = lax.axis_size("dp") * members
    kept = groups // members
    length = local_len * members
    seat = lax.axis_index("seq")
    me = lax.axis_index("dp") * members + seat
    share = query_key_value_weight.shape[0]
    inner_width = in_weight.shape[1]
    early = pack_rows([query_bias, value_bias], share)
    qkv_gather = Gather(
        jnp.concatenate([query_key_value_weight, early], 1), me, devices, "split"
    )
    late_vectors = [
        output_bias,
        norm1_gain,
        norm1_shift,
        in_bias,
        down_bias,
        norm2_gain,
        norm2_shift,
    ]
    late = pack_rows(late_vectors, share)
    in_gather = Gather(
        jnp.concatenate([in_weight, output_weight, late], 1), me, devices, "split"
    )
    down_gather = Gather(down_weight, me, devices, "yx")
    z_done = qkv_gather.along_z()
    flat = to_sequences(inputs, seat, members, devices)
    first_done = qkv_gather.first()
    in_z_done = in_gather.along_z(z_done)
    down_z_done = down_gather.along_z(z_done)
    wide_qkv, early = qkv_gather.second([(0, 3 * width), (3 * width, early.shape[1])])
    wide_qkv = wide_qkv.reshape(width, 3 * width)
    full_query_bias, full_value_bias = [
        v.reshape(-1).astype(F32) for v in unpack_rows(early, [share, share])
    ]
    bias_vector = jnp.concatenate([full_query_bias, jnp.zeros((width,), F32), full_value_bias])
    packed = (jnp.dot(flat, wide_qkv, preferred_element_type=F32) + bias_vector).astype(BF)
    in_gather.first(packed)
    mine = lax.dynamic_slice(lengths, (seat * kept,), (kept,))
    slots = jnp.arange(length, dtype=jnp.int32)
    positions = ((slots // local_len) ^ seat) * local_len + slots % local_len
    mask = jnp.where(positions[None, :] < mine[:, None], 0.0, -1e30).astype(BF)
    mask = jnp.broadcast_to(mask[:, :, None], (kept, length, 128))
    mixed, logsum = attention_forward(packed, mask, length)
    wide_in, wide_out, late = in_gather.second(
        [(0, inner_width), (inner_width, width), (inner_width + width, late.shape[1])]
    )
    wide_in = wide_in.reshape(width, inner_width)
    wide_out = wide_out.reshape(width, width)
    (
        full_out_bias,
        gain_one,
        shift_one,
        full_in_bias,
        full_down_bias,
        gain_two,
        shift_two,
    ) = [
        v.reshape(-1).astype(F32)
        for v in unpack_rows(late, [v.shape[0] for v in late_vectors])
    ]
    down_gather.first(mixed)
    attention_branch = jnp.dot(mixed, wide_out, preferred_element_type=F32) + full_out_bias
    first, norm_one_pull = jax.vjp(
        layer_norm, flat.astype(F32) + attention_branch, gain_one, shift_one
    )
    first_low = first.astype(BF)
    cot = to_sequences(after(cotangent, first_low), seat, members, devices)
    hidden = jnp.dot(first_low, wide_in, preferred_element_type=F32) + full_in_bias
    active, gelu_pull = jax.vjp(gelu_exact, hidden)
    active_low = active.astype(BF)
    (wide_down,) = down_gather.second()
    wide_down = wide_down.reshape(inner_width, width)
    branch_two = jnp.dot(active_low, wide_down, preferred_element_type=F32) + full_down_bias
    result, norm_two_pull = jax.vjp(
        layer_norm, first_low.astype(F32) + branch_two, gain_two, shift_two
    )
    grad_second, grad_gain_two, grad_shift_two = norm_two_pull(cot.astype(F32))
    grad_branch_two = grad_second.astype(BF)
    grad_down = over_rows(active_low, grad_branch_two).astype(BF)
    down_scatter = Scatter(grad_down.reshape(devices, -1, width), me, devices, "yx")
    grad_down_bias = jnp.sum(grad_branch_two.astype(F32), 0)
    (grad_hidden,) = gelu_pull(times_transposed(grad_branch_two, wide_down))
    grad_hidden_low = grad_hidden.astype(BF)
    grad_in = over_rows(first_low, grad_hidden_low).astype(BF)
    grad_in_bias = jnp.sum(grad_hidden_low.astype(F32), 0)
    grad_hidden_low = after(grad_hidden_low, down_scatter.total)
    down_half = down_scatter.first()
    grad_first = times_transposed(grad_hidden_low, wide_in) + grad_second
    grad_residual, grad_gain_one, grad_shift_one = norm_one_pull(grad_first)
    grad_branch_one = grad_residual.astype(BF)
    grad_out = over_rows(mixed, grad_branch_one).astype(BF)
    grad_out_bias = jnp.sum(grad_branch_one.astype(F32), 0)
    outputs = to_positions(
        result.astype(BF).reshape(kept, members, local_len, width), seat, members, devices
    )
    late_sums = [
        grad_out_bias,
        grad_gain_one,
        grad_shift_one,
        grad_in_bias,
        grad_down_bias,
        grad_gain_two,
        grad_shift_two,
    ]
    late_block = pack_rows([v.reshape(devices, -1) for v in late_sums], share).astype(BF)
    in_scatter = Scatter(
        jnp.concatenate(
            [
                grad_in.reshape(devices, share, inner_width),
                grad_out.reshape(devices, share, width),
                late_block,
            ],
            2,
        ),
        me,
        devices,
        "split",
    )
    grad_mixed = times_transposed(grad_branch_one, wide_out).astype(BF)
    grad_mixed = after(grad_mixed, *down_half)
    down_quarter = down_scatter.second()
    grad_queries, grad_keys, grad_values = attention_backward(
        packed, mask, logsum, grad_mixed, length
    )
    grad_packed = jnp.concatenate([grad_queries, grad_keys, grad_values], -1)
    grad_packed = after(grad_packed, in_scatter.total, *down_quarter)
    in_half = in_scatter.first()
    down_part = down_scatter.along_z()
    grad_qkv = over_rows(flat, grad_packed).astype(BF)
    column_sums = jnp.sum(grad_packed.astype(F32), 0)
    early_sums = [column_sums[:width], column_sums[2 * width :]]
    early_block = pack_rows([v.reshape(devices, -1) for v in early_sums], share).astype(BF)
    qkv_scatter = Scatter(
        jnp.concatenate([grad_qkv.reshape(devices, share, 3 * width), early_block], 2),
        me,
        devices,
        "split",
    )
    grad_inputs = (
        times_transposed(after(grad_packed, grad_qkv), wide_qkv) + grad_residual
    ).astype(BF)
    grad_inputs = to_positions(
        grad_inputs.reshape(kept, members, local_len, width), seat, members, devices
    )
    in_scatter.second()
    in_part = in_scatter.along_z()
    qkv_scatter.first()
    qkv_scatter.second()
    qkv_part = qkv_scatter.along_z()
    early_out = unpack_rows(qkv_part[:, 3 * width :], [share, share])
    late_out = unpack_rows(
        in_part[:, inner_width + width :], [v.shape[0] for v in late_vectors]
    )
    return (
        outputs,
        grad_inputs,
        qkv_part[:, : 3 * width],
        early_out[0],
        early_out[1],
        in_part[:, inner_width : inner_width + width],
        late_out[0],
        late_out[1],
        late_out[2],
        in_part[:, :inner_width],
        late_out[3],
        down_part,
        late_out[4],
        late_out[5],
        late_out[6],
    )


def solution(mesh):
    placed = (
        P("dp", "seq", None),
        P("dp"),
        P(("dp", "seq"), None),
        P(("dp", "seq")),
        P(("dp", "seq")),
        P(("dp", "seq"), None),
        P(("dp", "seq")),
        P(("dp", "seq")),
        P(("dp", "seq")),
        P(("dp", "seq"), None),
        P(("dp", "seq")),
        P(("dp", "seq"), None),
        P(("dp", "seq")),
        P(("dp", "seq")),
        P(("dp", "seq")),
        P("dp", "seq", None),
    )
    return jax.shard_map(
        on_device,
        mesh=mesh,
        in_specs=placed,
        out_specs=(
            P("dp", "seq", None),
            P("dp", "seq", None),
            P(("dp", "seq"), None),
            P(("dp", "seq")),
            P(("dp", "seq")),
            P(("dp", "seq"), None),
            P(("dp", "seq")),
            P(("dp", "seq")),
            P(("dp", "seq")),
            P(("dp", "seq"), None),
            P(("dp", "seq")),
            P(("dp", "seq"), None),
            P(("dp", "seq")),
            P(("dp", "seq")),
            P(("dp", "seq")),
        ),
        check_vma=False,
    )
```

```python
import functools

import jax
import jax.numpy as jnp
from jax import lax
from jax.experimental import pallas as pl
from jax.experimental.pallas import tpu as pltpu
from jax.sharding import PartitionSpec as P

BF = jnp.bfloat16
F32 = jnp.float32
HD = 64
BOTH = ("dp", "seq")

def layer_norm(value, gain, shift):
    center = jnp.mean(value, -1, keepdims=True)
    centered = value - center
    spread = jnp.mean(centered * centered, -1, keepdims=True)
    return centered * lax.rsqrt(spread + 1e-12) * gain + shift


def gelu_exact(value):
    return jax.nn.gelu(value, approximate=False)


def over_rows(left, right):
    return lax.dot_general(
        left, right, (((0,), (0,)), ((), ())), preferred_element_type=jnp.float32
    )


def times_transposed(left, right):
    return lax.dot_general(
        left, right, (((1,), (1,)), ((), ())), preferred_element_type=jnp.float32
    )


def nt(a, b):
    return lax.dot_general(a, b, (((1,), (1,)), ((), ())), preferred_element_type=F32)


def tn(a, b):
    return lax.dot_general(a, b, (((0,), (0,)), ((), ())), preferred_element_type=F32)


def nn(a, b):
    return lax.dot_general(a, b, (((1,), (0,)), ((), ())), preferred_element_type=F32)


def masked_pair(q, k, bias, head, lane):
    mine = (lane >= head * HD) & (lane < (head + 1) * HD)
    spare = lane == (HD if head == 0 else 0)
    zero = jnp.zeros((), BF)
    qh = jnp.where(mine, q * BF(0.125), jnp.where(spare, jnp.ones((), BF), zero))
    kh = jnp.where(mine, k, jnp.where(spare, bias, zero))
    return qh, kh


def forward_kernel(packed_ref, mask_ref, mixed_ref, logsum_ref):
    count = packed_ref.shape[0]
    lane = lax.broadcasted_iota(jnp.int32, (count, 128), 1)
    q, k, v = (packed_ref[:, i * 128 : (i + 1) * 128] for i in range(3))
    bias = mask_ref[0]
    halves = []
    for h in range(2):
        qh, kh = masked_pair(q, k, bias, h, lane)
        scores = nt(kh, qh)
        top = jnp.max(scores, 0, keepdims=True)
        raised = jnp.exp(scores - top)
        total = jnp.sum(raised, 0, keepdims=True)
        mixed = tn(v[:, h * HD : (h + 1) * HD], raised.astype(BF))
        halves.append(mixed * (1.0 / total))
        logsum_ref[0, h : h + 1, :] = top + jnp.log(total)
    mixed_ref[...] = jnp.concatenate(halves, 0).T.astype(BF)


def backward_kernel(packed_ref, mask_ref, logsum_ref, grad_ref, out_ref, sums_ref):
    count = packed_ref.shape[0]
    lane = lax.broadcasted_iota(jnp.int32, (count, 128), 1)
    q, k, v = (packed_ref[:, i * 128 : (i + 1) * 128] for i in range(3))
    bias = mask_ref[0]
    grad = grad_ref[...]
    q_scaled, k_scaled = q * BF(0.125), k * BF(0.125)
    dq, dk, dv = [], [], []
    for h in range(2):
        qh, kh = masked_pair(q, k, bias, h, lane)
        mine = (lane >= h * HD) & (lane < (h + 1) * HD)
        vh = jnp.where(mine, v, jnp.zeros((), BF))
        probs = jnp.exp(nt(kh, qh) - logsum_ref[0, h : h + 1, :])
        grad_probs = nt(vh, grad)
        inner = jnp.sum(probs * grad_probs, 0, keepdims=True)
        grad_scores = (probs * (grad_probs - inner)).astype(BF)
        dv.append(nn(probs.astype(BF), grad))
        dk.append(nn(grad_scores, q_scaled))
        dq.append(tn(k_scaled[:, h * HD : (h + 1) * HD], grad_scores))
    low_half = lane < HD
    parts = (
        jnp.concatenate(dq, 0).T,
        jnp.where(low_half, dk[0], dk[1]),
        jnp.where(low_half, dv[0], dv[1]),
    )
    for i, part in enumerate(parts):
        rounded = part.astype(BF)
        out_ref[:, i * 128 : (i + 1) * 128] = rounded
        sums_ref[0, :, i * 128 : (i + 1) * 128] = jnp.sum(
            rounded.astype(F32), 0, keepdims=True
        )


def attention_specs(packed, length):
    rows, wide = packed.shape
    pairs, seqs = wide // 384, rows // length
    block = lambda size: pl.BlockSpec((length, size), lambda s, p: (s, p))
    mask = pl.BlockSpec((1, length, 128), lambda s, p: (s, 0, 0))
    row = lambda count, size: pl.BlockSpec((1, count, size), lambda s, p: (s * pairs + p, 0, 0))
    return rows, pairs, seqs, block, mask, row


def attention_forward(packed, mask, length):
    rows, pairs, seqs, block, mask_spec, row = attention_specs(packed, length)
    return pl.pallas_call(
        forward_kernel,
        grid=(seqs, pairs),
        in_specs=[block(384), mask_spec],
        out_specs=[block(128), row(2, length)],
        out_shape=[
            jax.ShapeDtypeStruct((rows, pairs * 128), BF),
            jax.ShapeDtypeStruct((seqs * pairs, 2, length), F32),
        ],
        compiler_params=pltpu.CompilerParams(vmem_limit_bytes=48 * 2**20),
        name="attention_forward",
        cost_estimate=pl.CostEstimate(
            flops=16 * rows * length * pairs * 128,
            bytes_accessed=rows * pairs * 1024,
            transcendentals=2 * rows * length * pairs,
        ),
    )(packed, mask)


def attention_backward(packed, mask, logsum, grad, length):
    rows, pairs, seqs, block, mask_spec, row = attention_specs(packed, length)
    return pl.pallas_call(
        backward_kernel,
        grid=(seqs, pairs),
        in_specs=[block(384), mask_spec, row(2, length), block(128)],
        out_specs=[block(384), row(1, 384)],
        out_shape=[
            jax.ShapeDtypeStruct((rows, pairs * 384), BF),
            jax.ShapeDtypeStruct((seqs * pairs, 1, 384), F32),
        ],
        compiler_params=pltpu.CompilerParams(vmem_limit_bytes=48 * 2**20),
        name="attention_backward",
        cost_estimate=pl.CostEstimate(
            flops=28 * rows * length * pairs * 128,
            bytes_accessed=rows * pairs * 1792,
            transcendentals=2 * rows * length * pairs,
        ),
    )(packed, mask, logsum, grad)


def pair_major(block):
    lead = block.shape[:-1]
    return block.reshape(lead + (3, -1, 128)).swapaxes(-3, -2).reshape(block.shape)


def kind_major(block):
    lead = block.shape[:-1]
    return block.reshape(lead + (-1, 3, 128)).swapaxes(-3, -2).reshape(block.shape)


def swap(block, distance, devices):
    return lax.ppermute(block, BOTH, [(i, i ^ distance) for i in range(devices)])


def after(value, *done):
    return lax.optimization_barrier((value,) + done)[0]


def place_kernel(ids, counts, spans, me_ref, *refs):
    pieces, rest = refs[: len(counts)], refs[len(counts) :]
    outs, sems = rest[: len(spans)], rest[len(spans)]
    me = me_ref[0]
    copies = []
    at = 0
    for piece, count in zip(pieces, counts):
        for j in range(count):
            spot = me ^ ids[at]
            for out, (start, size) in zip(outs, spans):
                source = piece.at[j] if len(spans) == 1 else piece.at[j, :, pl.ds(start, size)]
                copy = pltpu.make_async_copy(source, out.at[spot], sems.at[len(copies)])
                copy.start()
                copies.append(copy)
            at += 1
    for copy in copies:
        copy.wait()


def place(pieces, ids, me, spans=None):
    counts = [p.shape[0] for p in pieces]
    total = sum(counts)
    tail = pieces[0].shape[1:]
    spans = spans or [(0, tail[-1])]
    any_space = pl.BlockSpec(memory_space=pl.ANY)
    moved = 2 * sum(p.size * p.dtype.itemsize for p in pieces)
    return pl.pallas_call(
        functools.partial(place_kernel, ids, counts, spans),
        in_specs=[pl.BlockSpec(memory_space=pltpu.SMEM)] + [any_space] * len(pieces),
        out_specs=[pl.BlockSpec(memory_space=pltpu.VMEM)] * len(spans),
        out_shape=[
            jax.ShapeDtypeStruct((total,) + tail[:-1] + (size,), pieces[0].dtype)
            for _, size in spans
        ],
        scratch_shapes=[pltpu.SemaphoreType.DMA((total * len(spans),))],
        compiler_params=pltpu.CompilerParams(vmem_limit_bytes=32 * 2**20),
        cost_estimate=pl.CostEstimate(flops=0, bytes_accessed=moved, transcendentals=0),
        name="place_blocks",
    )(me.reshape(1), *pieces)


def pack_rows(vectors, share):
    lead = vectors[0].shape[:-1]
    columns = []
    for at in range(0, len(vectors), share):
        rows = []
        for v in vectors[at : at + share]:
            rows.append(jnp.pad(v, [(0, 0)] * len(lead) + [(0, 128 - v.shape[-1])]))
        block = jnp.stack(rows, -2)
        columns.append(
            jnp.pad(block, [(0, 0)] * len(lead) + [(0, share - len(rows)), (0, 0)])
        )
    return columns[0] if len(columns) == 1 else jnp.concatenate(columns, -1)


def unpack_rows(block, sizes):
    share = block.shape[-2]
    out = []
    for i, size in enumerate(sizes):
        start = i // share * 128
        out.append(block[..., i % share, start : start + size])
    return out


class Gather:
    def __init__(self, block, me, devices, plan):
        self.me, self.devices, self.plan = me, devices, plan
        self.own, self.own_ids = block[None], [0]

    def swapped(self, block, distance):
        return swap(block, distance, self.devices)

    def along_z(self, *done):
        own, own_ids = self.own, self.own_ids
        if done:
            own = after(own, *done)
        distance = 32
        while distance < self.devices:
            own = jnp.concatenate([own, self.swapped(own, distance)])
            own_ids = own_ids + [i ^ distance for i in own_ids]
            distance *= 2
        far = [own] + [self.swapped(own, 8 * k) for k in (1, 2, 3)]
        far_ids = [[i ^ (8 * k) for i in own_ids] for k in range(4)]
        if self.plan == "split":
            parts = [((0, 1), (4, 2)), ((2, 3), (2, 4))]
        else:
            parts = [((0, 1, 2, 3), (4, 2) if self.plan == "xy" else (2, 4))]
        self.parts = []
        for which, order in parts:
            held = jnp.concatenate([far[k] for k in which])
            self.parts.append((held, [i for k in which for i in far_ids[k]], order))
        return far[1]

    def first(self, *done):
        grown = []
        for held, ids, order in self.parts:
            if done:
                held = after(held, *done)
            got = self.swapped(held, order[0])
            grown.append(
                (jnp.concatenate([held, got]), ids + [i ^ order[0] for i in ids], order)
            )
        self.parts = grown
        return grown[0][0]

    def second(self, *done):
        grown = []
        for held, ids, order in self.parts:
            if done:
                held = after(held, *done)
            grown.append((held, ids, self.swapped(held, order[1]), [i ^ order[1] for i in ids]))
        self.parts = grown
        return [part[2] for part in grown]

    def finish(self, spans=None):
        pieces, piece_ids = [], []
        for held, ids, last, last_ids in self.parts:
            for b, b_ids in ((held, ids), (last, last_ids)):
                pieces += [b, self.swapped(b, 1)]
                piece_ids += b_ids + [i ^ 1 for i in b_ids]
        return place(pieces, piece_ids, self.me, spans)


def pick(block, axis, index):
    return lax.dynamic_index_in_dim(block, index, axis, keepdims=False)


def fold(block, axis, me, distance, devices):
    digit = (me // distance) % 2
    got = swap(pick(block, axis, 1 - digit), distance, devices)
    return (pick(block, axis, digit).astype(F32) + got.astype(F32)).astype(BF)


class Scatter:
    def __init__(self, total, me, devices, plan):
        self.me, self.devices, self.plan = me, devices, plan
        self.tail = total.shape[1:]
        distance = devices // 2
        while distance >= 32:
            total = self.fold(total.reshape((2, distance) + self.tail), 0, distance)
            distance //= 2
        self.total = self.fold(total.reshape((16, 2) + self.tail), 1, 1)

    def fold(self, block, axis, distance):
        return fold(block, axis, self.me, distance, self.devices)

    def first(self):
        total = self.total.reshape((4, 2, 2) + self.tail)
        if self.plan == "split":
            z = (self.me // 8) % 4
            halves = total.reshape((2, 2, 2, 2) + self.tail)
            self.parts = [
                self.fold(pick(halves, 0, z // 2), 1, 4),
                self.fold(pick(halves, 0, 1 - z // 2), 2, 2),
            ]
        elif self.plan == "xy":
            self.parts = [self.fold(total, 1, 4)]
        else:
            self.parts = [self.fold(total, 2, 2)]
        return self.parts

    def second(self):
        z = (self.me // 8) % 4
        if self.plan == "split":
            near = self.fold(self.parts[0], 1, 2)
            away = self.fold(self.parts[1], 1, 4)
            odd = z % 2
            self.mine = [
                pick(near, 0, odd),
                pick(near, 0, 1 - odd),
                pick(away, 0, odd),
                pick(away, 0, 1 - odd),
            ]
        else:
            total = self.fold(self.parts[0], 1, 2 if self.plan == "xy" else 4)
            self.mine = [pick(total, 0, z ^ k) for k in range(4)]
        return self.mine

    def along_z(self):
        got = [swap(self.mine[k], 8 * k, self.devices).astype(F32) for k in (1, 2, 3)]
        return self.mine[0].astype(F32) + got[0] + got[1] + got[2]


def to_sequences(block, seat, members, devices):
    groups, count, width = block.shape
    parts = block.reshape(members, groups // members, count, width)
    pieces = [pick(parts, 0, seat)]
    pieces += [swap(pick(parts, 0, seat ^ k), k, devices) for k in range(1, members)]
    return jnp.stack(pieces, 1).reshape(groups * count, width)


def send_positions(block, members, devices):
    pieces = [block[:, 0][None]]
    return pieces + [swap(block[:, k][None], k, devices) for k in range(1, members)]


def put_positions(pieces, seat, *done):
    pieces = [after(pieces[0], *done)] + pieces[1:]
    (placed,) = place(pieces, list(range(len(pieces))), seat)
    return placed.reshape((-1,) + placed.shape[2:])


def on_device(
    inputs,
    lengths,
    query_key_value_weight,
    query_bias,
    value_bias,
    output_weight,
    output_bias,
    norm1_gain,
    norm1_shift,
    in_weight,
    in_bias,
    down_weight,
    down_bias,
    norm2_gain,
    norm2_shift,
    cotangent,
):
    groups, local_len, width = inputs.shape
    rows = groups * local_len
    members = lax.axis_size("seq")
    devices = lax.axis_size("dp") * members
    kept = groups // members
    length = local_len * members
    seat = lax.axis_index("seq")
    me = lax.axis_index("dp") * members + seat
    share = query_key_value_weight.shape[0]
    inner_width = in_weight.shape[1]
    early = pack_rows([query_bias, value_bias], share)
    qkv_gather = Gather(
        jnp.concatenate([pair_major(query_key_value_weight), early], 1), me, devices, "split"
    )
    late_vectors = [
        output_bias,
        norm1_gain,
        norm1_shift,
        in_bias,
        down_bias,
        norm2_gain,
        norm2_shift,
    ]
    late = pack_rows(late_vectors, share)
    in_gather = Gather(
        jnp.concatenate([in_weight, output_weight, late], 1), me, devices, "split"
    )
    down_gather = Gather(down_weight, me, devices, "yx")
    qkv_gather.along_z()
    flat = to_sequences(inputs, seat, members, devices)
    first_done = qkv_gather.first()
    last_done = qkv_gather.second()
    in_gather.along_z(first_done)
    in_gather.first(*last_done)
    wide_qkv, early = qkv_gather.finish([(0, 3 * width), (3 * width, early.shape[1])])
    in_gather.second(wide_qkv)
    wide_qkv = wide_qkv.reshape(width, 3 * width)
    full_query_bias, full_value_bias = [
        v.reshape(-1).astype(F32) for v in unpack_rows(early, [share, share])
    ]
    bias_vector = jnp.concatenate([full_query_bias, jnp.zeros((width,), F32), full_value_bias])
    packed = jnp.dot(flat, wide_qkv, preferred_element_type=F32) + pair_major(bias_vector)
    packed = packed.astype(BF)
    down_gather.along_z(packed)
    mine = lax.dynamic_slice(lengths, (seat * kept,), (kept,))
    slots = jnp.arange(length, dtype=jnp.int32)
    positions = ((slots // local_len) ^ seat) * local_len + slots % local_len
    mask = jnp.where(positions[None, :] < mine[:, None], 0.0, -1e30).astype(BF)
    mask = jnp.broadcast_to(mask[:, :, None], (kept, length, 128))
    mixed, logsum = attention_forward(packed, mask, length)
    wide_in, wide_out, late = in_gather.finish(
        [(0, inner_width), (inner_width, width), (inner_width + width, late.shape[1])]
    )
    wide_in = wide_in.reshape(width, inner_width)
    wide_out = wide_out.reshape(width, width)
    (
        full_out_bias,
        gain_one,
        shift_one,
        full_in_bias,
        full_down_bias,
        gain_two,
        shift_two,
    ) = [
        v.reshape(-1).astype(F32)
        for v in unpack_rows(late, [v.shape[0] for v in late_vectors])
    ]
    down_gather.first(mixed)
    attention_branch = jnp.dot(mixed, wide_out, preferred_element_type=F32) + full_out_bias
    first, norm_one_pull = jax.vjp(
        layer_norm, flat.astype(F32) + attention_branch, gain_one, shift_one
    )
    first_low = first.astype(BF)
    cot = to_sequences(after(cotangent, first_low), seat, members, devices)
    down_gather.second(first_low)
    hidden = jnp.dot(first_low, wide_in, preferred_element_type=F32) + full_in_bias
    active, gelu_pull = jax.vjp(gelu_exact, hidden)
    active_low = active.astype(BF)
    (wide_down,) = down_gather.finish()
    wide_down = wide_down.reshape(inner_width, width)
    branch_two = jnp.dot(active_low, wide_down, preferred_element_type=F32) + full_down_bias
    result, norm_two_pull = jax.vjp(
        layer_norm, first_low.astype(F32) + branch_two, gain_two, shift_two
    )
    outputs = send_positions(
        result.astype(BF).reshape(kept, members, local_len, width), members, devices
    )
    grad_second, grad_gain_two, grad_shift_two = norm_two_pull(cot.astype(F32))
    grad_branch_two = grad_second.astype(BF)
    grad_down = over_rows(active_low, grad_branch_two).astype(BF)
    down_scatter = Scatter(grad_down.reshape(devices, -1, width), me, devices, "yx")
    grad_down_bias = jnp.sum(grad_branch_two.astype(F32), 0)
    (grad_hidden,) = gelu_pull(times_transposed(grad_branch_two, wide_down))
    grad_hidden_low = grad_hidden.astype(BF)
    grad_in = over_rows(first_low, grad_hidden_low).astype(BF)
    grad_in_bias = jnp.sum(grad_hidden_low.astype(F32), 0)
    grad_hidden_low = after(grad_hidden_low, down_scatter.total)
    down_half = down_scatter.first()
    grad_first = times_transposed(grad_hidden_low, wide_in) + grad_second
    grad_residual, grad_gain_one, grad_shift_one = norm_one_pull(grad_first)
    grad_branch_one = grad_residual.astype(BF)
    grad_out = over_rows(mixed, grad_branch_one).astype(BF)
    grad_out_bias = jnp.sum(grad_branch_one.astype(F32), 0)
    late_sums = [
        grad_out_bias,
        grad_gain_one,
        grad_shift_one,
        grad_in_bias,
        grad_down_bias,
        grad_gain_two,
        grad_shift_two,
    ]
    late_block = pack_rows([v.reshape(devices, -1) for v in late_sums], share).astype(BF)
    in_scatter = Scatter(
        jnp.concatenate(
            [
                grad_in.reshape(devices, share, inner_width),
                grad_out.reshape(devices, share, width),
                late_block,
            ],
            2,
        ),
        me,
        devices,
        "split",
    )
    grad_mixed = times_transposed(grad_branch_one, wide_out).astype(BF)
    grad_mixed = after(grad_mixed, in_scatter.total, *down_half)
    in_half = in_scatter.first()
    down_quarter = down_scatter.second()
    grad_packed, column_sums = attention_backward(packed, mask, logsum, grad_mixed, length)
    grad_packed = after(grad_packed, *down_quarter, *in_half)
    down_part = down_scatter.along_z()
    in_quarter = in_scatter.second()
    grad_qkv = over_rows(flat, grad_packed).astype(BF)
    column_sums = kind_major(column_sums.reshape(kept, 3 * width).sum(0))
    early_sums = [column_sums[:width], column_sums[2 * width :]]
    early_block = pack_rows([v.reshape(devices, -1) for v in early_sums], share).astype(BF)
    qkv_scatter = Scatter(
        jnp.concatenate([grad_qkv.reshape(devices, share, 3 * width), early_block], 2),
        me,
        devices,
        "split",
    )
    grad_inputs = (
        times_transposed(after(grad_packed, grad_qkv), wide_qkv) + grad_residual
    ).astype(BF)
    grad_inputs = send_positions(
        grad_inputs.reshape(kept, members, local_len, width), members, devices
    )
    qkv_half = qkv_scatter.first()
    in_part = in_scatter.along_z()
    outputs = put_positions(outputs, seat, qkv_scatter.total)
    qkv_quarter = qkv_scatter.second()
    qkv_part = qkv_scatter.along_z()
    grad_inputs = put_positions(grad_inputs, seat, *qkv_half)
    early_out = unpack_rows(qkv_part[:, 3 * width :], [share, share])
    late_out = unpack_rows(
        in_part[:, inner_width + width :], [v.shape[0] for v in late_vectors]
    )
    return (
        outputs,
        grad_inputs,
        kind_major(qkv_part[:, : 3 * width]),
        early_out[0],
        early_out[1],
        in_part[:, inner_width : inner_width + width],
        late_out[0],
        late_out[1],
        late_out[2],
        in_part[:, :inner_width],
        late_out[3],
        down_part,
        late_out[4],
        late_out[5],
        late_out[6],
    )


def solution(mesh):
    placed = (
        P("dp", "seq", None),
        P("dp"),
        P(("dp", "seq"), None),
        P(("dp", "seq")),
        P(("dp", "seq")),
        P(("dp", "seq"), None),
        P(("dp", "seq")),
        P(("dp", "seq")),
        P(("dp", "seq")),
        P(("dp", "seq"), None),
        P(("dp", "seq")),
        P(("dp", "seq"), None),
        P(("dp", "seq")),
        P(("dp", "seq")),
        P(("dp", "seq")),
        P("dp", "seq", None),
    )
    return jax.shard_map(
        on_device,
        mesh=mesh,
        in_specs=placed,
        out_specs=(
            P("dp", "seq", None),
            P("dp", "seq", None),
            P(("dp", "seq"), None),
            P(("dp", "seq")),
            P(("dp", "seq")),
            P(("dp", "seq"), None),
            P(("dp", "seq")),
            P(("dp", "seq")),
            P(("dp", "seq")),
            P(("dp", "seq"), None),
            P(("dp", "seq")),
            P(("dp", "seq"), None),
            P(("dp", "seq")),
            P(("dp", "seq")),
            P(("dp", "seq")),
        ),
        check_vma=False,
    )
```

```python
import functools

import jax
import jax.numpy as jnp
from jax import lax
from jax.experimental import pallas as pl
from jax.experimental.pallas import tpu as pltpu
from jax.sharding import PartitionSpec as P

BF = jnp.bfloat16
F32 = jnp.float32
HD = 64
BOTH = ("dp", "seq")

def layer_norm(value, gain, shift):
    center = jnp.mean(value, -1, keepdims=True)
    centered = value - center
    spread = jnp.mean(centered * centered, -1, keepdims=True)
    return centered * lax.rsqrt(spread + 1e-12) * gain + shift


def over_rows(left, right):
    return lax.dot_general(
        left, right, (((0,), (0,)), ((), ())), preferred_element_type=jnp.float32
    )


def times_transposed(left, right):
    return lax.dot_general(
        left, right, (((1,), (1,)), ((), ())), preferred_element_type=jnp.float32
    )


def nt(a, b):
    return lax.dot_general(a, b, (((1,), (1,)), ((), ())), preferred_element_type=F32)


def tn(a, b):
    return lax.dot_general(a, b, (((0,), (0,)), ((), ())), preferred_element_type=F32)


def nn(a, b):
    return lax.dot_general(a, b, (((1,), (0,)), ((), ())), preferred_element_type=F32)


def masked_pair(q, k, bias, head, lane):
    mine = (lane >= head * HD) & (lane < (head + 1) * HD)
    spare = lane == (HD if head == 0 else 0)
    zero = jnp.zeros((), BF)
    qh = jnp.where(mine, q * BF(0.125), jnp.where(spare, jnp.ones((), BF), zero))
    kh = jnp.where(mine, k, jnp.where(spare, bias, zero))
    return qh, kh


def forward_kernel(packed_ref, mask_ref, mixed_ref, logsum_ref):
    count = packed_ref.shape[0]
    lane = lax.broadcasted_iota(jnp.int32, (count, 128), 1)
    q, k, v = (packed_ref[:, i * 128 : (i + 1) * 128] for i in range(3))
    bias = mask_ref[0]
    halves = []
    for h in range(2):
        qh, kh = masked_pair(q, k, bias, h, lane)
        scores = nt(kh, qh)
        top = jnp.max(scores, 0, keepdims=True)
        raised = jnp.exp(scores - top)
        total = jnp.sum(raised, 0, keepdims=True)
        mixed = tn(v[:, h * HD : (h + 1) * HD], raised.astype(BF))
        halves.append(mixed * (1.0 / total))
        logsum_ref[0, h : h + 1, :] = top + jnp.log(total)
    mixed_ref[...] = jnp.concatenate(halves, 0).T.astype(BF)


def backward_kernel(packed_ref, mask_ref, logsum_ref, grad_ref, out_ref, sums_ref):
    count = packed_ref.shape[0]
    lane = lax.broadcasted_iota(jnp.int32, (count, 128), 1)
    q, k, v = (packed_ref[:, i * 128 : (i + 1) * 128] for i in range(3))
    bias = mask_ref[0]
    grad = grad_ref[...]
    q_scaled, k_scaled = q * BF(0.125), k * BF(0.125)
    dq, dk, dv = [], [], []
    for h in range(2):
        qh, kh = masked_pair(q, k, bias, h, lane)
        mine = (lane >= h * HD) & (lane < (h + 1) * HD)
        vh = jnp.where(mine, v, jnp.zeros((), BF))
        probs = jnp.exp(nt(kh, qh) - logsum_ref[0, h : h + 1, :])
        grad_probs = nt(vh, grad)
        inner = jnp.sum(probs * grad_probs, 0, keepdims=True)
        grad_scores = (probs * (grad_probs - inner)).astype(BF)
        dv.append(nn(probs.astype(BF), grad))
        dk.append(nn(grad_scores, q_scaled))
        dq.append(tn(k_scaled[:, h * HD : (h + 1) * HD], grad_scores))
    low_half = lane < HD
    parts = (
        jnp.concatenate(dq, 0).T,
        jnp.where(low_half, dk[0], dk[1]),
        jnp.where(low_half, dv[0], dv[1]),
    )
    for i, part in enumerate(parts):
        rounded = part.astype(BF)
        out_ref[:, i * 128 : (i + 1) * 128] = rounded
        sums_ref[0, :, i * 128 : (i + 1) * 128] = jnp.sum(
            rounded.astype(F32), 0, keepdims=True
        )


def attention_specs(packed, length):
    rows, wide = packed.shape
    pairs, seqs = wide // 384, rows // length
    block = lambda size: pl.BlockSpec((length, size), lambda s, p: (s, p))
    mask = pl.BlockSpec((1, length, 128), lambda s, p: (s, 0, 0))
    row = lambda count, size: pl.BlockSpec((1, count, size), lambda s, p: (s * pairs + p, 0, 0))
    return rows, pairs, seqs, block, mask, row


def attention_forward(packed, mask, length):
    rows, pairs, seqs, block, mask_spec, row = attention_specs(packed, length)
    return pl.pallas_call(
        forward_kernel,
        grid=(seqs, pairs),
        in_specs=[block(384), mask_spec],
        out_specs=[block(128), row(2, length)],
        out_shape=[
            jax.ShapeDtypeStruct((rows, pairs * 128), BF),
            jax.ShapeDtypeStruct((seqs * pairs, 2, length), F32),
        ],
        compiler_params=pltpu.CompilerParams(vmem_limit_bytes=48 * 2**20),
        name="attention_forward",
        cost_estimate=pl.CostEstimate(
            flops=16 * rows * length * pairs * 128,
            bytes_accessed=rows * pairs * 1024,
            transcendentals=2 * rows * length * pairs,
        ),
    )(packed, mask)


def attention_backward(packed, mask, logsum, grad, length):
    rows, pairs, seqs, block, mask_spec, row = attention_specs(packed, length)
    return pl.pallas_call(
        backward_kernel,
        grid=(seqs, pairs),
        in_specs=[block(384), mask_spec, row(2, length), block(128)],
        out_specs=[block(384), row(1, 384)],
        out_shape=[
            jax.ShapeDtypeStruct((rows, pairs * 384), BF),
            jax.ShapeDtypeStruct((seqs * pairs, 1, 384), F32),
        ],
        compiler_params=pltpu.CompilerParams(vmem_limit_bytes=48 * 2**20),
        name="attention_backward",
        cost_estimate=pl.CostEstimate(
            flops=28 * rows * length * pairs * 128,
            bytes_accessed=rows * pairs * 1792,
            transcendentals=2 * rows * length * pairs,
        ),
    )(packed, mask, logsum, grad)


def pair_major(block):
    lead = block.shape[:-1]
    return block.reshape(lead + (3, -1, 128)).swapaxes(-3, -2).reshape(block.shape)


def kind_major(block):
    lead = block.shape[:-1]
    return block.reshape(lead + (-1, 3, 128)).swapaxes(-3, -2).reshape(block.shape)


def feed_forward_kernel(step, x_ref, w_ref, b_ref, active_ref, slope_ref):
    x = x_ref[...]
    for start in range(0, w_ref.shape[1], step):
        part = slice(start, start + step)
        hidden = nn(x, w_ref[:, part]) + b_ref[:, part]
        bell = jnp.exp(hidden * hidden * -0.5)
        share = 0.5 * (1.0 + lax.erf(hidden * 0.7071067811865476))
        active_ref[:, part] = (hidden * share).astype(BF)
        slope_ref[:, part] = (share + hidden * bell * 0.3989422804014327).astype(BF)


def feed_forward(x, weight, bias):
    rows, width = x.shape
    inner = weight.shape[1]
    block = 256
    out = jax.ShapeDtypeStruct((rows, inner), BF)
    return pl.pallas_call(
        functools.partial(feed_forward_kernel, 512),
        grid=(rows // block,),
        in_specs=[
            pl.BlockSpec((block, width), lambda i: (i, 0)),
            pl.BlockSpec((width, inner), lambda i: (0, 0)),
            pl.BlockSpec((1, inner), lambda i: (0, 0)),
        ],
        out_specs=[pl.BlockSpec((block, inner), lambda i: (i, 0))] * 2,
        out_shape=[out, out],
        compiler_params=pltpu.CompilerParams(vmem_limit_bytes=48 * 2**20),
        name="feed_forward",
        cost_estimate=pl.CostEstimate(
            flops=2 * rows * width * inner,
            bytes_accessed=4 * rows * inner + 2 * width * inner,
            transcendentals=2 * rows * inner,
        ),
    )(x, weight, bias)


def swap(block, distance, devices):
    return lax.ppermute(block, BOTH, [(i, i ^ distance) for i in range(devices)])


def after(value, *done):
    return lax.optimization_barrier((value,) + done)[0]


def place_kernel(ids, counts, spans, me_ref, *refs):
    pieces, rest = refs[: len(counts)], refs[len(counts) :]
    outs, sems = rest[: len(spans)], rest[len(spans)]
    me = me_ref[0]
    copies = []
    at = 0
    for piece, count in zip(pieces, counts):
        for j in range(count):
            spot = me ^ ids[at]
            for out, (start, size) in zip(outs, spans):
                source = piece.at[j] if len(spans) == 1 else piece.at[j, :, pl.ds(start, size)]
                copy = pltpu.make_async_copy(source, out.at[spot], sems.at[len(copies)])
                copy.start()
                copies.append(copy)
            at += 1
    for copy in copies:
        copy.wait()


def place(pieces, ids, me, spans=None):
    counts = [p.shape[0] for p in pieces]
    total = sum(counts)
    tail = pieces[0].shape[1:]
    spans = spans or [(0, tail[-1])]
    any_space = pl.BlockSpec(memory_space=pl.ANY)
    moved = 2 * sum(p.size * p.dtype.itemsize for p in pieces)
    return pl.pallas_call(
        functools.partial(place_kernel, ids, counts, spans),
        in_specs=[pl.BlockSpec(memory_space=pltpu.SMEM)] + [any_space] * len(pieces),
        out_specs=[pl.BlockSpec(memory_space=pltpu.VMEM)] * len(spans),
        out_shape=[
            jax.ShapeDtypeStruct((total,) + tail[:-1] + (size,), pieces[0].dtype)
            for _, size in spans
        ],
        scratch_shapes=[pltpu.SemaphoreType.DMA((total * len(spans),))],
        compiler_params=pltpu.CompilerParams(vmem_limit_bytes=32 * 2**20),
        cost_estimate=pl.CostEstimate(flops=0, bytes_accessed=moved, transcendentals=0),
        name="place_blocks",
    )(me.reshape(1), *pieces)


def pack_rows(vectors, share):
    lead = vectors[0].shape[:-1]
    columns = []
    for at in range(0, len(vectors), share):
        rows = []
        for v in vectors[at : at + share]:
            rows.append(jnp.pad(v, [(0, 0)] * len(lead) + [(0, 128 - v.shape[-1])]))
        block = jnp.stack(rows, -2)
        columns.append(
            jnp.pad(block, [(0, 0)] * len(lead) + [(0, share - len(rows)), (0, 0)])
        )
    return columns[0] if len(columns) == 1 else jnp.concatenate(columns, -1)


def unpack_rows(block, sizes):
    share = block.shape[-2]
    out = []
    for i, size in enumerate(sizes):
        start = i // share * 128
        out.append(block[..., i % share, start : start + size])
    return out


class Gather:
    def __init__(self, block, me, devices, plan):
        self.me, self.devices, self.plan = me, devices, plan
        self.own, self.own_ids = block[None], [0]

    def swapped(self, block, distance):
        return swap(block, distance, self.devices)

    def along_z(self, *done):
        own, own_ids = self.own, self.own_ids
        if done:
            own = after(own, *done)
        distance = 32
        while distance < self.devices:
            own = jnp.concatenate([own, self.swapped(own, distance)])
            own_ids = own_ids + [i ^ distance for i in own_ids]
            distance *= 2
        far = [own] + [self.swapped(own, 8 * k) for k in (1, 2, 3)]
        far_ids = [[i ^ (8 * k) for i in own_ids] for k in range(4)]
        if self.plan == "split":
            parts = [((0, 1), (4, 2)), ((2, 3), (2, 4))]
        else:
            parts = [((0, 1, 2, 3), (4, 2) if self.plan == "xy" else (2, 4))]
        self.parts = []
        for which, order in parts:
            held = jnp.concatenate([far[k] for k in which])
            self.parts.append((held, [i for k in which for i in far_ids[k]], order))
        return far[1]

    def first(self, *done):
        grown = []
        for held, ids, order in self.parts:
            if done:
                held = after(held, *done)
            got = self.swapped(held, order[0])
            grown.append(
                (jnp.concatenate([held, got]), ids + [i ^ order[0] for i in ids], order)
            )
        self.parts = grown
        return grown[0][0]

    def second(self, *done):
        grown = []
        for held, ids, order in self.parts:
            if done:
                held = after(held, *done)
            grown.append((held, ids, self.swapped(held, order[1]), [i ^ order[1] for i in ids]))
        self.parts = grown
        return [part[2] for part in grown]

    def finish(self, spans=None, *done):
        pieces, piece_ids = [], []
        for held, ids, last, last_ids in self.parts:
            if done:
                last = after(last, *done)
            for b, b_ids in ((held, ids), (last, last_ids)):
                pieces += [b, self.swapped(b, 1)]
                piece_ids += b_ids + [i ^ 1 for i in b_ids]
        return place(pieces, piece_ids, self.me, spans)


def pick(block, axis, index):
    return lax.dynamic_index_in_dim(block, index, axis, keepdims=False)


def fold(block, axis, me, distance, devices):
    digit = (me // distance) % 2
    got = swap(pick(block, axis, 1 - digit), distance, devices)
    return (pick(block, axis, digit).astype(F32) + got.astype(F32)).astype(BF)


class Scatter:
    def __init__(self, total, me, devices, plan):
        self.me, self.devices, self.plan = me, devices, plan
        self.tail = total.shape[1:]
        distance = devices // 2
        while distance >= 32:
            total = self.fold(total.reshape((2, distance) + self.tail), 0, distance)
            distance //= 2
        self.total = self.fold(total.reshape((16, 2) + self.tail), 1, 1)

    def fold(self, block, axis, distance):
        return fold(block, axis, self.me, distance, self.devices)

    def first(self):
        total = self.total.reshape((4, 2, 2) + self.tail)
        if self.plan == "split":
            z = (self.me // 8) % 4
            halves = total.reshape((2, 2, 2, 2) + self.tail)
            self.parts = [
                self.fold(pick(halves, 0, z // 2), 1, 4),
                self.fold(pick(halves, 0, 1 - z // 2), 2, 2),
            ]
        elif self.plan == "xy":
            self.parts = [self.fold(total, 1, 4)]
        else:
            self.parts = [self.fold(total, 2, 2)]
        return self.parts

    def second(self):
        z = (self.me // 8) % 4
        if self.plan == "split":
            near = self.fold(self.parts[0], 1, 2)
            away = self.fold(self.parts[1], 1, 4)
            odd = z % 2
            self.mine = [
                pick(near, 0, odd),
                pick(near, 0, 1 - odd),
                pick(away, 0, odd),
                pick(away, 0, 1 - odd),
            ]
        else:
            total = self.fold(self.parts[0], 1, 2 if self.plan == "xy" else 4)
            self.mine = [pick(total, 0, z ^ k) for k in range(4)]
        return self.mine

    def along_z(self):
        got = [swap(self.mine[k], 8 * k, self.devices).astype(F32) for k in (1, 2, 3)]
        return self.mine[0].astype(F32) + got[0] + got[1] + got[2]


def to_sequences(block, seat, members, devices):
    groups, count, width = block.shape
    parts = block.reshape(members, groups // members, count, width)
    pieces = [pick(parts, 0, seat)]
    pieces += [swap(pick(parts, 0, seat ^ k), k, devices) for k in range(1, members)]
    return jnp.stack(pieces, 1).reshape(groups * count, width)


def send_positions(block, members, devices):
    pieces = [block[:, 0][None]]
    return pieces + [swap(block[:, k][None], k, devices) for k in range(1, members)]


def put_positions(pieces, seat, *done):
    pieces = [after(pieces[0], *done)] + pieces[1:]
    (placed,) = place(pieces, list(range(len(pieces))), seat)
    return placed.reshape((-1,) + placed.shape[2:])


def on_device(
    inputs,
    lengths,
    query_key_value_weight,
    query_bias,
    value_bias,
    output_weight,
    output_bias,
    norm1_gain,
    norm1_shift,
    in_weight,
    in_bias,
    down_weight,
    down_bias,
    norm2_gain,
    norm2_shift,
    cotangent,
):
    groups, local_len, width = inputs.shape
    rows = groups * local_len
    members = lax.axis_size("seq")
    devices = lax.axis_size("dp") * members
    kept = groups // members
    length = local_len * members
    seat = lax.axis_index("seq")
    me = lax.axis_index("dp") * members + seat
    share = query_key_value_weight.shape[0]
    inner_width = in_weight.shape[1]
    early = pack_rows([query_bias, value_bias], share)
    qkv_gather = Gather(
        jnp.concatenate([pair_major(query_key_value_weight), early], 1), me, devices, "split"
    )
    late_vectors = [
        output_bias,
        norm1_gain,
        norm1_shift,
        in_bias,
        down_bias,
        norm2_gain,
        norm2_shift,
    ]
    late = pack_rows(late_vectors, share)
    in_gather = Gather(
        jnp.concatenate([in_weight, output_weight, late], 1), me, devices, "split"
    )
    down_gather = Gather(down_weight, me, devices, "yx")
    qkv_gather.along_z()
    flat = to_sequences(inputs, seat, members, devices)
    first_done = qkv_gather.first()
    last_done = qkv_gather.second(flat)
    in_gather.along_z(first_done)
    in_gather.first(*last_done)
    wide_qkv, early = qkv_gather.finish([(0, 3 * width), (3 * width, early.shape[1])])
    in_gather.second(wide_qkv)
    wide_qkv = wide_qkv.reshape(width, 3 * width)
    full_query_bias, full_value_bias = [
        v.reshape(-1).astype(F32) for v in unpack_rows(early, [share, share])
    ]
    bias_vector = jnp.concatenate([full_query_bias, jnp.zeros((width,), F32), full_value_bias])
    packed = jnp.dot(flat, wide_qkv, preferred_element_type=F32) + pair_major(bias_vector)
    packed = packed.astype(BF)
    down_gather.along_z(packed)
    mine = lax.dynamic_slice(lengths, (seat * kept,), (kept,))
    slots = jnp.arange(length, dtype=jnp.int32)
    positions = ((slots // local_len) ^ seat) * local_len + slots % local_len
    mask = jnp.where(positions[None, :] < mine[:, None], 0.0, -1e30).astype(BF)
    mask = jnp.broadcast_to(mask[:, :, None], (kept, length, 128))
    mixed, logsum = attention_forward(packed, mask, length)
    wide_in, wide_out, late = in_gather.finish(
        [(0, inner_width), (inner_width, width), (inner_width + width, late.shape[1])], mixed
    )
    wide_in = wide_in.reshape(width, inner_width)
    wide_out = wide_out.reshape(width, width)
    (
        full_out_bias,
        gain_one,
        shift_one,
        full_in_bias,
        full_down_bias,
        gain_two,
        shift_two,
    ) = [
        v.reshape(-1).astype(F32)
        for v in unpack_rows(late, [v.shape[0] for v in late_vectors])
    ]
    down_gather.first(mixed)
    attention_branch = jnp.dot(mixed, wide_out, preferred_element_type=F32) + full_out_bias
    first, norm_one_pull = jax.vjp(
        layer_norm, flat.astype(F32) + attention_branch, gain_one, shift_one
    )
    first_low = first.astype(BF)
    cot = to_sequences(after(cotangent, first_low), seat, members, devices)
    down_gather.second(first_low)
    active_low, slope = feed_forward(first_low, wide_in, full_in_bias[None])
    (wide_down,) = down_gather.finish(None, active_low)
    wide_down = wide_down.reshape(inner_width, width)
    branch_two = jnp.dot(active_low, wide_down, preferred_element_type=F32) + full_down_bias
    result, norm_two_pull = jax.vjp(
        layer_norm, first_low.astype(F32) + branch_two, gain_two, shift_two
    )
    outputs = send_positions(
        result.astype(BF).reshape(kept, members, local_len, width), members, devices
    )
    grad_second, grad_gain_two, grad_shift_two = norm_two_pull(cot.astype(F32))
    grad_branch_two = grad_second.astype(BF)
    grad_down = over_rows(active_low, grad_branch_two).astype(BF)
    down_scatter = Scatter(grad_down.reshape(devices, -1, width), me, devices, "split")
    grad_down_bias = jnp.sum(grad_branch_two.astype(F32), 0)
    grad_hidden_low = (
        times_transposed(grad_branch_two, wide_down) * slope.astype(F32)
    ).astype(BF)
    grad_in = over_rows(first_low, grad_hidden_low).astype(BF)
    grad_in_bias = jnp.sum(grad_hidden_low.astype(F32), 0)
    grad_hidden_low = after(grad_hidden_low, down_scatter.total)
    down_half = down_scatter.first()
    grad_first = times_transposed(grad_hidden_low, wide_in) + grad_second
    grad_first = after(grad_first, *down_half)
    down_quarter = down_scatter.second()
    grad_residual, grad_gain_one, grad_shift_one = norm_one_pull(grad_first)
    grad_branch_one = grad_residual.astype(BF)
    grad_out = over_rows(mixed, grad_branch_one).astype(BF)
    grad_out_bias = jnp.sum(grad_branch_one.astype(F32), 0)
    late_sums = [
        grad_out_bias,
        grad_gain_one,
        grad_shift_one,
        grad_in_bias,
        grad_down_bias,
        grad_gain_two,
        grad_shift_two,
    ]
    late_block = pack_rows([v.reshape(devices, -1) for v in late_sums], share).astype(BF)
    in_scatter = Scatter(
        jnp.concatenate(
            [
                grad_in.reshape(devices, share, inner_width),
                grad_out.reshape(devices, share, width),
                late_block,
            ],
            2,
        ),
        me,
        devices,
        "split",
    )
    grad_mixed = times_transposed(grad_branch_one, wide_out).astype(BF)
    grad_mixed = after(grad_mixed, in_scatter.total, *down_quarter)
    in_half = in_scatter.first()
    down_part = down_scatter.along_z()
    grad_packed, column_sums = attention_backward(packed, mask, logsum, grad_mixed, length)
    grad_packed = after(grad_packed, down_part, *in_half)
    in_quarter = in_scatter.second()
    grad_qkv = over_rows(flat, grad_packed).astype(BF)
    column_sums = kind_major(column_sums.reshape(kept, 3 * width).sum(0))
    early_sums = [column_sums[:width], column_sums[2 * width :]]
    early_block = pack_rows([v.reshape(devices, -1) for v in early_sums], share).astype(BF)
    qkv_scatter = Scatter(
        jnp.concatenate([grad_qkv.reshape(devices, share, 3 * width), early_block], 2),
        me,
        devices,
        "split",
    )
    grad_inputs = (
        times_transposed(after(grad_packed, grad_qkv, *in_quarter), wide_qkv) + grad_residual
    ).astype(BF)
    grad_inputs = send_positions(
        grad_inputs.reshape(kept, members, local_len, width), members, devices
    )
    qkv_half = qkv_scatter.first()
    in_part = in_scatter.along_z()
    outputs = put_positions(outputs, seat, qkv_scatter.total)
    qkv_quarter = qkv_scatter.second()
    qkv_part = qkv_scatter.along_z()
    grad_inputs = put_positions(grad_inputs, seat, *qkv_half)
    early_out = unpack_rows(qkv_part[:, 3 * width :], [share, share])
    late_out = unpack_rows(
        in_part[:, inner_width + width :], [v.shape[0] for v in late_vectors]
    )
    return (
        outputs,
        grad_inputs,
        kind_major(qkv_part[:, : 3 * width]),
        early_out[0],
        early_out[1],
        in_part[:, inner_width : inner_width + width],
        late_out[0],
        late_out[1],
        late_out[2],
        in_part[:, :inner_width],
        late_out[3],
        down_part,
        late_out[4],
        late_out[5],
        late_out[6],
    )


def solution(mesh):
    placed = (
        P("dp", "seq", None),
        P("dp"),
        P(("dp", "seq"), None),
        P(("dp", "seq")),
        P(("dp", "seq")),
        P(("dp", "seq"), None),
        P(("dp", "seq")),
        P(("dp", "seq")),
        P(("dp", "seq")),
        P(("dp", "seq"), None),
        P(("dp", "seq")),
        P(("dp", "seq"), None),
        P(("dp", "seq")),
        P(("dp", "seq")),
        P(("dp", "seq")),
        P("dp", "seq", None),
    )
    return jax.shard_map(
        on_device,
        mesh=mesh,
        in_specs=placed,
        out_specs=(
            P("dp", "seq", None),
            P("dp", "seq", None),
            P(("dp", "seq"), None),
            P(("dp", "seq")),
            P(("dp", "seq")),
            P(("dp", "seq"), None),
            P(("dp", "seq")),
            P(("dp", "seq")),
            P(("dp", "seq")),
            P(("dp", "seq"), None),
            P(("dp", "seq")),
            P(("dp", "seq"), None),
            P(("dp", "seq")),
            P(("dp", "seq")),
            P(("dp", "seq")),
        ),
        check_vma=False,
    )
```

```python
import functools

import jax
import jax.numpy as jnp
from jax import lax
from jax.experimental import pallas as pl
from jax.experimental.pallas import tpu as pltpu
from jax.sharding import PartitionSpec as P

BF = jnp.bfloat16
F32 = jnp.float32
HD = 64
BOTH = ("dp", "seq")

def layer_norm(value, gain, shift):
    center = jnp.mean(value, -1, keepdims=True)
    centered = value - center
    spread = jnp.mean(centered * centered, -1, keepdims=True)
    return centered * lax.rsqrt(spread + 1e-12) * gain + shift


def over_rows(left, right):
    return lax.dot_general(
        left, right, (((0,), (0,)), ((), ())), preferred_element_type=jnp.float32
    )


def times_transposed(left, right):
    return lax.dot_general(
        left, right, (((1,), (1,)), ((), ())), preferred_element_type=jnp.float32
    )


def nt(a, b):
    return lax.dot_general(a, b, (((1,), (1,)), ((), ())), preferred_element_type=F32)


def tn(a, b):
    return lax.dot_general(a, b, (((0,), (0,)), ((), ())), preferred_element_type=F32)


def nn(a, b):
    return lax.dot_general(a, b, (((1,), (0,)), ((), ())), preferred_element_type=F32)


def masked_pair(q, k, bias, head, lane):
    mine = (lane >= head * HD) & (lane < (head + 1) * HD)
    spare = lane == (HD if head == 0 else 0)
    zero = jnp.zeros((), BF)
    qh = jnp.where(mine, q * BF(0.125), jnp.where(spare, jnp.ones((), BF), zero))
    kh = jnp.where(mine, k, jnp.where(spare, bias, zero))
    return qh, kh


def forward_kernel(packed_ref, mask_ref, mixed_ref, logsum_ref):
    count = packed_ref.shape[0]
    lane = lax.broadcasted_iota(jnp.int32, (count, 128), 1)
    q, k, v = (packed_ref[:, i * 128 : (i + 1) * 128] for i in range(3))
    bias = mask_ref[0]
    halves = []
    for h in range(2):
        qh, kh = masked_pair(q, k, bias, h, lane)
        scores = nt(kh, qh)
        top = jnp.max(scores, 0, keepdims=True)
        raised = jnp.exp(scores - top)
        total = jnp.sum(raised, 0, keepdims=True)
        mixed = tn(v[:, h * HD : (h + 1) * HD], raised.astype(BF))
        halves.append(mixed * (1.0 / total))
        logsum_ref[0, h : h + 1, :] = top + jnp.log(total)
    mixed_ref[...] = jnp.concatenate(halves, 0).T.astype(BF)


def backward_kernel(packed_ref, mask_ref, logsum_ref, grad_ref, out_ref, sums_ref):
    count = packed_ref.shape[0]
    lane = lax.broadcasted_iota(jnp.int32, (count, 128), 1)
    q, k, v = (packed_ref[:, i * 128 : (i + 1) * 128] for i in range(3))
    bias = mask_ref[0]
    grad = grad_ref[...]
    q_scaled, k_scaled = q * BF(0.125), k * BF(0.125)
    dq, dk, dv = [], [], []
    for h in range(2):
        qh, kh = masked_pair(q, k, bias, h, lane)
        mine = (lane >= h * HD) & (lane < (h + 1) * HD)
        vh = jnp.where(mine, v, jnp.zeros((), BF))
        probs = jnp.exp(nt(kh, qh) - logsum_ref[0, h : h + 1, :])
        grad_probs = nt(vh, grad)
        inner = jnp.sum(probs * grad_probs, 0, keepdims=True)
        grad_scores = (probs * (grad_probs - inner)).astype(BF)
        dv.append(nn(probs.astype(BF), grad))
        dk.append(nn(grad_scores, q_scaled))
        dq.append(tn(k_scaled[:, h * HD : (h + 1) * HD], grad_scores))
    low_half = lane < HD
    parts = (
        jnp.concatenate(dq, 0).T,
        jnp.where(low_half, dk[0], dk[1]),
        jnp.where(low_half, dv[0], dv[1]),
    )
    for i, part in enumerate(parts):
        rounded = part.astype(BF)
        out_ref[:, i * 128 : (i + 1) * 128] = rounded
        sums_ref[0, :, i * 128 : (i + 1) * 128] = jnp.sum(
            rounded.astype(F32), 0, keepdims=True
        )


def attention_specs(packed, length):
    rows, wide = packed.shape
    pairs, seqs = wide // 384, rows // length
    block = lambda size: pl.BlockSpec((length, size), lambda s, p: (s, p))
    mask = pl.BlockSpec((1, length, 128), lambda s, p: (s, 0, 0))
    row = lambda count, size: pl.BlockSpec((1, count, size), lambda s, p: (s * pairs + p, 0, 0))
    return rows, pairs, seqs, block, mask, row


def attention_forward(packed, mask, length):
    rows, pairs, seqs, block, mask_spec, row = attention_specs(packed, length)
    return pl.pallas_call(
        forward_kernel,
        grid=(seqs, pairs),
        in_specs=[block(384), mask_spec],
        out_specs=[block(128), row(2, length)],
        out_shape=[
            jax.ShapeDtypeStruct((rows, pairs * 128), BF),
            jax.ShapeDtypeStruct((seqs * pairs, 2, length), F32),
        ],
        compiler_params=pltpu.CompilerParams(vmem_limit_bytes=48 * 2**20),
        name="attention_forward",
        cost_estimate=pl.CostEstimate(
            flops=16 * rows * length * pairs * 128,
            bytes_accessed=rows * pairs * 1024,
            transcendentals=2 * rows * length * pairs,
        ),
    )(packed, mask)


def attention_backward(packed, mask, logsum, grad, length):
    rows, pairs, seqs, block, mask_spec, row = attention_specs(packed, length)
    return pl.pallas_call(
        backward_kernel,
        grid=(seqs, pairs),
        in_specs=[block(384), mask_spec, row(2, length), block(128)],
        out_specs=[block(384), row(1, 384)],
        out_shape=[
            jax.ShapeDtypeStruct((rows, pairs * 384), BF),
            jax.ShapeDtypeStruct((seqs * pairs, 1, 384), F32),
        ],
        compiler_params=pltpu.CompilerParams(vmem_limit_bytes=48 * 2**20),
        name="attention_backward",
        cost_estimate=pl.CostEstimate(
            flops=28 * rows * length * pairs * 128,
            bytes_accessed=rows * pairs * 1792,
            transcendentals=2 * rows * length * pairs,
        ),
    )(packed, mask, logsum, grad)


def pair_major(block):
    lead = block.shape[:-1]
    return block.reshape(lead + (3, -1, 128)).swapaxes(-3, -2).reshape(block.shape)


def kind_major(block):
    lead = block.shape[:-1]
    return block.reshape(lead + (-1, 3, 128)).swapaxes(-3, -2).reshape(block.shape)


def feed_forward_kernel(step, x_ref, w_ref, b_ref, active_ref, slope_ref):
    x = x_ref[...]
    for start in range(0, w_ref.shape[1], step):
        part = slice(start, start + step)
        hidden = nn(x, w_ref[:, part]) + b_ref[:, part]
        bell = jnp.exp(hidden * hidden * -0.5)
        share = 0.5 * (1.0 + lax.erf(hidden * 0.7071067811865476))
        active_ref[:, part] = (hidden * share).astype(BF)
        slope_ref[:, part] = (share + hidden * bell * 0.3989422804014327).astype(BF)


def feed_forward(x, weight, bias):
    rows, width = x.shape
    inner = weight.shape[1]
    block = 256
    out = jax.ShapeDtypeStruct((rows, inner), BF)
    return pl.pallas_call(
        functools.partial(feed_forward_kernel, 512),
        grid=(rows // block,),
        in_specs=[
            pl.BlockSpec((block, width), lambda i: (i, 0)),
            pl.BlockSpec((width, inner), lambda i: (0, 0)),
            pl.BlockSpec((1, inner), lambda i: (0, 0)),
        ],
        out_specs=[pl.BlockSpec((block, inner), lambda i: (i, 0))] * 2,
        out_shape=[out, out],
        compiler_params=pltpu.CompilerParams(vmem_limit_bytes=48 * 2**20),
        name="feed_forward",
        cost_estimate=pl.CostEstimate(
            flops=2 * rows * width * inner,
            bytes_accessed=4 * rows * inner + 2 * width * inner,
            transcendentals=2 * rows * inner,
        ),
    )(x, weight, bias)


def swap(block, distance, devices):
    return lax.ppermute(block, BOTH, [(i, i ^ distance) for i in range(devices)])


def after(value, *done):
    return lax.optimization_barrier((value,) + done)[0]


def place_kernel(ids, counts, spans, me_ref, *refs):
    pieces, rest = refs[: len(counts)], refs[len(counts) :]
    outs, sems = rest[: len(spans)], rest[len(spans)]
    me = me_ref[0]
    copies = []
    at = 0
    for piece, count in zip(pieces, counts):
        for j in range(count):
            spot = me ^ ids[at]
            for out, (start, size) in zip(outs, spans):
                source = piece.at[j] if len(spans) == 1 else piece.at[j, :, pl.ds(start, size)]
                copy = pltpu.make_async_copy(source, out.at[spot], sems.at[len(copies)])
                copy.start()
                copies.append(copy)
            at += 1
    for copy in copies:
        copy.wait()


def place(pieces, ids, me, spans=None):
    counts = [p.shape[0] for p in pieces]
    total = sum(counts)
    tail = pieces[0].shape[1:]
    spans = spans or [(0, tail[-1])]
    any_space = pl.BlockSpec(memory_space=pl.ANY)
    moved = 2 * sum(p.size * p.dtype.itemsize for p in pieces)
    return pl.pallas_call(
        functools.partial(place_kernel, ids, counts, spans),
        in_specs=[pl.BlockSpec(memory_space=pltpu.SMEM)] + [any_space] * len(pieces),
        out_specs=[pl.BlockSpec(memory_space=pltpu.VMEM)] * len(spans),
        out_shape=[
            jax.ShapeDtypeStruct((total,) + tail[:-1] + (size,), pieces[0].dtype)
            for _, size in spans
        ],
        scratch_shapes=[pltpu.SemaphoreType.DMA((total * len(spans),))],
        compiler_params=pltpu.CompilerParams(vmem_limit_bytes=32 * 2**20),
        cost_estimate=pl.CostEstimate(flops=0, bytes_accessed=moved, transcendentals=0),
        name="place_blocks",
    )(me.reshape(1), *pieces)


def pack_rows(vectors, share):
    lead = vectors[0].shape[:-1]
    columns = []
    for at in range(0, len(vectors), share):
        rows = []
        for v in vectors[at : at + share]:
            rows.append(jnp.pad(v, [(0, 0)] * len(lead) + [(0, 128 - v.shape[-1])]))
        block = jnp.stack(rows, -2)
        columns.append(
            jnp.pad(block, [(0, 0)] * len(lead) + [(0, share - len(rows)), (0, 0)])
        )
    return columns[0] if len(columns) == 1 else jnp.concatenate(columns, -1)


def unpack_rows(block, sizes):
    share = block.shape[-2]
    out = []
    for i, size in enumerate(sizes):
        start = i // share * 128
        out.append(block[..., i % share, start : start + size])
    return out


def fence(holders, *values):
    arrays = [a for h in holders for a in h.arrays()]
    kept = lax.optimization_barrier(tuple(arrays) + values)
    at = 0
    for h in holders:
        count = len(h.arrays())
        h.put(list(kept[at : at + count]))
        at += count
    return kept[at:]


class Gather:
    def __init__(self, block, me, devices, plan):
        self.me, self.devices, self.plan = me, devices, plan
        self.held, self.ids = [block[None]], [[0]]

    def arrays(self):
        return self.held

    def put(self, arrays):
        self.held = arrays

    def swapped(self, block, distance):
        return swap(block, distance, self.devices)

    def along_z(self):
        own, own_ids = self.held[0], self.ids[0]
        distance = 32
        while distance < self.devices:
            own = jnp.concatenate([own, self.swapped(own, distance)])
            own_ids = own_ids + [i ^ distance for i in own_ids]
            distance *= 2
        self.held = [own] + [self.swapped(own, 8 * k) for k in (1, 2, 3)]
        self.ids = [[i ^ (8 * k) for i in own_ids] for k in range(4)]

    def grow(self, order):
        held, ids = [], []
        for block, block_ids, distance in zip(self.held, self.ids, order):
            held += [block, self.swapped(block, distance)]
            ids += [block_ids, [i ^ distance for i in block_ids]]
        self.held, self.ids = held, ids

    def join(self, pairs):
        self.held = [jnp.concatenate([self.held[i] for i in p]) for p in pairs]
        self.ids = [[i for j in p for i in self.ids[j]] for p in pairs]

    def first(self):
        if self.plan == "split":
            self.join([(0, 1), (2, 3)])
            self.grow((4, 2))
        else:
            self.join([(0, 1, 2, 3)])
            self.grow((4,) if self.plan == "xy" else (2,))

    def second(self):
        if self.plan == "split":
            self.join([(0, 1), (2, 3)])
            self.grow((2, 4))
        else:
            self.join([(0, 1)])
            self.grow((2,) if self.plan == "xy" else (4,))

    def core(self):
        self.grow((1,) * len(self.held))

    def finish(self, spans=None):
        return place(self.held, [i for ids in self.ids for i in ids], self.me, spans)


def pick(block, axis, index):
    return lax.dynamic_index_in_dim(block, index, axis, keepdims=False)


def fold(block, axis, me, distance, devices):
    digit = (me // distance) % 2
    got = swap(pick(block, axis, 1 - digit), distance, devices)
    return (pick(block, axis, digit).astype(F32) + got.astype(F32)).astype(BF)


def core_sum(total, me, devices):
    tail = total.shape[1:]
    distance = devices // 2
    while distance >= 32:
        total = fold(total.reshape((2, distance) + tail), 0, me, distance, devices)
        distance //= 2
    return fold(total.reshape((16, 2) + tail), 1, me, 1, devices)


class Scatter:
    def __init__(self, total, me, devices, plan):
        self.me, self.devices, self.plan = me, devices, plan
        self.tail = total.shape[1:]
        self.held = [total]

    def arrays(self):
        return self.held

    def put(self, arrays):
        self.held = arrays

    def fold(self, block, axis, distance):
        return fold(block, axis, self.me, distance, self.devices)

    def first(self):
        total = self.held[0].reshape((4, 2, 2) + self.tail)
        if self.plan == "split":
            z = (self.me // 8) % 4
            halves = total.reshape((2, 2, 2, 2) + self.tail)
            self.held = [
                self.fold(pick(halves, 0, z // 2), 1, 4),
                self.fold(pick(halves, 0, 1 - z // 2), 2, 2),
            ]
        elif self.plan == "xy":
            self.held = [self.fold(total, 1, 4)]
        else:
            self.held = [self.fold(total, 2, 2)]

    def second(self):
        z = (self.me // 8) % 4
        if self.plan == "split":
            near = self.fold(self.held[0], 1, 2)
            away = self.fold(self.held[1], 1, 4)
            odd = z % 2
            self.held = [
                pick(near, 0, odd),
                pick(near, 0, 1 - odd),
                pick(away, 0, odd),
                pick(away, 0, 1 - odd),
            ]
        else:
            total = self.fold(self.held[0], 1, 2 if self.plan == "xy" else 4)
            self.held = [pick(total, 0, z ^ k) for k in range(4)]

    def along_z(self):
        total = self.held[0].astype(F32)
        for k in (1, 2, 3):
            total = total + swap(self.held[k], 8 * k, self.devices).astype(F32)
        self.held = [total]


class ToSequences:
    def __init__(self, block, seat, members, devices):
        groups, count, width = block.shape
        parts = block.reshape(members, groups // members, count, width)
        self.devices = devices
        self.held = [pick(parts, 0, seat ^ k) for k in range(members)]

    def arrays(self):
        return self.held

    def put(self, arrays):
        self.held = arrays

    def send(self, k):
        self.held[k] = swap(self.held[k], k, self.devices)

    def finish(self):
        return jnp.stack(self.held, 1).reshape(-1, self.held[0].shape[-1])


class ToPositions:
    def __init__(self, block, members, devices):
        self.devices = devices
        self.held = [block[:, k][None] for k in range(members)]

    def arrays(self):
        return self.held

    def put(self, arrays):
        self.held = arrays

    def send(self, k):
        self.held[k] = swap(self.held[k], k, self.devices)

    def finish(self, seat):
        (placed,) = place(self.held, list(range(len(self.held))), seat)
        return placed.reshape((-1,) + placed.shape[2:])


def on_device(
    inputs,
    lengths,
    query_key_value_weight,
    query_bias,
    value_bias,
    output_weight,
    output_bias,
    norm1_gain,
    norm1_shift,
    in_weight,
    in_bias,
    down_weight,
    down_bias,
    norm2_gain,
    norm2_shift,
    cotangent,
):
    groups, local_len, width = inputs.shape
    rows = groups * local_len
    members = lax.axis_size("seq")
    devices = lax.axis_size("dp") * members
    kept = groups // members
    length = local_len * members
    seat = lax.axis_index("seq")
    me = lax.axis_index("dp") * members + seat
    share = query_key_value_weight.shape[0]
    inner_width = in_weight.shape[1]
    early = pack_rows([query_bias, value_bias], share)
    qkv_gather = Gather(
        jnp.concatenate([pair_major(query_key_value_weight), early], 1), me, devices, "split"
    )
    late_vectors = [
        output_bias,
        norm1_gain,
        norm1_shift,
        in_bias,
        down_bias,
        norm2_gain,
        norm2_shift,
    ]
    late = pack_rows(late_vectors, share)
    in_gather = Gather(
        jnp.concatenate([in_weight, output_weight, late], 1), me, devices, "split"
    )
    down_gather = Gather(down_weight, me, devices, "yx")
    near, far = range(1, (members + 1) // 2), range((members + 1) // 2, members)
    flat = ToSequences(inputs, seat, members, devices)
    for k in near:
        flat.send(k)
    for k in far[:1]:
        flat.send(k)
    qkv_gather.along_z()
    fence([qkv_gather])
    qkv_gather.first()
    fence([qkv_gather, flat])
    for k in far[1:]:
        flat.send(k)
    qkv_gather.second()
    in_gather.put([after(a, qkv_gather.held[0]) for a in in_gather.arrays()])
    in_gather.along_z()
    fence([qkv_gather])
    qkv_gather.core()
    fence([qkv_gather, in_gather, flat])
    in_gather.first()
    flat = flat.finish()
    wide_qkv, early = qkv_gather.finish([(0, 3 * width), (3 * width, early.shape[1])])
    (wide_qkv, early, flat) = fence([in_gather], wide_qkv, early, flat)
    in_gather.second()
    down_gather.put([after(a, wide_qkv) for a in down_gather.arrays()])
    down_gather.along_z()
    wide_qkv = wide_qkv.reshape(width, 3 * width)
    full_query_bias, full_value_bias = [
        v.reshape(-1).astype(F32) for v in unpack_rows(early, [share, share])
    ]
    bias_vector = jnp.concatenate([full_query_bias, jnp.zeros((width,), F32), full_value_bias])
    packed = jnp.dot(flat, wide_qkv, preferred_element_type=F32) + pair_major(bias_vector)
    packed = packed.astype(BF)
    mine = lax.dynamic_slice(lengths, (seat * kept,), (kept,))
    slots = jnp.arange(length, dtype=jnp.int32)
    positions = ((slots // local_len) ^ seat) * local_len + slots % local_len
    mask = jnp.where(positions[None, :] < mine[:, None], 0.0, -1e30).astype(BF)
    mask = jnp.broadcast_to(mask[:, :, None], (kept, length, 128))
    mixed, logsum = attention_forward(packed, mask, length)
    (mixed, logsum, packed) = fence([in_gather, down_gather], mixed, logsum, packed)
    in_gather.core()
    down_gather.first()
    fence([in_gather])
    wide_in, wide_out, late = in_gather.finish(
        [(0, inner_width), (inner_width, width), (inner_width + width, late.shape[1])]
    )
    (wide_in, wide_out, late) = fence([down_gather], wide_in, wide_out, late)
    down_gather.second()
    wide_in = wide_in.reshape(width, inner_width)
    wide_out = wide_out.reshape(width, width)
    (
        full_out_bias,
        gain_one,
        shift_one,
        full_in_bias,
        full_down_bias,
        gain_two,
        shift_two,
    ) = [
        v.reshape(-1).astype(F32)
        for v in unpack_rows(late, [v.shape[0] for v in late_vectors])
    ]
    attention_branch = jnp.dot(mixed, wide_out, preferred_element_type=F32) + full_out_bias
    first, norm_one_pull = jax.vjp(
        layer_norm, flat.astype(F32) + attention_branch, gain_one, shift_one
    )
    first_low = first.astype(BF)
    (first_low,) = fence([down_gather], first_low)
    down_gather.core()
    cot = ToSequences(after(cotangent, first_low), seat, members, devices)
    for k in range(1, members):
        cot.send(k)
    active_low, slope = feed_forward(first_low, wide_in, full_in_bias[None])
    (active_low, slope) = fence([down_gather, cot], active_low, slope)
    (wide_down,) = down_gather.finish()
    wide_down = wide_down.reshape(inner_width, width)
    branch_two = jnp.dot(active_low, wide_down, preferred_element_type=F32) + full_down_bias
    result, norm_two_pull = jax.vjp(
        layer_norm, first_low.astype(F32) + branch_two, gain_two, shift_two
    )
    outputs = result.astype(BF).reshape(kept, members, local_len, width)
    grad_second, grad_gain_two, grad_shift_two = norm_two_pull(cot.finish().astype(F32))
    grad_branch_two = grad_second.astype(BF)
    grad_down_bias = jnp.sum(grad_branch_two.astype(F32), 0)
    (outputs, grad_second, grad_branch_two, grad_gain_two, grad_shift_two, grad_down_bias) = fence(
        [],
        outputs,
        grad_second,
        grad_branch_two,
        grad_gain_two,
        grad_shift_two,
        grad_down_bias,
    )
    outputs = ToPositions(outputs, members, devices)
    for k in near:
        outputs.send(k)
    for k in far[:1]:
        outputs.send(k)
    grad_down = over_rows(active_low, grad_branch_two).astype(BF)
    (grad_down, grad_branch_two) = fence([outputs], grad_down, grad_branch_two)
    for k in far[1:]:
        outputs.send(k)
    down_scatter = Scatter(
        core_sum(grad_down.reshape(devices, -1, width), me, devices), me, devices, "split"
    )
    grad_hidden_low = (
        times_transposed(grad_branch_two, wide_down) * slope.astype(F32)
    ).astype(BF)
    grad_in_bias = jnp.sum(grad_hidden_low.astype(F32), 0)
    (grad_hidden_low, grad_in_bias) = fence([outputs, down_scatter], grad_hidden_low, grad_in_bias)
    down_scatter.first()
    grad_in = over_rows(first_low, grad_hidden_low).astype(BF)
    (grad_in, grad_hidden_low) = fence([down_scatter], grad_in, grad_hidden_low)
    down_scatter.second()
    in_core = core_sum(grad_in.reshape(devices, share, inner_width), me, devices)
    grad_first = times_transposed(grad_hidden_low, wide_in) + grad_second
    grad_residual, grad_gain_one, grad_shift_one = norm_one_pull(grad_first)
    grad_branch_one = grad_residual.astype(BF)
    grad_out_bias = jnp.sum(grad_branch_one.astype(F32), 0)
    grad_out = over_rows(mixed, grad_branch_one).astype(BF)
    late_sums = [
        grad_out_bias,
        grad_gain_one,
        grad_shift_one,
        grad_in_bias,
        grad_down_bias,
        grad_gain_two,
        grad_shift_two,
    ]
    late_block = pack_rows([v.reshape(devices, -1) for v in late_sums], share).astype(BF)
    out_core = core_sum(
        jnp.concatenate([grad_out.reshape(devices, share, width), late_block], 2), me, devices
    )
    grad_mixed = times_transposed(grad_branch_one, wide_out).astype(BF)
    in_scatter = Scatter(jnp.concatenate([in_core, out_core], 2), me, devices, "split")
    (grad_mixed, grad_residual) = fence([down_scatter, in_scatter], grad_mixed, grad_residual)
    in_scatter.first()
    down_scatter.along_z()
    grad_packed, column_sums = attention_backward(packed, mask, logsum, grad_mixed, length)
    (grad_packed, column_sums) = fence([in_scatter, down_scatter], grad_packed, column_sums)
    in_scatter.second()
    grad_qkv = over_rows(flat, grad_packed).astype(BF)
    column_sums = kind_major(column_sums.reshape(kept, 3 * width).sum(0))
    early_sums = [column_sums[:width], column_sums[2 * width :]]
    early_block = pack_rows([v.reshape(devices, -1) for v in early_sums], share).astype(BF)
    grad_qkv = jnp.concatenate([grad_qkv.reshape(devices, share, 3 * width), early_block], 2)
    (grad_qkv, grad_packed) = fence([], grad_qkv, grad_packed)
    qkv_scatter = Scatter(core_sum(grad_qkv, me, devices), me, devices, "split")
    grad_inputs = (times_transposed(grad_packed, wide_qkv) + grad_residual).astype(BF)
    (grad_inputs,) = fence([in_scatter, qkv_scatter], grad_inputs)
    qkv_scatter.first()
    in_scatter.along_z()
    grad_inputs = ToPositions(
        grad_inputs.reshape(kept, members, local_len, width), members, devices
    )
    for k in near:
        grad_inputs.send(k)
    for k in far[:1]:
        grad_inputs.send(k)
    fence([qkv_scatter])
    qkv_scatter.second()
    for k in far[1:]:
        grad_inputs.send(k)
    outputs.put([after(a, qkv_scatter.held[0]) for a in outputs.arrays()])
    outputs = outputs.finish(seat)
    (outputs,) = fence([qkv_scatter, grad_inputs], outputs)
    qkv_scatter.along_z()
    grad_inputs = grad_inputs.finish(seat)
    (qkv_part,), (in_part,), (down_part,) = (
        s.held for s in (qkv_scatter, in_scatter, down_scatter)
    )
    early_out = unpack_rows(qkv_part[:, 3 * width :], [share, share])
    late_out = unpack_rows(
        in_part[:, inner_width + width :], [v.shape[0] for v in late_vectors]
    )
    return (
        outputs,
        grad_inputs,
        kind_major(qkv_part[:, : 3 * width]),
        early_out[0],
        early_out[1],
        in_part[:, inner_width : inner_width + width],
        late_out[0],
        late_out[1],
        late_out[2],
        in_part[:, :inner_width],
        late_out[3],
        down_part,
        late_out[4],
        late_out[5],
        late_out[6],
    )


def solution(mesh):
    placed = (
        P("dp", "seq", None),
        P("dp"),
        P(("dp", "seq"), None),
        P(("dp", "seq")),
        P(("dp", "seq")),
        P(("dp", "seq"), None),
        P(("dp", "seq")),
        P(("dp", "seq")),
        P(("dp", "seq")),
        P(("dp", "seq"), None),
        P(("dp", "seq")),
        P(("dp", "seq"), None),
        P(("dp", "seq")),
        P(("dp", "seq")),
        P(("dp", "seq")),
        P("dp", "seq", None),
    )
    return jax.shard_map(
        on_device,
        mesh=mesh,
        in_specs=placed,
        out_specs=(
            P("dp", "seq", None),
            P("dp", "seq", None),
            P(("dp", "seq"), None),
            P(("dp", "seq")),
            P(("dp", "seq")),
            P(("dp", "seq"), None),
            P(("dp", "seq")),
            P(("dp", "seq")),
            P(("dp", "seq")),
            P(("dp", "seq"), None),
            P(("dp", "seq")),
            P(("dp", "seq"), None),
            P(("dp", "seq")),
            P(("dp", "seq")),
            P(("dp", "seq")),
        ),
        check_vma=False,
    )
```

```python
import functools

import jax
import jax.numpy as jnp
from jax import lax
from jax.experimental import pallas as pl
from jax.experimental.pallas import tpu as pltpu
from jax.sharding import PartitionSpec as P

BF = jnp.bfloat16
F32 = jnp.float32
HD = 64
BOTH = ("dp", "seq")

def layer_norm(value, gain, shift):
    center = jnp.mean(value, -1, keepdims=True)
    centered = value - center
    spread = jnp.mean(centered * centered, -1, keepdims=True)
    return centered * lax.rsqrt(spread + 1e-12) * gain + shift


def over_rows(left, right):
    return lax.dot_general(
        left, right, (((0,), (0,)), ((), ())), preferred_element_type=jnp.float32
    )


def times_transposed(left, right):
    return lax.dot_general(
        left, right, (((1,), (1,)), ((), ())), preferred_element_type=jnp.float32
    )


def nt(a, b):
    return lax.dot_general(a, b, (((1,), (1,)), ((), ())), preferred_element_type=F32)


def tn(a, b):
    return lax.dot_general(a, b, (((0,), (0,)), ((), ())), preferred_element_type=F32)


def nn(a, b):
    return lax.dot_general(a, b, (((1,), (0,)), ((), ())), preferred_element_type=F32)


def masked_pair(q, k, bias, head, lane):
    mine = (lane >= head * HD) & (lane < (head + 1) * HD)
    spare = lane == (HD if head == 0 else 0)
    zero = jnp.zeros((), BF)
    qh = jnp.where(mine, q * BF(0.125), jnp.where(spare, jnp.ones((), BF), zero))
    kh = jnp.where(mine, k, jnp.where(spare, bias, zero))
    return qh, kh


def forward_kernel(packed_ref, mask_ref, mixed_ref, logsum_ref):
    count = packed_ref.shape[0]
    lane = lax.broadcasted_iota(jnp.int32, (count, 128), 1)
    q, k, v = (packed_ref[:, i * 128 : (i + 1) * 128] for i in range(3))
    bias = mask_ref[0]
    halves = []
    for h in range(2):
        qh, kh = masked_pair(q, k, bias, h, lane)
        scores = nt(kh, qh)
        top = jnp.max(scores, 0, keepdims=True)
        raised = jnp.exp(scores - top)
        total = jnp.sum(raised, 0, keepdims=True)
        mixed = tn(v[:, h * HD : (h + 1) * HD], raised.astype(BF))
        halves.append(mixed * (1.0 / total))
        logsum_ref[0, h : h + 1, :] = top + jnp.log(total)
    mixed_ref[...] = jnp.concatenate(halves, 0).T.astype(BF)


def backward_kernel(packed_ref, mask_ref, logsum_ref, grad_ref, out_ref, sums_ref):
    count = packed_ref.shape[0]
    lane = lax.broadcasted_iota(jnp.int32, (count, 128), 1)
    q, k, v = (packed_ref[:, i * 128 : (i + 1) * 128] for i in range(3))
    bias = mask_ref[0]
    grad = grad_ref[...]
    q_scaled, k_scaled = q * BF(0.125), k * BF(0.125)
    dq, dk, dv = [], [], []
    for h in range(2):
        qh, kh = masked_pair(q, k, bias, h, lane)
        mine = (lane >= h * HD) & (lane < (h + 1) * HD)
        vh = jnp.where(mine, v, jnp.zeros((), BF))
        probs = jnp.exp(nt(kh, qh) - logsum_ref[0, h : h + 1, :])
        grad_probs = nt(vh, grad)
        inner = jnp.sum(probs * grad_probs, 0, keepdims=True)
        grad_scores = (probs * (grad_probs - inner)).astype(BF)
        dv.append(nn(probs.astype(BF), grad))
        dk.append(nn(grad_scores, q_scaled))
        dq.append(tn(k_scaled[:, h * HD : (h + 1) * HD], grad_scores))
    low_half = lane < HD
    parts = (
        jnp.concatenate(dq, 0).T,
        jnp.where(low_half, dk[0], dk[1]),
        jnp.where(low_half, dv[0], dv[1]),
    )
    for i, part in enumerate(parts):
        rounded = part.astype(BF)
        out_ref[:, i * 128 : (i + 1) * 128] = rounded
        sums_ref[0, :, i * 128 : (i + 1) * 128] = jnp.sum(
            rounded.astype(F32), 0, keepdims=True
        )


def attention_specs(packed, length):
    rows, wide = packed.shape
    pairs, seqs = wide // 384, rows // length
    block = lambda size: pl.BlockSpec((length, size), lambda s, p: (s, p))
    mask = pl.BlockSpec((1, length, 128), lambda s, p: (s, 0, 0))
    row = lambda count, size: pl.BlockSpec((1, count, size), lambda s, p: (s * pairs + p, 0, 0))
    return rows, pairs, seqs, block, mask, row


def attention_forward(packed, mask, length):
    rows, pairs, seqs, block, mask_spec, row = attention_specs(packed, length)
    return pl.pallas_call(
        forward_kernel,
        grid=(seqs, pairs),
        in_specs=[block(384), mask_spec],
        out_specs=[block(128), row(2, length)],
        out_shape=[
            jax.ShapeDtypeStruct((rows, pairs * 128), BF),
            jax.ShapeDtypeStruct((seqs * pairs, 2, length), F32),
        ],
        compiler_params=pltpu.CompilerParams(vmem_limit_bytes=48 * 2**20),
        name="attention_forward",
        cost_estimate=pl.CostEstimate(
            flops=16 * rows * length * pairs * 128,
            bytes_accessed=rows * pairs * 1024,
            transcendentals=2 * rows * length * pairs,
        ),
    )(packed, mask)


def attention_backward(packed, mask, logsum, grad, length):
    rows, pairs, seqs, block, mask_spec, row = attention_specs(packed, length)
    return pl.pallas_call(
        backward_kernel,
        grid=(seqs, pairs),
        in_specs=[block(384), mask_spec, row(2, length), block(128)],
        out_specs=[block(384), row(1, 384)],
        out_shape=[
            jax.ShapeDtypeStruct((rows, pairs * 384), BF),
            jax.ShapeDtypeStruct((seqs * pairs, 1, 384), F32),
        ],
        compiler_params=pltpu.CompilerParams(vmem_limit_bytes=48 * 2**20),
        name="attention_backward",
        cost_estimate=pl.CostEstimate(
            flops=28 * rows * length * pairs * 128,
            bytes_accessed=rows * pairs * 1792,
            transcendentals=2 * rows * length * pairs,
        ),
    )(packed, mask, logsum, grad)


def pair_major(block):
    lead = block.shape[:-1]
    return block.reshape(lead + (3, -1, 128)).swapaxes(-3, -2).reshape(block.shape)


def kind_major(block):
    lead = block.shape[:-1]
    return block.reshape(lead + (-1, 3, 128)).swapaxes(-3, -2).reshape(block.shape)


def feed_forward_kernel(step, x_ref, w_ref, b_ref, active_ref, slope_ref):
    x = x_ref[...]
    for start in range(0, w_ref.shape[1], step):
        part = slice(start, start + step)
        hidden = nn(x, w_ref[:, part]) + b_ref[:, part]
        bell = jnp.exp(hidden * hidden * -0.5)
        share = 0.5 * (1.0 + lax.erf(hidden * 0.7071067811865476))
        active_ref[:, part] = (hidden * share).astype(BF)
        slope_ref[:, part] = (share + hidden * bell * 0.3989422804014327).astype(BF)


def feed_forward(x, weight, bias):
    rows, width = x.shape
    inner = weight.shape[1]
    block = 256
    out = jax.ShapeDtypeStruct((rows, inner), BF)
    return pl.pallas_call(
        functools.partial(feed_forward_kernel, 512),
        grid=(rows // block,),
        in_specs=[
            pl.BlockSpec((block, width), lambda i: (i, 0)),
            pl.BlockSpec((width, inner), lambda i: (0, 0)),
            pl.BlockSpec((1, inner), lambda i: (0, 0)),
        ],
        out_specs=[pl.BlockSpec((block, inner), lambda i: (i, 0))] * 2,
        out_shape=[out, out],
        compiler_params=pltpu.CompilerParams(vmem_limit_bytes=48 * 2**20),
        name="feed_forward",
        cost_estimate=pl.CostEstimate(
            flops=2 * rows * width * inner,
            bytes_accessed=4 * rows * inner + 2 * width * inner,
            transcendentals=2 * rows * inner,
        ),
    )(x, weight, bias)


def swap(block, distance, devices):
    return lax.ppermute(block, BOTH, [(i, i ^ distance) for i in range(devices)])


def after(value, *done):
    return lax.optimization_barrier((value,) + done)[0]


def place_kernel(ids, counts, spans, me_ref, *refs):
    pieces, rest = refs[: len(counts)], refs[len(counts) :]
    outs, sems = rest[: len(spans)], rest[len(spans)]
    me = me_ref[0]
    copies = []
    at = 0
    for piece, count in zip(pieces, counts):
        for j in range(count):
            spot = me ^ ids[at]
            for out, (start, size) in zip(outs, spans):
                source = piece.at[j] if len(spans) == 1 else piece.at[j, :, pl.ds(start, size)]
                copy = pltpu.make_async_copy(source, out.at[spot], sems.at[len(copies)])
                copy.start()
                copies.append(copy)
            at += 1
    for copy in copies:
        copy.wait()


def place(pieces, ids, me, spans=None):
    counts = [p.shape[0] for p in pieces]
    total = sum(counts)
    tail = pieces[0].shape[1:]
    spans = spans or [(0, tail[-1])]
    any_space = pl.BlockSpec(memory_space=pl.ANY)
    moved = 2 * sum(p.size * p.dtype.itemsize for p in pieces)
    return pl.pallas_call(
        functools.partial(place_kernel, ids, counts, spans),
        in_specs=[pl.BlockSpec(memory_space=pltpu.SMEM)] + [any_space] * len(pieces),
        out_specs=[pl.BlockSpec(memory_space=pltpu.VMEM)] * len(spans),
        out_shape=[
            jax.ShapeDtypeStruct((total,) + tail[:-1] + (size,), pieces[0].dtype)
            for _, size in spans
        ],
        scratch_shapes=[pltpu.SemaphoreType.DMA((total * len(spans),))],
        compiler_params=pltpu.CompilerParams(vmem_limit_bytes=32 * 2**20),
        cost_estimate=pl.CostEstimate(flops=0, bytes_accessed=moved, transcendentals=0),
        name="place_blocks",
    )(me.reshape(1), *pieces)


def pack_rows(vectors, share):
    lead = vectors[0].shape[:-1]
    columns = []
    for at in range(0, len(vectors), share):
        rows = []
        for v in vectors[at : at + share]:
            rows.append(jnp.pad(v, [(0, 0)] * len(lead) + [(0, 128 - v.shape[-1])]))
        block = jnp.stack(rows, -2)
        columns.append(
            jnp.pad(block, [(0, 0)] * len(lead) + [(0, share - len(rows)), (0, 0)])
        )
    return columns[0] if len(columns) == 1 else jnp.concatenate(columns, -1)


def unpack_rows(block, sizes):
    share = block.shape[-2]
    out = []
    for i, size in enumerate(sizes):
        start = i // share * 128
        out.append(block[..., i % share, start : start + size])
    return out


def fence(holders, *values):
    arrays = [a for h in holders for a in h.arrays()]
    kept = lax.optimization_barrier(tuple(arrays) + values)
    at = 0
    for h in holders:
        count = len(h.arrays())
        h.put(list(kept[at : at + count]))
        at += count
    return kept[at:]


class Gather:
    def __init__(self, block, me, devices, plan):
        self.me, self.devices, self.plan = me, devices, plan
        self.held, self.ids = [block[None]], [[0]]

    def arrays(self):
        return self.held

    def put(self, arrays):
        self.held = arrays

    def swapped(self, block, distance):
        return swap(block, distance, self.devices)

    def along_z(self):
        own, own_ids = self.held[0], self.ids[0]
        distance = 32
        while distance < self.devices:
            own = jnp.concatenate([own, self.swapped(own, distance)])
            own_ids = own_ids + [i ^ distance for i in own_ids]
            distance *= 2
        self.held = [own] + [self.swapped(own, 8 * k) for k in (1, 2, 3)]
        self.ids = [[i ^ (8 * k) for i in own_ids] for k in range(4)]

    def grow(self, order):
        held, ids = [], []
        for block, block_ids, distance in zip(self.held, self.ids, order):
            held += [block, self.swapped(block, distance)]
            ids += [block_ids, [i ^ distance for i in block_ids]]
        self.held, self.ids = held, ids

    def join(self, pairs):
        self.held = [jnp.concatenate([self.held[i] for i in p]) for p in pairs]
        self.ids = [[i for j in p for i in self.ids[j]] for p in pairs]

    def first(self):
        if self.plan == "split":
            self.join([(0, 1), (2, 3)])
            self.grow((4, 2))
        else:
            self.join([(0, 1, 2, 3)])
            self.grow((4,) if self.plan == "xy" else (2,))

    def second(self):
        if self.plan == "split":
            self.join([(0, 1), (2, 3)])
            self.grow((2, 4))
        else:
            self.join([(0, 1)])
            self.grow((2,) if self.plan == "xy" else (4,))

    def core(self):
        self.grow((1,) * len(self.held))

    def finish(self, spans=None):
        return place(self.held, [i for ids in self.ids for i in ids], self.me, spans)


def pick(block, axis, index):
    return lax.dynamic_index_in_dim(block, index, axis, keepdims=False)


def fold(block, axis, me, distance, devices):
    digit = (me // distance) % 2
    got = swap(pick(block, axis, 1 - digit), distance, devices)
    return (pick(block, axis, digit).astype(F32) + got.astype(F32)).astype(BF)


def core_sum(total, me, devices):
    tail = total.shape[1:]
    distance = devices // 2
    while distance >= 32:
        total = fold(total.reshape((2, distance) + tail), 0, me, distance, devices)
        distance //= 2
    return fold(total.reshape((16, 2) + tail), 1, me, 1, devices)


class Scatter:
    def __init__(self, total, me, devices, plan):
        self.me, self.devices, self.plan = me, devices, plan
        self.tail = total.shape[1:]
        self.held = [total]

    def arrays(self):
        return self.held

    def put(self, arrays):
        self.held = arrays

    def fold(self, block, axis, distance):
        return fold(block, axis, self.me, distance, self.devices)

    def first(self):
        total = self.held[0].reshape((4, 2, 2) + self.tail)
        if self.plan == "split":
            z = (self.me // 8) % 4
            halves = total.reshape((2, 2, 2, 2) + self.tail)
            self.held = [
                self.fold(pick(halves, 0, z // 2), 1, 4),
                self.fold(pick(halves, 0, 1 - z // 2), 2, 2),
            ]
        elif self.plan == "xy":
            self.held = [self.fold(total, 1, 4)]
        else:
            self.held = [self.fold(total, 2, 2)]

    def second(self):
        z = (self.me // 8) % 4
        if self.plan == "split":
            near = self.fold(self.held[0], 1, 2)
            away = self.fold(self.held[1], 1, 4)
            odd = z % 2
            self.held = [
                pick(near, 0, odd),
                pick(near, 0, 1 - odd),
                pick(away, 0, odd),
                pick(away, 0, 1 - odd),
            ]
        else:
            total = self.fold(self.held[0], 1, 2 if self.plan == "xy" else 4)
            self.held = [pick(total, 0, z ^ k) for k in range(4)]

    def along_z(self):
        sent = [swap(self.held[k], 8 * k, self.devices) for k in (1, 2, 3)]
        self.held = [self.held[0]] + sent

    def result(self):
        return sum(block.astype(F32) for block in self.held)


class ToSequences:
    def __init__(self, block, seat, members, devices):
        groups, count, width = block.shape
        parts = block.reshape(members, groups // members, count, width)
        self.devices = devices
        self.held = [pick(parts, 0, seat ^ k) for k in range(members)]

    def arrays(self):
        return self.held

    def put(self, arrays):
        self.held = arrays

    def send(self, k):
        self.held[k] = swap(self.held[k], k, self.devices)

    def finish(self):
        return jnp.stack(self.held, 1).reshape(-1, self.held[0].shape[-1])


class ToPositions:
    def __init__(self, block, members, devices):
        self.devices = devices
        self.held = [block[:, k][None] for k in range(members)]

    def arrays(self):
        return self.held

    def put(self, arrays):
        self.held = arrays

    def send(self, k):
        self.held[k] = swap(self.held[k], k, self.devices)

    def finish(self, seat):
        (placed,) = place(self.held, list(range(len(self.held))), seat)
        return placed.reshape((-1,) + placed.shape[2:])


def on_device(
    inputs,
    lengths,
    query_key_value_weight,
    query_bias,
    value_bias,
    output_weight,
    output_bias,
    norm1_gain,
    norm1_shift,
    in_weight,
    in_bias,
    down_weight,
    down_bias,
    norm2_gain,
    norm2_shift,
    cotangent,
):
    groups, local_len, width = inputs.shape
    rows = groups * local_len
    members = lax.axis_size("seq")
    devices = lax.axis_size("dp") * members
    kept = groups // members
    length = local_len * members
    seat = lax.axis_index("seq")
    me = lax.axis_index("dp") * members + seat
    share = query_key_value_weight.shape[0]
    inner_width = in_weight.shape[1]
    early = pack_rows([query_bias, value_bias], share)
    qkv_gather = Gather(
        jnp.concatenate([pair_major(query_key_value_weight), early], 1), me, devices, "split"
    )
    late_vectors = [
        output_bias,
        norm1_gain,
        norm1_shift,
        in_bias,
        down_bias,
        norm2_gain,
        norm2_shift,
    ]
    late = pack_rows(late_vectors, share)
    in_gather = Gather(
        jnp.concatenate([in_weight, output_weight, late], 1), me, devices, "split"
    )
    down_gather = Gather(down_weight, me, devices, "split")
    near, far = range(1, (members + 1) // 2), range((members + 1) // 2, members)
    flat = ToSequences(inputs, seat, members, devices)
    for k in range(1, members):
        flat.send(k)
    qkv_gather.along_z()
    fence([qkv_gather])
    qkv_gather.first()
    fence([qkv_gather, flat])
    qkv_gather.second()
    in_gather.put([after(a, qkv_gather.held[0]) for a in in_gather.arrays()])
    in_gather.along_z()
    fence([qkv_gather])
    qkv_gather.core()
    fence([qkv_gather])
    flat = flat.finish()
    wide_qkv, early = qkv_gather.finish([(0, 3 * width), (3 * width, early.shape[1])])
    (wide_qkv, early, flat) = fence([in_gather], wide_qkv, early, flat)
    in_gather.first()
    wide_qkv = wide_qkv.reshape(width, 3 * width)
    full_query_bias, full_value_bias = [
        v.reshape(-1).astype(F32) for v in unpack_rows(early, [share, share])
    ]
    bias_vector = jnp.concatenate([full_query_bias, jnp.zeros((width,), F32), full_value_bias])
    packed = jnp.dot(flat, wide_qkv, preferred_element_type=F32) + pair_major(bias_vector)
    packed = packed.astype(BF)
    (packed,) = fence([in_gather], packed)
    in_gather.second()
    down_gather.put([after(a, packed) for a in down_gather.arrays()])
    down_gather.along_z()
    mine = lax.dynamic_slice(lengths, (seat * kept,), (kept,))
    slots = jnp.arange(length, dtype=jnp.int32)
    positions = ((slots // local_len) ^ seat) * local_len + slots % local_len
    mask = jnp.where(positions[None, :] < mine[:, None], 0.0, -1e30).astype(BF)
    mask = jnp.broadcast_to(mask[:, :, None], (kept, length, 128))
    mixed, logsum = attention_forward(packed, mask, length)
    (mixed, logsum, packed) = fence([in_gather, down_gather], mixed, logsum, packed)
    in_gather.core()
    down_gather.first()
    fence([in_gather])
    wide_in, wide_out, late = in_gather.finish(
        [(0, inner_width), (inner_width, width), (inner_width + width, late.shape[1])]
    )
    (wide_in, wide_out, late) = fence([down_gather], wide_in, wide_out, late)
    down_gather.second()
    wide_in = wide_in.reshape(width, inner_width)
    wide_out = wide_out.reshape(width, width)
    (
        full_out_bias,
        gain_one,
        shift_one,
        full_in_bias,
        full_down_bias,
        gain_two,
        shift_two,
    ) = [
        v.reshape(-1).astype(F32)
        for v in unpack_rows(late, [v.shape[0] for v in late_vectors])
    ]
    attention_branch = jnp.dot(mixed, wide_out, preferred_element_type=F32) + full_out_bias
    first, norm_one_pull = jax.vjp(
        layer_norm, flat.astype(F32) + attention_branch, gain_one, shift_one
    )
    first_low = first.astype(BF)
    (first_low,) = fence([down_gather], first_low)
    down_gather.core()
    cot = ToSequences(after(cotangent, first_low), seat, members, devices)
    for k in range(1, members):
        cot.send(k)
    active_low, slope = feed_forward(first_low, wide_in, full_in_bias[None])
    (active_low, slope) = fence([down_gather, cot], active_low, slope)
    (wide_down,) = down_gather.finish()
    wide_down = wide_down.reshape(inner_width, width)
    branch_two = jnp.dot(active_low, wide_down, preferred_element_type=F32) + full_down_bias
    result, norm_two_pull = jax.vjp(
        layer_norm, first_low.astype(F32) + branch_two, gain_two, shift_two
    )
    outputs = result.astype(BF).reshape(kept, members, local_len, width)
    grad_second, grad_gain_two, grad_shift_two = norm_two_pull(cot.finish().astype(F32))
    grad_branch_two = grad_second.astype(BF)
    grad_down_bias = jnp.sum(grad_branch_two.astype(F32), 0)
    (outputs, grad_second, grad_branch_two, grad_gain_two, grad_shift_two, grad_down_bias) = fence(
        [],
        outputs,
        grad_second,
        grad_branch_two,
        grad_gain_two,
        grad_shift_two,
        grad_down_bias,
    )
    outputs = ToPositions(outputs, members, devices)
    for k in near:
        outputs.send(k)
    for k in far[:1]:
        outputs.send(k)
    grad_down = over_rows(active_low, grad_branch_two).astype(BF)
    (grad_down, grad_branch_two) = fence([outputs], grad_down, grad_branch_two)
    for k in far[1:]:
        outputs.send(k)
    down_scatter = Scatter(
        core_sum(grad_down.reshape(devices, -1, width), me, devices), me, devices, "split"
    )
    grad_hidden_low = (
        times_transposed(grad_branch_two, wide_down) * slope.astype(F32)
    ).astype(BF)
    grad_in_bias = jnp.sum(grad_hidden_low.astype(F32), 0)
    (grad_hidden_low, grad_in_bias) = fence([outputs, down_scatter], grad_hidden_low, grad_in_bias)
    down_scatter.first()
    grad_in = over_rows(first_low, grad_hidden_low).astype(BF)
    (grad_in, grad_hidden_low) = fence([down_scatter], grad_in, grad_hidden_low)
    down_scatter.second()
    in_core = core_sum(grad_in.reshape(devices, share, inner_width), me, devices)
    grad_first = times_transposed(grad_hidden_low, wide_in) + grad_second
    grad_residual, grad_gain_one, grad_shift_one = norm_one_pull(grad_first)
    grad_branch_one = grad_residual.astype(BF)
    grad_out_bias = jnp.sum(grad_branch_one.astype(F32), 0)
    grad_out = over_rows(mixed, grad_branch_one).astype(BF)
    late_sums = [
        grad_out_bias,
        grad_gain_one,
        grad_shift_one,
        grad_in_bias,
        grad_down_bias,
        grad_gain_two,
        grad_shift_two,
    ]
    late_block = pack_rows([v.reshape(devices, -1) for v in late_sums], share).astype(BF)
    out_core = core_sum(
        jnp.concatenate([grad_out.reshape(devices, share, width), late_block], 2), me, devices
    )
    grad_mixed = times_transposed(grad_branch_one, wide_out).astype(BF)
    in_scatter = Scatter(jnp.concatenate([in_core, out_core], 2), me, devices, "split")
    (grad_mixed, grad_residual) = fence([down_scatter, in_scatter], grad_mixed, grad_residual)
    in_scatter.first()
    down_scatter.along_z()
    grad_packed, column_sums = attention_backward(packed, mask, logsum, grad_mixed, length)
    (grad_packed, column_sums) = fence([in_scatter, down_scatter], grad_packed, column_sums)
    in_scatter.second()
    grad_qkv = over_rows(flat, grad_packed).astype(BF)
    column_sums = kind_major(column_sums.reshape(kept, 3 * width).sum(0))
    early_sums = [column_sums[:width], column_sums[2 * width :]]
    early_block = pack_rows([v.reshape(devices, -1) for v in early_sums], share).astype(BF)
    grad_qkv = jnp.concatenate([grad_qkv.reshape(devices, share, 3 * width), early_block], 2)
    (grad_qkv, grad_packed) = fence([], grad_qkv, grad_packed)
    qkv_scatter = Scatter(core_sum(grad_qkv, me, devices), me, devices, "split")
    grad_inputs = (times_transposed(grad_packed, wide_qkv) + grad_residual).astype(BF)
    (grad_inputs,) = fence([in_scatter, qkv_scatter], grad_inputs)
    grad_inputs = ToPositions(
        grad_inputs.reshape(kept, members, local_len, width), members, devices
    )
    qkv_scatter.first()
    in_scatter.along_z()
    fence([qkv_scatter, grad_inputs])
    qkv_scatter.second()
    fence([qkv_scatter, grad_inputs, in_scatter])
    for k in range(1, members):
        grad_inputs.send(k)
    qkv_scatter.along_z()
    outputs.put([after(a, *qkv_scatter.held[:1]) for a in outputs.arrays()])
    outputs = outputs.finish(seat)
    in_part = in_scatter.result()
    down_part = down_scatter.result()
    (in_part, outputs) = fence([qkv_scatter, grad_inputs], in_part, outputs)
    qkv_part = qkv_scatter.result()
    grad_inputs = grad_inputs.finish(seat)
    early_out = unpack_rows(qkv_part[:, 3 * width :], [share, share])
    late_out = unpack_rows(
        in_part[:, inner_width + width :], [v.shape[0] for v in late_vectors]
    )
    return (
        outputs,
        grad_inputs,
        kind_major(qkv_part[:, : 3 * width]),
        early_out[0],
        early_out[1],
        in_part[:, inner_width : inner_width + width],
        late_out[0],
        late_out[1],
        late_out[2],
        in_part[:, :inner_width],
        late_out[3],
        down_part,
        late_out[4],
        late_out[5],
        late_out[6],
    )


def solution(mesh):
    placed = (
        P("dp", "seq", None),
        P("dp"),
        P(("dp", "seq"), None),
        P(("dp", "seq")),
        P(("dp", "seq")),
        P(("dp", "seq"), None),
        P(("dp", "seq")),
        P(("dp", "seq")),
        P(("dp", "seq")),
        P(("dp", "seq"), None),
        P(("dp", "seq")),
        P(("dp", "seq"), None),
        P(("dp", "seq")),
        P(("dp", "seq")),
        P(("dp", "seq")),
        P("dp", "seq", None),
    )
    return jax.shard_map(
        on_device,
        mesh=mesh,
        in_specs=placed,
        out_specs=(
            P("dp", "seq", None),
            P("dp", "seq", None),
            P(("dp", "seq"), None),
            P(("dp", "seq")),
            P(("dp", "seq")),
            P(("dp", "seq"), None),
            P(("dp", "seq")),
            P(("dp", "seq")),
            P(("dp", "seq")),
            P(("dp", "seq"), None),
            P(("dp", "seq")),
            P(("dp", "seq"), None),
            P(("dp", "seq")),
            P(("dp", "seq")),
            P(("dp", "seq")),
        ),
        check_vma=False,
    )
```

```python
import functools

import jax
import jax.numpy as jnp
from jax import lax
from jax.experimental import pallas as pl
from jax.experimental.pallas import tpu as pltpu
from jax.sharding import PartitionSpec as P

BF = jnp.bfloat16
F32 = jnp.float32
HD = 64
BOTH = ("dp", "seq")

def layer_norm(value, gain, shift):
    center = jnp.mean(value, -1, keepdims=True)
    centered = value - center
    spread = jnp.mean(centered * centered, -1, keepdims=True)
    return centered * lax.rsqrt(spread + 1e-12) * gain + shift


def over_rows(left, right):
    return lax.dot_general(
        left, right, (((0,), (0,)), ((), ())), preferred_element_type=jnp.float32
    )


def times_transposed(left, right):
    return lax.dot_general(
        left, right, (((1,), (1,)), ((), ())), preferred_element_type=jnp.float32
    )


def nt(a, b):
    return lax.dot_general(a, b, (((1,), (1,)), ((), ())), preferred_element_type=F32)


def tn(a, b):
    return lax.dot_general(a, b, (((0,), (0,)), ((), ())), preferred_element_type=F32)


def nn(a, b):
    return lax.dot_general(a, b, (((1,), (0,)), ((), ())), preferred_element_type=F32)


def masked_pair(q, k, bias, head, lane):
    mine = (lane >= head * HD) & (lane < (head + 1) * HD)
    spare = lane == (HD if head == 0 else 0)
    zero = jnp.zeros((), BF)
    qh = jnp.where(mine, q * BF(0.125), jnp.where(spare, jnp.ones((), BF), zero))
    kh = jnp.where(mine, k, jnp.where(spare, bias, zero))
    return qh, kh


def forward_kernel(packed_ref, mask_ref, mixed_ref, logsum_ref):
    count = packed_ref.shape[0]
    lane = lax.broadcasted_iota(jnp.int32, (count, 128), 1)
    q, k, v = (packed_ref[:, i * 128 : (i + 1) * 128] for i in range(3))
    bias = mask_ref[0]
    halves = []
    for h in range(2):
        qh, kh = masked_pair(q, k, bias, h, lane)
        scores = nt(kh, qh)
        top = jnp.max(scores, 0, keepdims=True)
        raised = jnp.exp(scores - top)
        total = jnp.sum(raised, 0, keepdims=True)
        mixed = tn(v[:, h * HD : (h + 1) * HD], raised.astype(BF))
        halves.append(mixed * (1.0 / total))
        logsum_ref[0, h : h + 1, :] = top + jnp.log(total)
    mixed_ref[...] = jnp.concatenate(halves, 0).T.astype(BF)


def backward_kernel(packed_ref, mask_ref, logsum_ref, grad_ref, out_ref, sums_ref):
    count = packed_ref.shape[0]
    lane = lax.broadcasted_iota(jnp.int32, (count, 128), 1)
    q, k, v = (packed_ref[:, i * 128 : (i + 1) * 128] for i in range(3))
    bias = mask_ref[0]
    grad = grad_ref[...]
    q_scaled, k_scaled = q * BF(0.125), k * BF(0.125)
    dq, dk, dv = [], [], []
    for h in range(2):
        qh, kh = masked_pair(q, k, bias, h, lane)
        mine = (lane >= h * HD) & (lane < (h + 1) * HD)
        vh = jnp.where(mine, v, jnp.zeros((), BF))
        probs = jnp.exp(nt(kh, qh) - logsum_ref[0, h : h + 1, :])
        grad_probs = nt(vh, grad)
        inner = jnp.sum(probs * grad_probs, 0, keepdims=True)
        grad_scores = (probs * (grad_probs - inner)).astype(BF)
        dv.append(nn(probs.astype(BF), grad))
        dk.append(nn(grad_scores, q_scaled))
        dq.append(tn(k_scaled[:, h * HD : (h + 1) * HD], grad_scores))
    low_half = lane < HD
    parts = (
        jnp.concatenate(dq, 0).T,
        jnp.where(low_half, dk[0], dk[1]),
        jnp.where(low_half, dv[0], dv[1]),
    )
    for i, part in enumerate(parts):
        rounded = part.astype(BF)
        out_ref[:, i * 128 : (i + 1) * 128] = rounded
        sums_ref[0, :, i * 128 : (i + 1) * 128] = jnp.sum(
            rounded.astype(F32), 0, keepdims=True
        )


def attention_specs(packed, length):
    rows, wide = packed.shape
    pairs, seqs = wide // 384, rows // length
    block = lambda size: pl.BlockSpec((length, size), lambda s, p: (s, p))
    mask = pl.BlockSpec((1, length, 128), lambda s, p: (s, 0, 0))
    row = lambda count, size: pl.BlockSpec((1, count, size), lambda s, p: (s * pairs + p, 0, 0))
    return rows, pairs, seqs, block, mask, row


def attention_forward(packed, mask, length):
    rows, pairs, seqs, block, mask_spec, row = attention_specs(packed, length)
    return pl.pallas_call(
        forward_kernel,
        grid=(seqs, pairs),
        in_specs=[block(384), mask_spec],
        out_specs=[block(128), row(2, length)],
        out_shape=[
            jax.ShapeDtypeStruct((rows, pairs * 128), BF),
            jax.ShapeDtypeStruct((seqs * pairs, 2, length), F32),
        ],
        compiler_params=pltpu.CompilerParams(vmem_limit_bytes=48 * 2**20),
        name="attention_forward",
        cost_estimate=pl.CostEstimate(
            flops=16 * rows * length * pairs * 128,
            bytes_accessed=rows * pairs * 1024,
            transcendentals=2 * rows * length * pairs,
        ),
    )(packed, mask)


def attention_backward(packed, mask, logsum, grad, length):
    rows, pairs, seqs, block, mask_spec, row = attention_specs(packed, length)
    return pl.pallas_call(
        backward_kernel,
        grid=(seqs, pairs),
        in_specs=[block(384), mask_spec, row(2, length), block(128)],
        out_specs=[block(384), row(1, 384)],
        out_shape=[
            jax.ShapeDtypeStruct((rows, pairs * 384), BF),
            jax.ShapeDtypeStruct((seqs * pairs, 1, 384), F32),
        ],
        compiler_params=pltpu.CompilerParams(vmem_limit_bytes=48 * 2**20),
        name="attention_backward",
        cost_estimate=pl.CostEstimate(
            flops=28 * rows * length * pairs * 128,
            bytes_accessed=rows * pairs * 1792,
            transcendentals=2 * rows * length * pairs,
        ),
    )(packed, mask, logsum, grad)


def pair_major(block):
    lead = block.shape[:-1]
    return block.reshape(lead + (3, -1, 128)).swapaxes(-3, -2).reshape(block.shape)


def kind_major(block):
    lead = block.shape[:-1]
    return block.reshape(lead + (-1, 3, 128)).swapaxes(-3, -2).reshape(block.shape)


def feed_forward_kernel(step, x_ref, w_ref, b_ref, active_ref, slope_ref):
    x = x_ref[...]
    for start in range(0, w_ref.shape[1], step):
        part = slice(start, start + step)
        hidden = nn(x, w_ref[:, part]) + b_ref[:, part]
        bell = jnp.exp(hidden * hidden * -0.5)
        share = 0.5 * (1.0 + lax.erf(hidden * 0.7071067811865476))
        active_ref[:, part] = (hidden * share).astype(BF)
        slope_ref[:, part] = (share + hidden * bell * 0.3989422804014327).astype(BF)


def feed_forward(x, weight, bias):
    rows, width = x.shape
    inner = weight.shape[1]
    block = 256
    out = jax.ShapeDtypeStruct((rows, inner), BF)
    return pl.pallas_call(
        functools.partial(feed_forward_kernel, 512),
        grid=(rows // block,),
        in_specs=[
            pl.BlockSpec((block, width), lambda i: (i, 0)),
            pl.BlockSpec((width, inner), lambda i: (0, 0)),
            pl.BlockSpec((1, inner), lambda i: (0, 0)),
        ],
        out_specs=[pl.BlockSpec((block, inner), lambda i: (i, 0))] * 2,
        out_shape=[out, out],
        compiler_params=pltpu.CompilerParams(vmem_limit_bytes=48 * 2**20),
        name="feed_forward",
        cost_estimate=pl.CostEstimate(
            flops=2 * rows * width * inner,
            bytes_accessed=4 * rows * inner + 2 * width * inner,
            transcendentals=2 * rows * inner,
        ),
    )(x, weight, bias)


def swap(block, distance, devices):
    return lax.ppermute(block, BOTH, [(i, i ^ distance) for i in range(devices)])


def after(value, *done):
    return lax.optimization_barrier((value,) + done)[0]


def place_kernel(ids, counts, spans, me_ref, *refs):
    pieces, rest = refs[: len(counts)], refs[len(counts) :]
    outs, sems = rest[: len(spans)], rest[len(spans)]
    me = me_ref[0]
    copies = []
    at = 0
    for piece, count in zip(pieces, counts):
        for j in range(count):
            spot = me ^ ids[at]
            for out, (start, size) in zip(outs, spans):
                source = piece.at[j] if len(spans) == 1 else piece.at[j, :, pl.ds(start, size)]
                copy = pltpu.make_async_copy(source, out.at[spot], sems.at[len(copies)])
                copy.start()
                copies.append(copy)
            at += 1
    for copy in copies:
        copy.wait()


def place(pieces, ids, me, spans=None):
    counts = [p.shape[0] for p in pieces]
    total = sum(counts)
    tail = pieces[0].shape[1:]
    spans = spans or [(0, tail[-1])]
    any_space = pl.BlockSpec(memory_space=pl.ANY)
    moved = 2 * sum(p.size * p.dtype.itemsize for p in pieces)
    return pl.pallas_call(
        functools.partial(place_kernel, ids, counts, spans),
        in_specs=[pl.BlockSpec(memory_space=pltpu.SMEM)] + [any_space] * len(pieces),
        out_specs=[pl.BlockSpec(memory_space=pltpu.VMEM)] * len(spans),
        out_shape=[
            jax.ShapeDtypeStruct((total,) + tail[:-1] + (size,), pieces[0].dtype)
            for _, size in spans
        ],
        scratch_shapes=[pltpu.SemaphoreType.DMA((total * len(spans),))],
        compiler_params=pltpu.CompilerParams(vmem_limit_bytes=32 * 2**20),
        cost_estimate=pl.CostEstimate(flops=0, bytes_accessed=moved, transcendentals=0),
        name="place_blocks",
    )(me.reshape(1), *pieces)


def pack_rows(vectors, share):
    lead = vectors[0].shape[:-1]
    columns = []
    for at in range(0, len(vectors), share):
        rows = []
        for v in vectors[at : at + share]:
            rows.append(jnp.pad(v, [(0, 0)] * len(lead) + [(0, 128 - v.shape[-1])]))
        block = jnp.stack(rows, -2)
        columns.append(
            jnp.pad(block, [(0, 0)] * len(lead) + [(0, share - len(rows)), (0, 0)])
        )
    return columns[0] if len(columns) == 1 else jnp.concatenate(columns, -1)


def unpack_rows(block, sizes):
    share = block.shape[-2]
    out = []
    for i, size in enumerate(sizes):
        start = i // share * 128
        out.append(block[..., i % share, start : start + size])
    return out


def fence(holders, *values):
    arrays = [a for h in holders for a in h.arrays()]
    kept = lax.optimization_barrier(tuple(arrays) + values)
    at = 0
    for h in holders:
        count = len(h.arrays())
        h.put(list(kept[at : at + count]))
        at += count
    return kept[at:]


class Gather:
    def __init__(self, block, me, devices, plan):
        self.me, self.devices, self.plan = me, devices, plan
        self.held, self.ids = [block[None]], [[0]]

    def arrays(self):
        return self.held

    def put(self, arrays):
        self.held = arrays

    def swapped(self, block, distance):
        return swap(block, distance, self.devices)

    def along_z(self):
        own, own_ids = self.held[0], self.ids[0]
        distance = 32
        while distance < self.devices:
            own = jnp.concatenate([own, self.swapped(own, distance)])
            own_ids = own_ids + [i ^ distance for i in own_ids]
            distance *= 2
        self.held = [own] + [self.swapped(own, 8 * k) for k in (1, 2, 3)]
        self.ids = [[i ^ (8 * k) for i in own_ids] for k in range(4)]

    def grow(self, order):
        held, ids = [], []
        for block, block_ids, distance in zip(self.held, self.ids, order):
            held += [block, self.swapped(block, distance)]
            ids += [block_ids, [i ^ distance for i in block_ids]]
        self.held, self.ids = held, ids

    def join(self, pairs):
        self.held = [jnp.concatenate([self.held[i] for i in p]) for p in pairs]
        self.ids = [[i for j in p for i in self.ids[j]] for p in pairs]

    def first(self):
        if self.plan == "split":
            self.join([(0, 1), (2, 3)])
            self.grow((4, 2))
        else:
            self.join([(0, 1, 2, 3)])
            self.grow((4,) if self.plan == "xy" else (2,))

    def second(self):
        if self.plan == "split":
            self.join([(0, 1), (2, 3)])
            self.grow((2, 4))
        else:
            self.join([(0, 1)])
            self.grow((2,) if self.plan == "xy" else (4,))

    def core(self):
        self.grow((1,) * len(self.held))

    def finish(self, spans=None):
        return place(self.held, [i for ids in self.ids for i in ids], self.me, spans)


def pick(block, axis, index):
    return lax.dynamic_index_in_dim(block, index, axis, keepdims=False)


def fold(block, axis, me, distance, devices):
    digit = (me // distance) % 2
    got = swap(pick(block, axis, 1 - digit), distance, devices)
    return (pick(block, axis, digit).astype(F32) + got.astype(F32)).astype(BF)


def core_sum(total, me, devices):
    tail = total.shape[1:]
    distance = devices // 2
    while distance >= 32:
        total = fold(total.reshape((2, distance) + tail), 0, me, distance, devices)
        distance //= 2
    return fold(total.reshape((16, 2) + tail), 1, me, 1, devices)


class Scatter:
    def __init__(self, total, me, devices, plan):
        self.me, self.devices, self.plan = me, devices, plan
        self.tail = total.shape[1:]
        self.held = [total]

    def arrays(self):
        return self.held

    def put(self, arrays):
        self.held = arrays

    def fold(self, block, axis, distance):
        return fold(block, axis, self.me, distance, self.devices)

    def first(self):
        total = self.held[0].reshape((4, 2, 2) + self.tail)
        if self.plan == "split":
            z = (self.me // 8) % 4
            halves = total.reshape((2, 2, 2, 2) + self.tail)
            self.held = [
                self.fold(pick(halves, 0, z // 2), 1, 4),
                self.fold(pick(halves, 0, 1 - z // 2), 2, 2),
            ]
        elif self.plan == "xy":
            self.held = [self.fold(total, 1, 4)]
        else:
            self.held = [self.fold(total, 2, 2)]

    def second(self):
        z = (self.me // 8) % 4
        if self.plan == "split":
            near = self.fold(self.held[0], 1, 2)
            away = self.fold(self.held[1], 1, 4)
            odd = z % 2
            self.held = [
                pick(near, 0, odd),
                pick(near, 0, 1 - odd),
                pick(away, 0, odd),
                pick(away, 0, 1 - odd),
            ]
        else:
            total = self.fold(self.held[0], 1, 2 if self.plan == "xy" else 4)
            self.held = [pick(total, 0, z ^ k) for k in range(4)]

    def along_z(self):
        sent = [swap(self.held[k], 8 * k, self.devices) for k in (1, 2, 3)]
        self.held = [self.held[0]] + sent

    def result(self):
        return sum(block.astype(F32) for block in self.held)


class ToSequences:
    def __init__(self, block, seat, members, devices):
        groups, count, width = block.shape
        parts = block.reshape(members, groups // members, count, width)
        self.devices = devices
        self.held = [pick(parts, 0, seat ^ k) for k in range(members)]

    def arrays(self):
        return self.held

    def put(self, arrays):
        self.held = arrays

    def send(self, k):
        self.held[k] = swap(self.held[k], k, self.devices)

    def finish(self):
        return jnp.stack(self.held, 1).reshape(-1, self.held[0].shape[-1])


class ToPositions:
    def __init__(self, block, members, devices):
        self.devices = devices
        self.held = [block[:, k][None] for k in range(members)]

    def arrays(self):
        return self.held

    def put(self, arrays):
        self.held = arrays

    def send(self, k):
        self.held[k] = swap(self.held[k], k, self.devices)

    def finish(self, seat):
        (placed,) = place(self.held, list(range(len(self.held))), seat)
        return placed.reshape((-1,) + placed.shape[2:])


def on_device(
    inputs,
    lengths,
    query_key_value_weight,
    query_bias,
    value_bias,
    output_weight,
    output_bias,
    norm1_gain,
    norm1_shift,
    in_weight,
    in_bias,
    down_weight,
    down_bias,
    norm2_gain,
    norm2_shift,
    cotangent,
):
    groups, local_len, width = inputs.shape
    rows = groups * local_len
    members = lax.axis_size("seq")
    devices = lax.axis_size("dp") * members
    kept = groups // members
    length = local_len * members
    seat = lax.axis_index("seq")
    me = lax.axis_index("dp") * members + seat
    share = query_key_value_weight.shape[0]
    inner_width = in_weight.shape[1]
    early = pack_rows([query_bias, value_bias], share)
    qkv_gather = Gather(
        jnp.concatenate([pair_major(query_key_value_weight), early], 1), me, devices, "split"
    )
    late_vectors = [
        output_bias,
        norm1_gain,
        norm1_shift,
        in_bias,
        down_bias,
        norm2_gain,
        norm2_shift,
    ]
    late = pack_rows(late_vectors, share)
    in_gather = Gather(
        jnp.concatenate([in_weight, output_weight, late], 1), me, devices, "split"
    )
    down_gather = Gather(down_weight, me, devices, "split")
    near, far = range(1, (members + 1) // 2), range((members + 1) // 2, members)
    flat = ToSequences(inputs, seat, members, devices)
    for k in range(1, members):
        flat.send(k)
    qkv_gather.along_z()
    (in_block,) = fence([qkv_gather], in_gather.held[0])
    in_gather.put([in_block])
    qkv_gather.first()
    in_gather.along_z()
    fence([qkv_gather, in_gather, flat])
    qkv_gather.second()
    fence([qkv_gather])
    qkv_gather.core()
    fence([qkv_gather, in_gather])
    in_gather.first()
    flat = flat.finish()
    wide_qkv, early = qkv_gather.finish([(0, 3 * width), (3 * width, early.shape[1])])
    (wide_qkv, early, flat) = fence([in_gather], wide_qkv, early, flat)
    in_gather.second()
    wide_qkv = wide_qkv.reshape(width, 3 * width)
    full_query_bias, full_value_bias = [
        v.reshape(-1).astype(F32) for v in unpack_rows(early, [share, share])
    ]
    bias_vector = jnp.concatenate([full_query_bias, jnp.zeros((width,), F32), full_value_bias])
    packed = jnp.dot(flat, wide_qkv, preferred_element_type=F32) + pair_major(bias_vector)
    packed = packed.astype(BF)
    (packed,) = fence([], packed)
    down_gather.put([after(a, packed) for a in down_gather.arrays()])
    down_gather.along_z()
    mine = lax.dynamic_slice(lengths, (seat * kept,), (kept,))
    slots = jnp.arange(length, dtype=jnp.int32)
    positions = ((slots // local_len) ^ seat) * local_len + slots % local_len
    mask = jnp.where(positions[None, :] < mine[:, None], 0.0, -1e30).astype(BF)
    mask = jnp.broadcast_to(mask[:, :, None], (kept, length, 128))
    mixed, logsum = attention_forward(packed, mask, length)
    (mixed, logsum, packed) = fence([in_gather, down_gather], mixed, logsum, packed)
    in_gather.core()
    down_gather.first()
    fence([in_gather])
    wide_in, wide_out, late = in_gather.finish(
        [(0, inner_width), (inner_width, width), (inner_width + width, late.shape[1])]
    )
    (wide_in, wide_out, late) = fence([down_gather], wide_in, wide_out, late)
    down_gather.second()
    wide_in = wide_in.reshape(width, inner_width)
    wide_out = wide_out.reshape(width, width)
    (
        full_out_bias,
        gain_one,
        shift_one,
        full_in_bias,
        full_down_bias,
        gain_two,
        shift_two,
    ) = [
        v.reshape(-1).astype(F32)
        for v in unpack_rows(late, [v.shape[0] for v in late_vectors])
    ]
    attention_branch = jnp.dot(mixed, wide_out, preferred_element_type=F32) + full_out_bias
    first, norm_one_pull = jax.vjp(
        layer_norm, flat.astype(F32) + attention_branch, gain_one, shift_one
    )
    first_low = first.astype(BF)
    (first_low,) = fence([down_gather], first_low)
    down_gather.core()
    cot = ToSequences(after(cotangent, first_low), seat, members, devices)
    for k in range(1, members):
        cot.send(k)
    active_low, slope = feed_forward(first_low, wide_in, full_in_bias[None])
    (active_low, slope) = fence([down_gather, cot], active_low, slope)
    (wide_down,) = down_gather.finish()
    wide_down = wide_down.reshape(inner_width, width)
    branch_two = jnp.dot(active_low, wide_down, preferred_element_type=F32) + full_down_bias
    result, norm_two_pull = jax.vjp(
        layer_norm, first_low.astype(F32) + branch_two, gain_two, shift_two
    )
    outputs = result.astype(BF).reshape(kept, members, local_len, width)
    grad_second, grad_gain_two, grad_shift_two = norm_two_pull(cot.finish().astype(F32))
    grad_branch_two = grad_second.astype(BF)
    grad_down_bias = jnp.sum(grad_branch_two.astype(F32), 0)
    (outputs, grad_second, grad_branch_two, grad_gain_two, grad_shift_two, grad_down_bias) = fence(
        [],
        outputs,
        grad_second,
        grad_branch_two,
        grad_gain_two,
        grad_shift_two,
        grad_down_bias,
    )
    outputs = ToPositions(outputs, members, devices)
    for k in near:
        outputs.send(k)
    for k in far[:1]:
        outputs.send(k)
    grad_down = over_rows(active_low, grad_branch_two).astype(BF)
    (grad_down, grad_branch_two) = fence([outputs], grad_down, grad_branch_two)
    for k in far[1:]:
        outputs.send(k)
    down_scatter = Scatter(
        core_sum(grad_down.reshape(devices, -1, width), me, devices), me, devices, "split"
    )
    grad_hidden_low = (
        times_transposed(grad_branch_two, wide_down) * slope.astype(F32)
    ).astype(BF)
    grad_in_bias = jnp.sum(grad_hidden_low.astype(F32), 0)
    (grad_hidden_low, grad_in_bias) = fence([outputs, down_scatter], grad_hidden_low, grad_in_bias)
    down_scatter.first()
    grad_in = over_rows(first_low, grad_hidden_low).astype(BF)
    (grad_in, grad_hidden_low) = fence([down_scatter], grad_in, grad_hidden_low)
    down_scatter.second()
    in_core = core_sum(grad_in.reshape(devices, share, inner_width), me, devices)
    grad_first = times_transposed(grad_hidden_low, wide_in) + grad_second
    grad_residual, grad_gain_one, grad_shift_one = norm_one_pull(grad_first)
    grad_branch_one = grad_residual.astype(BF)
    grad_out_bias = jnp.sum(grad_branch_one.astype(F32), 0)
    grad_out = over_rows(mixed, grad_branch_one).astype(BF)
    late_sums = [
        grad_out_bias,
        grad_gain_one,
        grad_shift_one,
        grad_in_bias,
        grad_down_bias,
        grad_gain_two,
        grad_shift_two,
    ]
    late_block = pack_rows([v.reshape(devices, -1) for v in late_sums], share).astype(BF)
    out_core = core_sum(
        jnp.concatenate([grad_out.reshape(devices, share, width), late_block], 2), me, devices
    )
    grad_mixed = times_transposed(grad_branch_one, wide_out).astype(BF)
    in_scatter = Scatter(jnp.concatenate([in_core, out_core], 2), me, devices, "split")
    (grad_mixed, grad_residual) = fence([down_scatter, in_scatter], grad_mixed, grad_residual)
    in_scatter.first()
    down_scatter.along_z()
    grad_packed, column_sums = attention_backward(packed, mask, logsum, grad_mixed, length)
    (grad_packed, column_sums) = fence([in_scatter, down_scatter], grad_packed, column_sums)
    in_scatter.second()
    grad_inputs = (times_transposed(grad_packed, wide_qkv) + grad_residual).astype(BF)
    (grad_inputs, grad_packed) = fence([in_scatter], grad_inputs, grad_packed)
    grad_inputs = ToPositions(
        grad_inputs.reshape(kept, members, local_len, width), members, devices
    )
    for k in near:
        grad_inputs.send(k)
    for k in far[:1]:
        grad_inputs.send(k)
    in_scatter.along_z()
    grad_qkv = over_rows(flat, grad_packed).astype(BF)
    column_sums = kind_major(column_sums.reshape(kept, 3 * width).sum(0))
    early_sums = [column_sums[:width], column_sums[2 * width :]]
    early_block = pack_rows([v.reshape(devices, -1) for v in early_sums], share).astype(BF)
    grad_qkv = jnp.concatenate([grad_qkv.reshape(devices, share, 3 * width), early_block], 2)
    (grad_qkv,) = fence([grad_inputs], grad_qkv)
    qkv_scatter = Scatter(core_sum(grad_qkv, me, devices), me, devices, "split")
    for k in far[1:]:
        grad_inputs.send(k)
    fence([qkv_scatter])
    qkv_scatter.first()
    fence([qkv_scatter, grad_inputs, in_scatter])
    qkv_scatter.second()
    down_part = down_scatter.result()
    in_part = in_scatter.result()
    outputs = outputs.finish(seat)
    (in_part, down_part, outputs) = fence([qkv_scatter], in_part, down_part, outputs)
    qkv_scatter.along_z()
    grad_inputs = grad_inputs.finish(seat)
    (grad_inputs,) = fence([qkv_scatter], grad_inputs)
    qkv_part = qkv_scatter.result()
    early_out = unpack_rows(qkv_part[:, 3 * width :], [share, share])
    late_out = unpack_rows(
        in_part[:, inner_width + width :], [v.shape[0] for v in late_vectors]
    )
    return (
        outputs,
        grad_inputs,
        kind_major(qkv_part[:, : 3 * width]),
        early_out[0],
        early_out[1],
        in_part[:, inner_width : inner_width + width],
        late_out[0],
        late_out[1],
        late_out[2],
        in_part[:, :inner_width],
        late_out[3],
        down_part,
        late_out[4],
        late_out[5],
        late_out[6],
    )


def solution(mesh):
    placed = (
        P("dp", "seq", None),
        P("dp"),
        P(("dp", "seq"), None),
        P(("dp", "seq")),
        P(("dp", "seq")),
        P(("dp", "seq"), None),
        P(("dp", "seq")),
        P(("dp", "seq")),
        P(("dp", "seq")),
        P(("dp", "seq"), None),
        P(("dp", "seq")),
        P(("dp", "seq"), None),
        P(("dp", "seq")),
        P(("dp", "seq")),
        P(("dp", "seq")),
        P("dp", "seq", None),
    )
    return jax.shard_map(
        on_device,
        mesh=mesh,
        in_specs=placed,
        out_specs=(
            P("dp", "seq", None),
            P("dp", "seq", None),
            P(("dp", "seq"), None),
            P(("dp", "seq")),
            P(("dp", "seq")),
            P(("dp", "seq"), None),
            P(("dp", "seq")),
            P(("dp", "seq")),
            P(("dp", "seq")),
            P(("dp", "seq"), None),
            P(("dp", "seq")),
            P(("dp", "seq"), None),
            P(("dp", "seq")),
            P(("dp", "seq")),
            P(("dp", "seq")),
        ),
        check_vma=False,
    )
```

```python
import functools

import jax
import jax.numpy as jnp
from jax import lax
from jax.experimental import pallas as pl
from jax.experimental.pallas import tpu as pltpu
from jax.sharding import PartitionSpec as P

BF = jnp.bfloat16
F32 = jnp.float32
HD = 64
BOTH = ("dp", "seq")

def layer_norm(value, gain, shift):
    center = jnp.mean(value, -1, keepdims=True)
    centered = value - center
    spread = jnp.mean(centered * centered, -1, keepdims=True)
    return centered * lax.rsqrt(spread + 1e-12) * gain + shift


def over_rows(left, right):
    return lax.dot_general(
        left, right, (((0,), (0,)), ((), ())), preferred_element_type=jnp.float32
    )


def times_transposed(left, right):
    return lax.dot_general(
        left, right, (((1,), (1,)), ((), ())), preferred_element_type=jnp.float32
    )


def nt(a, b):
    return lax.dot_general(a, b, (((1,), (1,)), ((), ())), preferred_element_type=F32)


def tn(a, b):
    return lax.dot_general(a, b, (((0,), (0,)), ((), ())), preferred_element_type=F32)


def nn(a, b):
    return lax.dot_general(a, b, (((1,), (0,)), ((), ())), preferred_element_type=F32)


def masked_pair(q, k, bias, head, lane):
    mine = (lane >= head * HD) & (lane < (head + 1) * HD)
    spare = lane == (HD if head == 0 else 0)
    zero = jnp.zeros((), BF)
    qh = jnp.where(mine, q * BF(0.125), jnp.where(spare, jnp.ones((), BF), zero))
    kh = jnp.where(mine, k, jnp.where(spare, bias, zero))
    return qh, kh


def forward_kernel(packed_ref, mask_ref, mixed_ref, logsum_ref):
    count = packed_ref.shape[0]
    lane = lax.broadcasted_iota(jnp.int32, (count, 128), 1)
    q, k, v = (packed_ref[:, i * 128 : (i + 1) * 128] for i in range(3))
    bias = mask_ref[0]
    halves = []
    for h in range(2):
        qh, kh = masked_pair(q, k, bias, h, lane)
        scores = nt(kh, qh)
        top = jnp.max(scores, 0, keepdims=True)
        raised = jnp.exp(scores - top)
        total = jnp.sum(raised, 0, keepdims=True)
        mixed = tn(v[:, h * HD : (h + 1) * HD], raised.astype(BF))
        halves.append(mixed * (1.0 / total))
        logsum_ref[0, h : h + 1, :] = top + jnp.log(total)
    mixed_ref[...] = jnp.concatenate(halves, 0).T.astype(BF)


def backward_kernel(packed_ref, mask_ref, logsum_ref, grad_ref, out_ref, sums_ref):
    count = packed_ref.shape[0]
    lane = lax.broadcasted_iota(jnp.int32, (count, 128), 1)
    q, k, v = (packed_ref[:, i * 128 : (i + 1) * 128] for i in range(3))
    bias = mask_ref[0]
    grad = grad_ref[...]
    q_scaled, k_scaled = q * BF(0.125), k * BF(0.125)
    dq, dk, dv = [], [], []
    for h in range(2):
        qh, kh = masked_pair(q, k, bias, h, lane)
        mine = (lane >= h * HD) & (lane < (h + 1) * HD)
        vh = jnp.where(mine, v, jnp.zeros((), BF))
        probs = jnp.exp(nt(kh, qh) - logsum_ref[0, h : h + 1, :])
        grad_probs = nt(vh, grad)
        inner = jnp.sum(probs * grad_probs, 0, keepdims=True)
        grad_scores = (probs * (grad_probs - inner)).astype(BF)
        dv.append(nn(probs.astype(BF), grad))
        dk.append(nn(grad_scores, q_scaled))
        dq.append(tn(k_scaled[:, h * HD : (h + 1) * HD], grad_scores))
    low_half = lane < HD
    parts = (
        jnp.concatenate(dq, 0).T,
        jnp.where(low_half, dk[0], dk[1]),
        jnp.where(low_half, dv[0], dv[1]),
    )
    for i, part in enumerate(parts):
        rounded = part.astype(BF)
        out_ref[:, i * 128 : (i + 1) * 128] = rounded
        sums_ref[0, :, i * 128 : (i + 1) * 128] = jnp.sum(
            rounded.astype(F32), 0, keepdims=True
        )


def attention_specs(packed, length):
    rows, wide = packed.shape
    pairs, seqs = wide // 384, rows // length
    block = lambda size: pl.BlockSpec((length, size), lambda s, p: (s, p))
    mask = pl.BlockSpec((1, length, 128), lambda s, p: (s, 0, 0))
    row = lambda count, size: pl.BlockSpec((1, count, size), lambda s, p: (s * pairs + p, 0, 0))
    return rows, pairs, seqs, block, mask, row


def attention_forward(packed, mask, length):
    rows, pairs, seqs, block, mask_spec, row = attention_specs(packed, length)
    return pl.pallas_call(
        forward_kernel,
        grid=(seqs, pairs),
        in_specs=[block(384), mask_spec],
        out_specs=[block(128), row(2, length)],
        out_shape=[
            jax.ShapeDtypeStruct((rows, pairs * 128), BF),
            jax.ShapeDtypeStruct((seqs * pairs, 2, length), F32),
        ],
        compiler_params=pltpu.CompilerParams(vmem_limit_bytes=48 * 2**20),
        name="attention_forward",
        cost_estimate=pl.CostEstimate(
            flops=16 * rows * length * pairs * 128,
            bytes_accessed=rows * pairs * 1024,
            transcendentals=2 * rows * length * pairs,
        ),
    )(packed, mask)


def attention_backward(packed, mask, logsum, grad, length):
    rows, pairs, seqs, block, mask_spec, row = attention_specs(packed, length)
    return pl.pallas_call(
        backward_kernel,
        grid=(seqs, pairs),
        in_specs=[block(384), mask_spec, row(2, length), block(128)],
        out_specs=[block(384), row(1, 384)],
        out_shape=[
            jax.ShapeDtypeStruct((rows, pairs * 384), BF),
            jax.ShapeDtypeStruct((seqs * pairs, 1, 384), F32),
        ],
        compiler_params=pltpu.CompilerParams(vmem_limit_bytes=48 * 2**20),
        name="attention_backward",
        cost_estimate=pl.CostEstimate(
            flops=28 * rows * length * pairs * 128,
            bytes_accessed=rows * pairs * 1792,
            transcendentals=2 * rows * length * pairs,
        ),
    )(packed, mask, logsum, grad)


def pair_major(block):
    lead = block.shape[:-1]
    return block.reshape(lead + (3, -1, 128)).swapaxes(-3, -2).reshape(block.shape)


def kind_major(block):
    lead = block.shape[:-1]
    return block.reshape(lead + (-1, 3, 128)).swapaxes(-3, -2).reshape(block.shape)


def feed_forward_kernel(step, x_ref, w_ref, b_ref, active_ref, slope_ref):
    x = x_ref[...]
    for start in range(0, w_ref.shape[1], step):
        part = slice(start, start + step)
        hidden = nn(x, w_ref[:, part]) + b_ref[:, part]
        bell = jnp.exp(hidden * hidden * -0.5)
        share = 0.5 * (1.0 + lax.erf(hidden * 0.7071067811865476))
        active_ref[:, part] = (hidden * share).astype(BF)
        slope_ref[:, part] = (share + hidden * bell * 0.3989422804014327).astype(BF)


def feed_forward(x, weight, bias):
    rows, width = x.shape
    inner = weight.shape[1]
    block = 256
    out = jax.ShapeDtypeStruct((rows, inner), BF)
    return pl.pallas_call(
        functools.partial(feed_forward_kernel, 512),
        grid=(rows // block,),
        in_specs=[
            pl.BlockSpec((block, width), lambda i: (i, 0)),
            pl.BlockSpec((width, inner), lambda i: (0, 0)),
            pl.BlockSpec((1, inner), lambda i: (0, 0)),
        ],
        out_specs=[pl.BlockSpec((block, inner), lambda i: (i, 0))] * 2,
        out_shape=[out, out],
        compiler_params=pltpu.CompilerParams(vmem_limit_bytes=48 * 2**20),
        name="feed_forward",
        cost_estimate=pl.CostEstimate(
            flops=2 * rows * width * inner,
            bytes_accessed=4 * rows * inner + 2 * width * inner,
            transcendentals=2 * rows * inner,
        ),
    )(x, weight, bias)


def second_norm_kernel(
    active_ref, weight_ref, first_ref, cot_ref, rows_ref, out_ref, grad_ref, low_ref, sums_ref
):
    bias, gain, shift = rows_ref[0:1, :], rows_ref[1:2, :], rows_ref[2:3, :]
    value = first_ref[...].astype(F32) + (nn(active_ref[...], weight_ref[...]) + bias)
    centered = value - jnp.mean(value, -1, keepdims=True)
    scale = lax.rsqrt(jnp.mean(centered * centered, -1, keepdims=True) + 1e-12)
    normal = centered * scale
    out_ref[...] = (normal * gain + shift).astype(BF)
    cot = cot_ref[...].astype(F32)
    scaled = cot * gain
    inner = jnp.mean(scaled * normal, -1, keepdims=True)
    grad = scale * (scaled - jnp.mean(scaled, -1, keepdims=True) - normal * inner)
    low = grad.astype(BF)
    grad_ref[...] = grad
    low_ref[...] = low

    @pl.when(pl.program_id(0) == 0)
    def _():
        sums_ref[...] = jnp.zeros_like(sums_ref)

    sums_ref[0:1, :] += jnp.sum(low.astype(F32), 0, keepdims=True)
    sums_ref[1:2, :] += jnp.sum(cot * normal, 0, keepdims=True)
    sums_ref[2:3, :] += jnp.sum(cot, 0, keepdims=True)


def second_norm(active, weight, first, cot, bias, gain, shift):
    rows, inner = active.shape
    width = weight.shape[1]
    block = 256
    side = jnp.stack([bias, gain, shift] + [jnp.zeros_like(bias)] * 5)
    tile = lambda size: pl.BlockSpec((block, size), lambda i: (i, 0))
    whole = lambda count: pl.BlockSpec((count, width), lambda i: (0, 0))
    return pl.pallas_call(
        second_norm_kernel,
        grid=(rows // block,),
        in_specs=[tile(inner), whole(inner), tile(width), tile(width), whole(8)],
        out_specs=[tile(width), tile(width), tile(width), whole(8)],
        out_shape=[
            jax.ShapeDtypeStruct((rows, width), BF),
            jax.ShapeDtypeStruct((rows, width), F32),
            jax.ShapeDtypeStruct((rows, width), BF),
            jax.ShapeDtypeStruct((8, width), F32),
        ],
        compiler_params=pltpu.CompilerParams(vmem_limit_bytes=48 * 2**20),
        name="second_norm",
        cost_estimate=pl.CostEstimate(
            flops=2 * rows * width * inner,
            bytes_accessed=2 * (rows * inner + inner * width) + 12 * rows * width,
            transcendentals=rows,
        ),
    )(active, weight, first, cot, side)


def swap(block, distance, devices):
    return lax.ppermute(block, BOTH, [(i, i ^ distance) for i in range(devices)])


def after(value, *done):
    return lax.optimization_barrier((value,) + done)[0]


def place_kernel(ids, counts, spans, me_ref, *refs):
    pieces, rest = refs[: len(counts)], refs[len(counts) :]
    outs, sems = rest[: len(spans)], rest[len(spans)]
    me = me_ref[0]
    copies = []
    at = 0
    for piece, count in zip(pieces, counts):
        for j in range(count):
            spot = me ^ ids[at]
            for out, (start, size) in zip(outs, spans):
                source = piece.at[j] if len(spans) == 1 else piece.at[j, :, pl.ds(start, size)]
                copy = pltpu.make_async_copy(source, out.at[spot], sems.at[len(copies)])
                copy.start()
                copies.append(copy)
            at += 1
    for copy in copies:
        copy.wait()


def place(pieces, ids, me, spans=None):
    counts = [p.shape[0] for p in pieces]
    total = sum(counts)
    tail = pieces[0].shape[1:]
    spans = spans or [(0, tail[-1])]
    any_space = pl.BlockSpec(memory_space=pl.ANY)
    moved = 2 * sum(p.size * p.dtype.itemsize for p in pieces)
    return pl.pallas_call(
        functools.partial(place_kernel, ids, counts, spans),
        in_specs=[pl.BlockSpec(memory_space=pltpu.SMEM)] + [any_space] * len(pieces),
        out_specs=[pl.BlockSpec(memory_space=pltpu.VMEM)] * len(spans),
        out_shape=[
            jax.ShapeDtypeStruct((total,) + tail[:-1] + (size,), pieces[0].dtype)
            for _, size in spans
        ],
        scratch_shapes=[pltpu.SemaphoreType.DMA((total * len(spans),))],
        compiler_params=pltpu.CompilerParams(vmem_limit_bytes=32 * 2**20),
        cost_estimate=pl.CostEstimate(flops=0, bytes_accessed=moved, transcendentals=0),
        name="place_blocks",
    )(me.reshape(1), *pieces)


def pack_rows(vectors, share):
    lead = vectors[0].shape[:-1]
    columns = []
    for at in range(0, len(vectors), share):
        rows = []
        for v in vectors[at : at + share]:
            rows.append(jnp.pad(v, [(0, 0)] * len(lead) + [(0, 128 - v.shape[-1])]))
        block = jnp.stack(rows, -2)
        columns.append(
            jnp.pad(block, [(0, 0)] * len(lead) + [(0, share - len(rows)), (0, 0)])
        )
    return columns[0] if len(columns) == 1 else jnp.concatenate(columns, -1)


def unpack_rows(block, sizes):
    share = block.shape[-2]
    out = []
    for i, size in enumerate(sizes):
        start = i // share * 128
        out.append(block[..., i % share, start : start + size])
    return out


def fence(holders, *values):
    arrays = [a for h in holders for a in h.arrays()]
    kept = lax.optimization_barrier(tuple(arrays) + values)
    at = 0
    for h in holders:
        count = len(h.arrays())
        h.put(list(kept[at : at + count]))
        at += count
    return kept[at:]


class Gather:
    def __init__(self, block, me, devices, plan):
        self.me, self.devices, self.plan = me, devices, plan
        self.held, self.ids = [block[None]], [[0]]

    def arrays(self):
        return self.held

    def put(self, arrays):
        self.held = arrays

    def swapped(self, block, distance):
        return swap(block, distance, self.devices)

    def along_z(self):
        own, own_ids = self.held[0], self.ids[0]
        distance = 32
        while distance < self.devices:
            own = jnp.concatenate([own, self.swapped(own, distance)])
            own_ids = own_ids + [i ^ distance for i in own_ids]
            distance *= 2
        self.held = [own] + [self.swapped(own, 8 * k) for k in (1, 2, 3)]
        self.ids = [[i ^ (8 * k) for i in own_ids] for k in range(4)]

    def grow(self, order):
        held, ids = [], []
        for block, block_ids, distance in zip(self.held, self.ids, order):
            held += [block, self.swapped(block, distance)]
            ids += [block_ids, [i ^ distance for i in block_ids]]
        self.held, self.ids = held, ids

    def join(self, pairs):
        self.held = [jnp.concatenate([self.held[i] for i in p]) for p in pairs]
        self.ids = [[i for j in p for i in self.ids[j]] for p in pairs]

    def first(self):
        if self.plan == "split":
            self.join([(0, 1), (2, 3)])
            self.grow((4, 2))
        else:
            self.join([(0, 1, 2, 3)])
            self.grow((4,) if self.plan == "xy" else (2,))

    def second(self):
        if self.plan == "split":
            self.join([(0, 1), (2, 3)])
            self.grow((2, 4))
        else:
            self.join([(0, 1)])
            self.grow((2,) if self.plan == "xy" else (4,))

    def core(self):
        self.grow((1,) * len(self.held))

    def finish(self, spans=None):
        return place(self.held, [i for ids in self.ids for i in ids], self.me, spans)


def pick(block, axis, index):
    return lax.dynamic_index_in_dim(block, index, axis, keepdims=False)


def fold(block, axis, me, distance, devices):
    digit = (me // distance) % 2
    got = swap(pick(block, axis, 1 - digit), distance, devices)
    return (pick(block, axis, digit).astype(F32) + got.astype(F32)).astype(BF)


def core_sum(total, me, devices):
    tail = total.shape[1:]
    distance = devices // 2
    while distance >= 32:
        total = fold(total.reshape((2, distance) + tail), 0, me, distance, devices)
        distance //= 2
    return fold(total.reshape((16, 2) + tail), 1, me, 1, devices)


class Scatter:
    def __init__(self, total, me, devices, plan):
        self.me, self.devices, self.plan = me, devices, plan
        self.tail = total.shape[1:]
        self.held = [total]

    def arrays(self):
        return self.held

    def put(self, arrays):
        self.held = arrays

    def fold(self, block, axis, distance):
        return fold(block, axis, self.me, distance, self.devices)

    def first(self):
        total = self.held[0].reshape((4, 2, 2) + self.tail)
        if self.plan == "split":
            z = (self.me // 8) % 4
            halves = total.reshape((2, 2, 2, 2) + self.tail)
            self.held = [
                self.fold(pick(halves, 0, z // 2), 1, 4),
                self.fold(pick(halves, 0, 1 - z // 2), 2, 2),
            ]
        elif self.plan == "xy":
            self.held = [self.fold(total, 1, 4)]
        else:
            self.held = [self.fold(total, 2, 2)]

    def second(self):
        z = (self.me // 8) % 4
        if self.plan == "split":
            near = self.fold(self.held[0], 1, 2)
            away = self.fold(self.held[1], 1, 4)
            odd = z % 2
            self.held = [
                pick(near, 0, odd),
                pick(near, 0, 1 - odd),
                pick(away, 0, odd),
                pick(away, 0, 1 - odd),
            ]
        else:
            total = self.fold(self.held[0], 1, 2 if self.plan == "xy" else 4)
            self.held = [pick(total, 0, z ^ k) for k in range(4)]

    def along_z(self):
        sent = [swap(self.held[k], 8 * k, self.devices) for k in (1, 2, 3)]
        self.held = [self.held[0]] + sent

    def result(self):
        return sum(block.astype(F32) for block in self.held)


class ToSequences:
    def __init__(self, block, seat, members, devices):
        groups, count, width = block.shape
        parts = block.reshape(members, groups // members, count, width)
        self.devices = devices
        self.held = [pick(parts, 0, seat ^ k) for k in range(members)]

    def arrays(self):
        return self.held

    def put(self, arrays):
        self.held = arrays

    def send(self, k):
        self.held[k] = swap(self.held[k], k, self.devices)

    def finish(self):
        return jnp.stack(self.held, 1).reshape(-1, self.held[0].shape[-1])


class ToPositions:
    def __init__(self, block, members, devices):
        self.devices = devices
        self.held = [block[:, k][None] for k in range(members)]

    def arrays(self):
        return self.held

    def put(self, arrays):
        self.held = arrays

    def send(self, k):
        self.held[k] = swap(self.held[k], k, self.devices)

    def finish(self, seat):
        (placed,) = place(self.held, list(range(len(self.held))), seat)
        return placed.reshape((-1,) + placed.shape[2:])


def on_device(
    inputs,
    lengths,
    query_key_value_weight,
    query_bias,
    value_bias,
    output_weight,
    output_bias,
    norm1_gain,
    norm1_shift,
    in_weight,
    in_bias,
    down_weight,
    down_bias,
    norm2_gain,
    norm2_shift,
    cotangent,
):
    groups, local_len, width = inputs.shape
    rows = groups * local_len
    members = lax.axis_size("seq")
    devices = lax.axis_size("dp") * members
    kept = groups // members
    length = local_len * members
    seat = lax.axis_index("seq")
    me = lax.axis_index("dp") * members + seat
    share = query_key_value_weight.shape[0]
    inner_width = in_weight.shape[1]
    early = pack_rows([query_bias, value_bias], share)
    qkv_gather = Gather(
        jnp.concatenate([pair_major(query_key_value_weight), early], 1), me, devices, "split"
    )
    late_vectors = [
        output_bias,
        norm1_gain,
        norm1_shift,
        in_bias,
        down_bias,
        norm2_gain,
        norm2_shift,
    ]
    late = pack_rows(late_vectors, share)
    in_gather = Gather(
        jnp.concatenate([in_weight, output_weight, late], 1), me, devices, "split"
    )
    down_gather = Gather(down_weight, me, devices, "split")
    near, far = range(1, (members + 1) // 2), range((members + 1) // 2, members)
    flat = ToSequences(inputs, seat, members, devices)
    for k in range(1, members):
        flat.send(k)
    qkv_gather.along_z()
    fence([qkv_gather])
    qkv_gather.first()
    in_gather.put([after(a, qkv_gather.held[1]) for a in in_gather.arrays()])
    in_gather.along_z()
    in_gather.held[:2] = fence([qkv_gather, flat], *in_gather.held[:2])
    qkv_gather.second()
    fence([qkv_gather, in_gather])
    qkv_gather.core()
    fence([qkv_gather])
    in_gather.first()
    flat = flat.finish()
    wide_qkv, early = qkv_gather.finish([(0, 3 * width), (3 * width, early.shape[1])])
    (wide_qkv, early, flat) = fence([in_gather], wide_qkv, early, flat)
    in_gather.second()
    wide_qkv = wide_qkv.reshape(width, 3 * width)
    full_query_bias, full_value_bias = [
        v.reshape(-1).astype(F32) for v in unpack_rows(early, [share, share])
    ]
    bias_vector = jnp.concatenate([full_query_bias, jnp.zeros((width,), F32), full_value_bias])
    packed = jnp.dot(flat, wide_qkv, preferred_element_type=F32) + pair_major(bias_vector)
    packed = packed.astype(BF)
    (packed,) = fence([], packed)
    down_gather.put([after(a, packed) for a in down_gather.arrays()])
    down_gather.along_z()
    mine = lax.dynamic_slice(lengths, (seat * kept,), (kept,))
    slots = jnp.arange(length, dtype=jnp.int32)
    positions = ((slots // local_len) ^ seat) * local_len + slots % local_len
    mask = jnp.where(positions[None, :] < mine[:, None], 0.0, -1e30).astype(BF)
    mask = jnp.broadcast_to(mask[:, :, None], (kept, length, 128))
    mixed, logsum = attention_forward(packed, mask, length)
    (mixed, logsum, packed) = fence([in_gather, down_gather], mixed, logsum, packed)
    in_gather.core()
    down_gather.first()
    fence([in_gather])
    wide_in, wide_out, late = in_gather.finish(
        [(0, inner_width), (inner_width, width), (inner_width + width, late.shape[1])]
    )
    (wide_in, wide_out, late) = fence([down_gather], wide_in, wide_out, late)
    down_gather.second()
    wide_in = wide_in.reshape(width, inner_width)
    wide_out = wide_out.reshape(width, width)
    (
        full_out_bias,
        gain_one,
        shift_one,
        full_in_bias,
        full_down_bias,
        gain_two,
        shift_two,
    ) = [
        v.reshape(-1).astype(F32)
        for v in unpack_rows(late, [v.shape[0] for v in late_vectors])
    ]
    attention_branch = jnp.dot(mixed, wide_out, preferred_element_type=F32) + full_out_bias
    first, norm_one_pull = jax.vjp(
        layer_norm, flat.astype(F32) + attention_branch, gain_one, shift_one
    )
    first_low = first.astype(BF)
    (first_low,) = fence([down_gather], first_low)
    down_gather.core()
    cot = ToSequences(after(cotangent, first_low), seat, members, devices)
    for k in range(1, members):
        cot.send(k)
    active_low, slope = feed_forward(first_low, wide_in, full_in_bias[None])
    (active_low, slope) = fence([down_gather, cot], active_low, slope)
    (wide_down,) = down_gather.finish()
    wide_down = wide_down.reshape(inner_width, width)
    outputs, grad_second, grad_branch_two, norm_sums = second_norm(
        active_low, wide_down, first_low, cot.finish(), full_down_bias, gain_two, shift_two
    )
    (outputs, grad_second, grad_branch_two, norm_sums) = fence(
        [], outputs, grad_second, grad_branch_two, norm_sums
    )
    outputs = outputs.reshape(kept, members, local_len, width)
    grad_down_bias, grad_gain_two, grad_shift_two = (norm_sums[i] for i in range(3))
    outputs = ToPositions(outputs, members, devices)
    for k in near:
        outputs.send(k)
    for k in far[:1]:
        outputs.send(k)
    grad_down = over_rows(active_low, grad_branch_two).astype(BF)
    (grad_down, grad_branch_two) = fence([outputs], grad_down, grad_branch_two)
    for k in far[1:]:
        outputs.send(k)
    down_scatter = Scatter(
        core_sum(grad_down.reshape(devices, -1, width), me, devices), me, devices, "split"
    )
    grad_hidden_low = (
        times_transposed(grad_branch_two, wide_down) * slope.astype(F32)
    ).astype(BF)
    grad_in_bias = jnp.sum(grad_hidden_low.astype(F32), 0)
    (grad_hidden_low, grad_in_bias) = fence([outputs, down_scatter], grad_hidden_low, grad_in_bias)
    down_scatter.first()
    grad_in = over_rows(first_low, grad_hidden_low).astype(BF)
    (grad_in, grad_hidden_low) = fence([down_scatter], grad_in, grad_hidden_low)
    down_scatter.second()
    in_core = core_sum(grad_in.reshape(devices, share, inner_width), me, devices)
    grad_first = times_transposed(grad_hidden_low, wide_in) + grad_second
    grad_residual, grad_gain_one, grad_shift_one = norm_one_pull(grad_first)
    grad_branch_one = grad_residual.astype(BF)
    grad_out_bias = jnp.sum(grad_branch_one.astype(F32), 0)
    grad_out = over_rows(mixed, grad_branch_one).astype(BF)
    late_sums = [
        grad_out_bias,
        grad_gain_one,
        grad_shift_one,
        grad_in_bias,
        grad_down_bias,
        grad_gain_two,
        grad_shift_two,
    ]
    late_block = pack_rows([v.reshape(devices, -1) for v in late_sums], share).astype(BF)
    out_core = core_sum(
        jnp.concatenate([grad_out.reshape(devices, share, width), late_block], 2), me, devices
    )
    grad_mixed = times_transposed(grad_branch_one, wide_out).astype(BF)
    in_scatter = Scatter(jnp.concatenate([in_core, out_core], 2), me, devices, "split")
    (grad_mixed, grad_residual) = fence([down_scatter, in_scatter], grad_mixed, grad_residual)
    in_scatter.first()
    down_scatter.along_z()
    grad_packed, column_sums = attention_backward(packed, mask, logsum, grad_mixed, length)
    (grad_packed, column_sums) = fence([in_scatter, down_scatter], grad_packed, column_sums)
    in_scatter.second()
    grad_qkv = over_rows(flat, grad_packed).astype(BF)
    column_sums = kind_major(column_sums.reshape(kept, 3 * width).sum(0))
    early_sums = [column_sums[:width], column_sums[2 * width :]]
    early_block = pack_rows([v.reshape(devices, -1) for v in early_sums], share).astype(BF)
    grad_qkv = jnp.concatenate([grad_qkv.reshape(devices, share, 3 * width), early_block], 2)
    (grad_qkv, grad_packed) = fence([], grad_qkv, grad_packed)
    qkv_scatter = Scatter(core_sum(grad_qkv, me, devices), me, devices, "split")
    grad_inputs = (times_transposed(grad_packed, wide_qkv) + grad_residual).astype(BF)
    (grad_inputs,) = fence([in_scatter, qkv_scatter], grad_inputs)
    grad_inputs = ToPositions(
        grad_inputs.reshape(kept, members, local_len, width), members, devices
    )
    qkv_scatter.first()
    in_scatter.along_z()
    fence([qkv_scatter, grad_inputs])
    qkv_scatter.second()
    for k in near:
        grad_inputs.send(k)
    for k in far[:1]:
        grad_inputs.send(k)
    fence([qkv_scatter, grad_inputs, in_scatter])
    for k in far[1:]:
        grad_inputs.send(k)
    qkv_scatter.along_z()
    outputs.put([after(a, *qkv_scatter.held[:1]) for a in outputs.arrays()])
    outputs = outputs.finish(seat)
    in_part = in_scatter.result()
    down_part = down_scatter.result()
    (in_part, outputs) = fence([qkv_scatter, grad_inputs], in_part, outputs)
    qkv_part = qkv_scatter.result()
    grad_inputs = grad_inputs.finish(seat)
    early_out = unpack_rows(qkv_part[:, 3 * width :], [share, share])
    late_out = unpack_rows(
        in_part[:, inner_width + width :], [v.shape[0] for v in late_vectors]
    )
    return (
        outputs,
        grad_inputs,
        kind_major(qkv_part[:, : 3 * width]),
        early_out[0],
        early_out[1],
        in_part[:, inner_width : inner_width + width],
        late_out[0],
        late_out[1],
        late_out[2],
        in_part[:, :inner_width],
        late_out[3],
        down_part,
        late_out[4],
        late_out[5],
        late_out[6],
    )


def solution(mesh):
    placed = (
        P("dp", "seq", None),
        P("dp"),
        P(("dp", "seq"), None),
        P(("dp", "seq")),
        P(("dp", "seq")),
        P(("dp", "seq"), None),
        P(("dp", "seq")),
        P(("dp", "seq")),
        P(("dp", "seq")),
        P(("dp", "seq"), None),
        P(("dp", "seq")),
        P(("dp", "seq"), None),
        P(("dp", "seq")),
        P(("dp", "seq")),
        P(("dp", "seq")),
        P("dp", "seq", None),
    )
    return jax.shard_map(
        on_device,
        mesh=mesh,
        in_specs=placed,
        out_specs=(
            P("dp", "seq", None),
            P("dp", "seq", None),
            P(("dp", "seq"), None),
            P(("dp", "seq")),
            P(("dp", "seq")),
            P(("dp", "seq"), None),
            P(("dp", "seq")),
            P(("dp", "seq")),
            P(("dp", "seq")),
            P(("dp", "seq"), None),
            P(("dp", "seq")),
            P(("dp", "seq"), None),
            P(("dp", "seq")),
            P(("dp", "seq")),
            P(("dp", "seq")),
        ),
        check_vma=False,
    )
```

```python
import functools

import jax
import jax.numpy as jnp
from jax import lax
from jax.experimental import pallas as pl
from jax.experimental.pallas import tpu as pltpu
from jax.sharding import PartitionSpec as P

BF = jnp.bfloat16
F32 = jnp.float32
HD = 64
BOTH = ("dp", "seq")

def layer_norm(value, gain, shift):
    center = jnp.mean(value, -1, keepdims=True)
    centered = value - center
    spread = jnp.mean(centered * centered, -1, keepdims=True)
    return centered * lax.rsqrt(spread + 1e-12) * gain + shift


def over_rows(left, right):
    return lax.dot_general(
        left, right, (((0,), (0,)), ((), ())), preferred_element_type=jnp.float32
    )


def times_transposed(left, right):
    return lax.dot_general(
        left, right, (((1,), (1,)), ((), ())), preferred_element_type=jnp.float32
    )


def nt(a, b):
    return lax.dot_general(a, b, (((1,), (1,)), ((), ())), preferred_element_type=F32)


def tn(a, b):
    return lax.dot_general(a, b, (((0,), (0,)), ((), ())), preferred_element_type=F32)


def nn(a, b):
    return lax.dot_general(a, b, (((1,), (0,)), ((), ())), preferred_element_type=F32)


def masked_pair(q, k, bias, head, lane):
    mine = (lane >= head * HD) & (lane < (head + 1) * HD)
    spare = lane == (HD if head == 0 else 0)
    zero = jnp.zeros((), BF)
    qh = jnp.where(mine, q * BF(0.125), jnp.where(spare, jnp.ones((), BF), zero))
    kh = jnp.where(mine, k, jnp.where(spare, bias, zero))
    return qh, kh


def forward_kernel(packed_ref, mask_ref, mixed_ref, logsum_ref):
    count = packed_ref.shape[0]
    lane = lax.broadcasted_iota(jnp.int32, (count, 128), 1)
    q, k, v = (packed_ref[:, i * 128 : (i + 1) * 128] for i in range(3))
    bias = mask_ref[0]
    halves = []
    for h in range(2):
        qh, kh = masked_pair(q, k, bias, h, lane)
        scores = nt(kh, qh)
        top = jnp.max(scores, 0, keepdims=True)
        raised = jnp.exp(scores - top)
        total = jnp.sum(raised, 0, keepdims=True)
        mixed = tn(v[:, h * HD : (h + 1) * HD], raised.astype(BF))
        halves.append(mixed * (1.0 / total))
        logsum_ref[0, h : h + 1, :] = top + jnp.log(total)
    mixed_ref[...] = jnp.concatenate(halves, 0).T.astype(BF)


def backward_kernel(packed_ref, mask_ref, logsum_ref, grad_ref, out_ref, sums_ref):
    count = packed_ref.shape[0]
    lane = lax.broadcasted_iota(jnp.int32, (count, 128), 1)
    q, k, v = (packed_ref[:, i * 128 : (i + 1) * 128] for i in range(3))
    bias = mask_ref[0]
    grad = grad_ref[...]
    q_scaled, k_scaled = q * BF(0.125), k * BF(0.125)
    dq, dk, dv = [], [], []
    for h in range(2):
        qh, kh = masked_pair(q, k, bias, h, lane)
        mine = (lane >= h * HD) & (lane < (h + 1) * HD)
        vh = jnp.where(mine, v, jnp.zeros((), BF))
        probs = jnp.exp(nt(kh, qh) - logsum_ref[0, h : h + 1, :])
        grad_probs = nt(vh, grad)
        inner = jnp.sum(probs * grad_probs, 0, keepdims=True)
        grad_scores = (probs * (grad_probs - inner)).astype(BF)
        dv.append(nn(probs.astype(BF), grad))
        dk.append(nn(grad_scores, q_scaled))
        dq.append(tn(k_scaled[:, h * HD : (h + 1) * HD], grad_scores))
    low_half = lane < HD
    parts = (
        jnp.concatenate(dq, 0).T,
        jnp.where(low_half, dk[0], dk[1]),
        jnp.where(low_half, dv[0], dv[1]),
    )
    for i, part in enumerate(parts):
        rounded = part.astype(BF)
        out_ref[:, i * 128 : (i + 1) * 128] = rounded
        sums_ref[0, :, i * 128 : (i + 1) * 128] = jnp.sum(
            rounded.astype(F32), 0, keepdims=True
        )


def attention_specs(packed, length):
    rows, wide = packed.shape
    pairs, seqs = wide // 384, rows // length
    block = lambda size: pl.BlockSpec((length, size), lambda s, p: (s, p))
    mask = pl.BlockSpec((1, length, 128), lambda s, p: (s, 0, 0))
    row = lambda count, size: pl.BlockSpec((1, count, size), lambda s, p: (s * pairs + p, 0, 0))
    return rows, pairs, seqs, block, mask, row


def attention_forward(packed, mask, length):
    rows, pairs, seqs, block, mask_spec, row = attention_specs(packed, length)
    return pl.pallas_call(
        forward_kernel,
        grid=(seqs, pairs),
        in_specs=[block(384), mask_spec],
        out_specs=[block(128), row(2, length)],
        out_shape=[
            jax.ShapeDtypeStruct((rows, pairs * 128), BF),
            jax.ShapeDtypeStruct((seqs * pairs, 2, length), F32),
        ],
        compiler_params=pltpu.CompilerParams(vmem_limit_bytes=48 * 2**20),
        name="attention_forward",
        cost_estimate=pl.CostEstimate(
            flops=16 * rows * length * pairs * 128,
            bytes_accessed=rows * pairs * 1024,
            transcendentals=2 * rows * length * pairs,
        ),
    )(packed, mask)


def attention_backward(packed, mask, logsum, grad, length):
    rows, pairs, seqs, block, mask_spec, row = attention_specs(packed, length)
    return pl.pallas_call(
        backward_kernel,
        grid=(seqs, pairs),
        in_specs=[block(384), mask_spec, row(2, length), block(128)],
        out_specs=[block(384), row(1, 384)],
        out_shape=[
            jax.ShapeDtypeStruct((rows, pairs * 384), BF),
            jax.ShapeDtypeStruct((seqs * pairs, 1, 384), F32),
        ],
        compiler_params=pltpu.CompilerParams(vmem_limit_bytes=48 * 2**20),
        name="attention_backward",
        cost_estimate=pl.CostEstimate(
            flops=28 * rows * length * pairs * 128,
            bytes_accessed=rows * pairs * 1792,
            transcendentals=2 * rows * length * pairs,
        ),
    )(packed, mask, logsum, grad)


def pair_major(block):
    lead = block.shape[:-1]
    return block.reshape(lead + (3, -1, 128)).swapaxes(-3, -2).reshape(block.shape)


def kind_major(block):
    lead = block.shape[:-1]
    return block.reshape(lead + (-1, 3, 128)).swapaxes(-3, -2).reshape(block.shape)


def feed_forward_kernel(step, x_ref, w_ref, b_ref, active_ref, slope_ref):
    x = x_ref[...]
    for start in range(0, w_ref.shape[1], step):
        part = slice(start, start + step)
        hidden = nn(x, w_ref[:, part]) + b_ref[:, part]
        bell = jnp.exp(hidden * hidden * -0.5)
        share = 0.5 * (1.0 + lax.erf(hidden * 0.7071067811865476))
        active_ref[:, part] = (hidden * share).astype(BF)
        slope_ref[:, part] = (share + hidden * bell * 0.3989422804014327).astype(BF)


def feed_forward(x, weight, bias):
    rows, width = x.shape
    inner = weight.shape[1]
    block = 256
    out = jax.ShapeDtypeStruct((rows, inner), BF)
    return pl.pallas_call(
        functools.partial(feed_forward_kernel, 512),
        grid=(rows // block,),
        in_specs=[
            pl.BlockSpec((block, width), lambda i: (i, 0)),
            pl.BlockSpec((width, inner), lambda i: (0, 0)),
            pl.BlockSpec((1, inner), lambda i: (0, 0)),
        ],
        out_specs=[pl.BlockSpec((block, inner), lambda i: (i, 0))] * 2,
        out_shape=[out, out],
        compiler_params=pltpu.CompilerParams(vmem_limit_bytes=48 * 2**20),
        name="feed_forward",
        cost_estimate=pl.CostEstimate(
            flops=2 * rows * width * inner,
            bytes_accessed=4 * rows * inner + 2 * width * inner,
            transcendentals=2 * rows * inner,
        ),
    )(x, weight, bias)


def second_norm_kernel(
    active_ref, weight_ref, first_ref, cot_ref, rows_ref, out_ref, grad_ref, low_ref, sums_ref
):
    bias, gain, shift = rows_ref[0:1, :], rows_ref[1:2, :], rows_ref[2:3, :]
    value = first_ref[...].astype(F32) + (nn(active_ref[...], weight_ref[...]) + bias)
    centered = value - jnp.mean(value, -1, keepdims=True)
    scale = lax.rsqrt(jnp.mean(centered * centered, -1, keepdims=True) + 1e-12)
    normal = centered * scale
    out_ref[...] = (normal * gain + shift).astype(BF)
    cot = cot_ref[...].astype(F32)
    scaled = cot * gain
    inner = jnp.mean(scaled * normal, -1, keepdims=True)
    grad = scale * (scaled - jnp.mean(scaled, -1, keepdims=True) - normal * inner)
    low = grad.astype(BF)
    grad_ref[...] = grad
    low_ref[...] = low

    @pl.when(pl.program_id(0) == 0)
    def _():
        sums_ref[...] = jnp.zeros_like(sums_ref)

    sums_ref[0:1, :] += jnp.sum(low.astype(F32), 0, keepdims=True)
    sums_ref[1:2, :] += jnp.sum(cot * normal, 0, keepdims=True)
    sums_ref[2:3, :] += jnp.sum(cot, 0, keepdims=True)


def second_norm(active, weight, first, cot, bias, gain, shift):
    rows, inner = active.shape
    width = weight.shape[1]
    block = 256
    side = jnp.stack([bias, gain, shift] + [jnp.zeros_like(bias)] * 5)
    tile = lambda size: pl.BlockSpec((block, size), lambda i: (i, 0))
    whole = lambda count: pl.BlockSpec((count, width), lambda i: (0, 0))
    return pl.pallas_call(
        second_norm_kernel,
        grid=(rows // block,),
        in_specs=[tile(inner), whole(inner), tile(width), tile(width), whole(8)],
        out_specs=[tile(width), tile(width), tile(width), whole(8)],
        out_shape=[
            jax.ShapeDtypeStruct((rows, width), BF),
            jax.ShapeDtypeStruct((rows, width), F32),
            jax.ShapeDtypeStruct((rows, width), BF),
            jax.ShapeDtypeStruct((8, width), F32),
        ],
        compiler_params=pltpu.CompilerParams(vmem_limit_bytes=48 * 2**20),
        name="second_norm",
        cost_estimate=pl.CostEstimate(
            flops=2 * rows * width * inner,
            bytes_accessed=2 * (rows * inner + inner * width) + 12 * rows * width,
            transcendentals=rows,
        ),
    )(active, weight, first, cot, side)


def swap(block, distance, devices):
    return lax.ppermute(block, BOTH, [(i, i ^ distance) for i in range(devices)])


def after(value, *done):
    return lax.optimization_barrier((value,) + done)[0]


def place_kernel(ids, counts, spans, me_ref, *refs):
    pieces, rest = refs[: len(counts)], refs[len(counts) :]
    outs, sems = rest[: len(spans)], rest[len(spans)]
    me = me_ref[0]
    copies = []
    at = 0
    for piece, count in zip(pieces, counts):
        for j in range(count):
            spot = me ^ ids[at]
            for out, (start, size) in zip(outs, spans):
                source = piece.at[j] if len(spans) == 1 else piece.at[j, :, pl.ds(start, size)]
                copy = pltpu.make_async_copy(source, out.at[spot], sems.at[len(copies)])
                copy.start()
                copies.append(copy)
            at += 1
    for copy in copies:
        copy.wait()


def place(pieces, ids, me, spans=None):
    counts = [p.shape[0] for p in pieces]
    total = sum(counts)
    tail = pieces[0].shape[1:]
    spans = spans or [(0, tail[-1])]
    any_space = pl.BlockSpec(memory_space=pl.ANY)
    moved = 2 * sum(p.size * p.dtype.itemsize for p in pieces)
    return pl.pallas_call(
        functools.partial(place_kernel, ids, counts, spans),
        in_specs=[pl.BlockSpec(memory_space=pltpu.SMEM)] + [any_space] * len(pieces),
        out_specs=[pl.BlockSpec(memory_space=pltpu.VMEM)] * len(spans),
        out_shape=[
            jax.ShapeDtypeStruct((total,) + tail[:-1] + (size,), pieces[0].dtype)
            for _, size in spans
        ],
        scratch_shapes=[pltpu.SemaphoreType.DMA((total * len(spans),))],
        compiler_params=pltpu.CompilerParams(vmem_limit_bytes=32 * 2**20),
        cost_estimate=pl.CostEstimate(flops=0, bytes_accessed=moved, transcendentals=0),
        name="place_blocks",
    )(me.reshape(1), *pieces)


def pack_rows(vectors, share):
    lead = vectors[0].shape[:-1]
    columns = []
    for at in range(0, len(vectors), share):
        rows = []
        for v in vectors[at : at + share]:
            rows.append(jnp.pad(v, [(0, 0)] * len(lead) + [(0, 128 - v.shape[-1])]))
        block = jnp.stack(rows, -2)
        columns.append(
            jnp.pad(block, [(0, 0)] * len(lead) + [(0, share - len(rows)), (0, 0)])
        )
    return columns[0] if len(columns) == 1 else jnp.concatenate(columns, -1)


def unpack_rows(block, sizes):
    share = block.shape[-2]
    out = []
    for i, size in enumerate(sizes):
        start = i // share * 128
        out.append(block[..., i % share, start : start + size])
    return out


def fence(holders, *values):
    arrays = [a for h in holders for a in h.arrays()]
    kept = lax.optimization_barrier(tuple(arrays) + values)
    at = 0
    for h in holders:
        count = len(h.arrays())
        h.put(list(kept[at : at + count]))
        at += count
    return kept[at:]


class Gather:
    def __init__(self, block, me, devices, plan):
        self.me, self.devices, self.plan = me, devices, plan
        self.held, self.ids = [block[None]], [[0]]

    def arrays(self):
        return self.held

    def put(self, arrays):
        self.held = arrays

    def swapped(self, block, distance):
        return swap(block, distance, self.devices)

    def along_z(self):
        own, own_ids = self.held[0], self.ids[0]
        distance = 32
        while distance < self.devices:
            own = jnp.concatenate([own, self.swapped(own, distance)])
            own_ids = own_ids + [i ^ distance for i in own_ids]
            distance *= 2
        self.held = [own] + [self.swapped(own, 8 * k) for k in (1, 2, 3)]
        self.ids = [[i ^ (8 * k) for i in own_ids] for k in range(4)]

    def grow(self, order):
        held, ids = [], []
        for block, block_ids, distance in zip(self.held, self.ids, order):
            held += [block, self.swapped(block, distance)]
            ids += [block_ids, [i ^ distance for i in block_ids]]
        self.held, self.ids = held, ids

    def join(self, pairs):
        self.held = [jnp.concatenate([self.held[i] for i in p]) for p in pairs]
        self.ids = [[i for j in p for i in self.ids[j]] for p in pairs]

    def first(self):
        if self.plan == "split":
            self.join([(0, 1), (2, 3)])
            self.grow((4, 2))
        else:
            self.join([(0, 1, 2, 3)])
            self.grow((4,) if self.plan == "xy" else (2,))

    def second(self):
        if self.plan == "split":
            self.join([(0, 1), (2, 3)])
            self.grow((2, 4))
        else:
            self.join([(0, 1)])
            self.grow((2,) if self.plan == "xy" else (4,))

    def core(self):
        self.grow((1,) * len(self.held))

    def finish(self, spans=None):
        return place(self.held, [i for ids in self.ids for i in ids], self.me, spans)


def pick(block, axis, index):
    return lax.dynamic_index_in_dim(block, index, axis, keepdims=False)


def fold(block, axis, me, distance, devices):
    digit = (me // distance) % 2
    got = swap(pick(block, axis, 1 - digit), distance, devices)
    return (pick(block, axis, digit).astype(F32) + got.astype(F32)).astype(BF)


def core_sum(total, me, devices):
    tail = total.shape[1:]
    distance = devices // 2
    while distance >= 32:
        total = fold(total.reshape((2, distance) + tail), 0, me, distance, devices)
        distance //= 2
    return fold(total.reshape((16, 2) + tail), 1, me, 1, devices)


class Scatter:
    def __init__(self, total, me, devices, plan):
        self.me, self.devices, self.plan = me, devices, plan
        self.tail = total.shape[1:]
        self.held = [total]

    def arrays(self):
        return self.held

    def put(self, arrays):
        self.held = arrays

    def fold(self, block, axis, distance):
        return fold(block, axis, self.me, distance, self.devices)

    def first(self):
        total = self.held[0].reshape((4, 2, 2) + self.tail)
        if self.plan == "split":
            z = (self.me // 8) % 4
            halves = total.reshape((2, 2, 2, 2) + self.tail)
            self.held = [
                self.fold(pick(halves, 0, z // 2), 1, 4),
                self.fold(pick(halves, 0, 1 - z // 2), 2, 2),
            ]
        elif self.plan == "xy":
            self.held = [self.fold(total, 1, 4)]
        else:
            self.held = [self.fold(total, 2, 2)]

    def second(self):
        z = (self.me // 8) % 4
        if self.plan == "split":
            near = self.fold(self.held[0], 1, 2)
            away = self.fold(self.held[1], 1, 4)
            odd = z % 2
            self.held = [
                pick(near, 0, odd),
                pick(near, 0, 1 - odd),
                pick(away, 0, odd),
                pick(away, 0, 1 - odd),
            ]
        else:
            total = self.fold(self.held[0], 1, 2 if self.plan == "xy" else 4)
            self.held = [pick(total, 0, z ^ k) for k in range(4)]

    def along_z(self):
        sent = [swap(self.held[k], 8 * k, self.devices) for k in (1, 2, 3)]
        self.held = [self.held[0]] + sent

    def result(self):
        return sum(block.astype(F32) for block in self.held)


class ToSequences:
    def __init__(self, block, seat, members, devices):
        groups, count, width = block.shape
        parts = block.reshape(members, groups // members, count, width)
        self.devices = devices
        self.held = [pick(parts, 0, seat ^ k) for k in range(members)]

    def arrays(self):
        return self.held

    def put(self, arrays):
        self.held = arrays

    def send(self, k):
        self.held[k] = swap(self.held[k], k, self.devices)

    def finish(self):
        return jnp.stack(self.held, 1).reshape(-1, self.held[0].shape[-1])


class ToPositions:
    def __init__(self, block, members, devices):
        self.devices = devices
        self.held = [block[:, k][None] for k in range(members)]

    def arrays(self):
        return self.held

    def put(self, arrays):
        self.held = arrays

    def send(self, k):
        self.held[k] = swap(self.held[k], k, self.devices)

    def finish(self, seat):
        (placed,) = place(self.held, list(range(len(self.held))), seat)
        return placed.reshape((-1,) + placed.shape[2:])


def on_device(
    inputs,
    lengths,
    query_key_value_weight,
    query_bias,
    value_bias,
    output_weight,
    output_bias,
    norm1_gain,
    norm1_shift,
    in_weight,
    in_bias,
    down_weight,
    down_bias,
    norm2_gain,
    norm2_shift,
    cotangent,
):
    groups, local_len, width = inputs.shape
    rows = groups * local_len
    members = lax.axis_size("seq")
    devices = lax.axis_size("dp") * members
    kept = groups // members
    length = local_len * members
    seat = lax.axis_index("seq")
    me = lax.axis_index("dp") * members + seat
    share = query_key_value_weight.shape[0]
    inner_width = in_weight.shape[1]
    early = pack_rows([query_bias, value_bias], share)
    qkv_gather = Gather(
        jnp.concatenate([pair_major(query_key_value_weight), early], 1), me, devices, "split"
    )
    late_vectors = [
        output_bias,
        norm1_gain,
        norm1_shift,
        in_bias,
        down_bias,
        norm2_gain,
        norm2_shift,
    ]
    late = pack_rows(late_vectors, share)
    in_gather = Gather(
        jnp.concatenate([in_weight, output_weight, late], 1), me, devices, "split"
    )
    down_gather = Gather(down_weight, me, devices, "split")
    near, far = range(1, (members + 1) // 2), range((members + 1) // 2, members)
    flat = ToSequences(inputs, seat, members, devices)
    for k in range(1, members):
        flat.send(k)
    qkv_gather.along_z()
    fence([qkv_gather])
    qkv_gather.first()
    in_gather.put([after(a, qkv_gather.held[1]) for a in in_gather.arrays()])
    in_gather.along_z()
    in_gather.held[:3] = fence([qkv_gather, flat], *in_gather.held[:3])
    qkv_gather.second()
    fence([qkv_gather, in_gather])
    qkv_gather.core()
    fence([qkv_gather])
    in_gather.first()
    flat = flat.finish()
    wide_qkv, early = qkv_gather.finish([(0, 3 * width), (3 * width, early.shape[1])])
    (wide_qkv, early, flat) = fence([in_gather], wide_qkv, early, flat)
    in_gather.second()
    wide_qkv = wide_qkv.reshape(width, 3 * width)
    full_query_bias, full_value_bias = [
        v.reshape(-1).astype(F32) for v in unpack_rows(early, [share, share])
    ]
    bias_vector = jnp.concatenate([full_query_bias, jnp.zeros((width,), F32), full_value_bias])
    packed = jnp.dot(flat, wide_qkv, preferred_element_type=F32) + pair_major(bias_vector)
    packed = packed.astype(BF)
    (packed,) = fence([], packed)
    down_gather.put([after(a, packed) for a in down_gather.arrays()])
    down_gather.along_z()
    cot = ToSequences(after(cotangent, packed), seat, members, devices)
    for k in range(1, members):
        cot.send(k)
    mine = lax.dynamic_slice(lengths, (seat * kept,), (kept,))
    slots = jnp.arange(length, dtype=jnp.int32)
    positions = ((slots // local_len) ^ seat) * local_len + slots % local_len
    mask = jnp.where(positions[None, :] < mine[:, None], 0.0, -1e30).astype(BF)
    mask = jnp.broadcast_to(mask[:, :, None], (kept, length, 128))
    mixed, logsum = attention_forward(packed, mask, length)
    (mixed, logsum, packed) = fence(
        [in_gather, down_gather, cot], mixed, logsum, packed
    )
    in_gather.core()
    down_gather.first()
    fence([in_gather])
    wide_in, wide_out, late = in_gather.finish(
        [(0, inner_width), (inner_width, width), (inner_width + width, late.shape[1])]
    )
    (wide_in, wide_out, late) = fence([down_gather], wide_in, wide_out, late)
    down_gather.second()
    wide_in = wide_in.reshape(width, inner_width)
    wide_out = wide_out.reshape(width, width)
    (
        full_out_bias,
        gain_one,
        shift_one,
        full_in_bias,
        full_down_bias,
        gain_two,
        shift_two,
    ) = [
        v.reshape(-1).astype(F32)
        for v in unpack_rows(late, [v.shape[0] for v in late_vectors])
    ]
    attention_branch = jnp.dot(mixed, wide_out, preferred_element_type=F32) + full_out_bias
    first, norm_one_pull = jax.vjp(
        layer_norm, flat.astype(F32) + attention_branch, gain_one, shift_one
    )
    first_low = first.astype(BF)
    (first_low,) = fence([down_gather], first_low)
    down_gather.core()
    active_low, slope = feed_forward(first_low, wide_in, full_in_bias[None])
    (active_low, slope) = fence([down_gather], active_low, slope)
    (wide_down,) = down_gather.finish()
    wide_down = wide_down.reshape(inner_width, width)
    outputs, grad_second, grad_branch_two, norm_sums = second_norm(
        active_low, wide_down, first_low, cot.finish(), full_down_bias, gain_two, shift_two
    )
    (outputs, grad_second, grad_branch_two, norm_sums) = fence(
        [], outputs, grad_second, grad_branch_two, norm_sums
    )
    outputs = outputs.reshape(kept, members, local_len, width)
    grad_down_bias, grad_gain_two, grad_shift_two = (norm_sums[i] for i in range(3))
    outputs = ToPositions(outputs, members, devices)
    for k in near:
        outputs.send(k)
    for k in far[:1]:
        outputs.send(k)
    grad_down = over_rows(active_low, grad_branch_two).astype(BF)
    (grad_down, grad_branch_two) = fence([outputs], grad_down, grad_branch_two)
    for k in far[1:]:
        outputs.send(k)
    down_scatter = Scatter(
        core_sum(grad_down.reshape(devices, -1, width), me, devices), me, devices, "split"
    )
    grad_hidden_low = (
        times_transposed(grad_branch_two, wide_down) * slope.astype(F32)
    ).astype(BF)
    grad_in_bias = jnp.sum(grad_hidden_low.astype(F32), 0)
    (grad_hidden_low, grad_in_bias) = fence([outputs, down_scatter], grad_hidden_low, grad_in_bias)
    down_scatter.first()
    grad_in = over_rows(first_low, grad_hidden_low).astype(BF)
    (grad_in, grad_hidden_low) = fence([down_scatter], grad_in, grad_hidden_low)
    down_scatter.second()
    in_core = core_sum(grad_in.reshape(devices, share, inner_width), me, devices)
    grad_first = times_transposed(grad_hidden_low, wide_in) + grad_second
    grad_residual, grad_gain_one, grad_shift_one = norm_one_pull(grad_first)
    grad_branch_one = grad_residual.astype(BF)
    grad_out_bias = jnp.sum(grad_branch_one.astype(F32), 0)
    grad_out = over_rows(mixed, grad_branch_one).astype(BF)
    late_sums = [
        grad_out_bias,
        grad_gain_one,
        grad_shift_one,
        grad_in_bias,
        grad_down_bias,
        grad_gain_two,
        grad_shift_two,
    ]
    late_block = pack_rows([v.reshape(devices, -1) for v in late_sums], share).astype(BF)
    out_core = core_sum(
        jnp.concatenate([grad_out.reshape(devices, share, width), late_block], 2), me, devices
    )
    grad_mixed = times_transposed(grad_branch_one, wide_out).astype(BF)
    in_scatter = Scatter(jnp.concatenate([in_core, out_core], 2), me, devices, "split")
    (grad_mixed, grad_residual) = fence([down_scatter, in_scatter], grad_mixed, grad_residual)
    in_scatter.first()
    down_scatter.along_z()
    grad_packed, column_sums = attention_backward(packed, mask, logsum, grad_mixed, length)
    (grad_packed, column_sums) = fence([in_scatter, down_scatter], grad_packed, column_sums)
    in_scatter.second()
    grad_qkv = over_rows(flat, grad_packed).astype(BF)
    column_sums = kind_major(column_sums.reshape(kept, 3 * width).sum(0))
    early_sums = [column_sums[:width], column_sums[2 * width :]]
    early_block = pack_rows([v.reshape(devices, -1) for v in early_sums], share).astype(BF)
    grad_qkv = jnp.concatenate([grad_qkv.reshape(devices, share, 3 * width), early_block], 2)
    (grad_qkv, grad_packed) = fence([], grad_qkv, grad_packed)
    qkv_scatter = Scatter(core_sum(grad_qkv, me, devices), me, devices, "split")
    grad_inputs = (times_transposed(grad_packed, wide_qkv) + grad_residual).astype(BF)
    (grad_inputs,) = fence([in_scatter, qkv_scatter], grad_inputs)
    grad_inputs = ToPositions(
        grad_inputs.reshape(kept, members, local_len, width), members, devices
    )
    for k in near:
        grad_inputs.send(k)
    for k in far[:1]:
        grad_inputs.send(k)
    qkv_scatter.first()
    in_scatter.along_z()
    fence([qkv_scatter, grad_inputs])
    qkv_scatter.second()
    fence([qkv_scatter, grad_inputs, in_scatter])
    for k in far[1:]:
        grad_inputs.send(k)
    qkv_scatter.along_z()
    outputs.put([after(a, *qkv_scatter.held[:1]) for a in outputs.arrays()])
    outputs = outputs.finish(seat)
    in_part = in_scatter.result()
    down_part = down_scatter.result()
    (in_part, outputs) = fence([qkv_scatter, grad_inputs], in_part, outputs)
    qkv_part = qkv_scatter.result()
    grad_inputs = grad_inputs.finish(seat)
    early_out = unpack_rows(qkv_part[:, 3 * width :], [share, share])
    late_out = unpack_rows(
        in_part[:, inner_width + width :], [v.shape[0] for v in late_vectors]
    )
    return (
        outputs,
        grad_inputs,
        kind_major(qkv_part[:, : 3 * width]),
        early_out[0],
        early_out[1],
        in_part[:, inner_width : inner_width + width],
        late_out[0],
        late_out[1],
        late_out[2],
        in_part[:, :inner_width],
        late_out[3],
        down_part,
        late_out[4],
        late_out[5],
        late_out[6],
    )


def solution(mesh):
    placed = (
        P("dp", "seq", None),
        P("dp"),
        P(("dp", "seq"), None),
        P(("dp", "seq")),
        P(("dp", "seq")),
        P(("dp", "seq"), None),
        P(("dp", "seq")),
        P(("dp", "seq")),
        P(("dp", "seq")),
        P(("dp", "seq"), None),
        P(("dp", "seq")),
        P(("dp", "seq"), None),
        P(("dp", "seq")),
        P(("dp", "seq")),
        P(("dp", "seq")),
        P("dp", "seq", None),
    )
    return jax.shard_map(
        on_device,
        mesh=mesh,
        in_specs=placed,
        out_specs=(
            P("dp", "seq", None),
            P("dp", "seq", None),
            P(("dp", "seq"), None),
            P(("dp", "seq")),
            P(("dp", "seq")),
            P(("dp", "seq"), None),
            P(("dp", "seq")),
            P(("dp", "seq")),
            P(("dp", "seq")),
            P(("dp", "seq"), None),
            P(("dp", "seq")),
            P(("dp", "seq"), None),
            P(("dp", "seq")),
            P(("dp", "seq")),
            P(("dp", "seq")),
        ),
        check_vma=False,
    )
```

```python
import functools

import jax
import jax.numpy as jnp
from jax import lax
from jax.experimental import pallas as pl
from jax.experimental.pallas import tpu as pltpu
from jax.sharding import PartitionSpec as P

BF = jnp.bfloat16
F32 = jnp.float32
HD = 64
BOTH = ("dp", "seq")

def layer_norm(value, gain, shift):
    center = jnp.mean(value, -1, keepdims=True)
    centered = value - center
    spread = jnp.mean(centered * centered, -1, keepdims=True)
    return centered * lax.rsqrt(spread + 1e-12) * gain + shift


def over_rows(left, right):
    return lax.dot_general(
        left, right, (((0,), (0,)), ((), ())), preferred_element_type=jnp.float32
    )


def times_transposed(left, right):
    return lax.dot_general(
        left, right, (((1,), (1,)), ((), ())), preferred_element_type=jnp.float32
    )


def nt(a, b):
    return lax.dot_general(a, b, (((1,), (1,)), ((), ())), preferred_element_type=F32)


def tn(a, b):
    return lax.dot_general(a, b, (((0,), (0,)), ((), ())), preferred_element_type=F32)


def nn(a, b):
    return lax.dot_general(a, b, (((1,), (0,)), ((), ())), preferred_element_type=F32)


def masked_pair(q, k, bias, head, lane):
    mine = (lane >= head * HD) & (lane < (head + 1) * HD)
    spare = lane == (HD if head == 0 else 0)
    zero = jnp.zeros((), BF)
    qh = jnp.where(mine, q * BF(0.125), jnp.where(spare, jnp.ones((), BF), zero))
    kh = jnp.where(mine, k, jnp.where(spare, bias, zero))
    return qh, kh


def forward_kernel(packed_ref, mask_ref, mixed_ref, logsum_ref):
    count = packed_ref.shape[0]
    lane = lax.broadcasted_iota(jnp.int32, (count, 128), 1)
    q, k, v = (packed_ref[:, i * 128 : (i + 1) * 128] for i in range(3))
    bias = mask_ref[0]
    halves = []
    for h in range(2):
        qh, kh = masked_pair(q, k, bias, h, lane)
        scores = nt(kh, qh)
        top = jnp.max(scores, 0, keepdims=True)
        raised = jnp.exp(scores - top)
        total = jnp.sum(raised, 0, keepdims=True)
        mixed = tn(v[:, h * HD : (h + 1) * HD], raised.astype(BF))
        halves.append(mixed * (1.0 / total))
        logsum_ref[0, h : h + 1, :] = top + jnp.log(total)
    mixed_ref[...] = jnp.concatenate(halves, 0).T.astype(BF)


def backward_kernel(packed_ref, mask_ref, logsum_ref, grad_ref, out_ref, sums_ref):
    count = packed_ref.shape[0]
    lane = lax.broadcasted_iota(jnp.int32, (count, 128), 1)
    q, k, v = (packed_ref[:, i * 128 : (i + 1) * 128] for i in range(3))
    bias = mask_ref[0]
    grad = grad_ref[...]
    q_scaled, k_scaled = q * BF(0.125), k * BF(0.125)
    dq, dk, dv = [], [], []
    for h in range(2):
        qh, kh = masked_pair(q, k, bias, h, lane)
        mine = (lane >= h * HD) & (lane < (h + 1) * HD)
        vh = jnp.where(mine, v, jnp.zeros((), BF))
        probs = jnp.exp(nt(kh, qh) - logsum_ref[0, h : h + 1, :])
        grad_probs = nt(vh, grad)
        inner = jnp.sum(probs * grad_probs, 0, keepdims=True)
        grad_scores = (probs * (grad_probs - inner)).astype(BF)
        dv.append(nn(probs.astype(BF), grad))
        dk.append(nn(grad_scores, q_scaled))
        dq.append(tn(k_scaled[:, h * HD : (h + 1) * HD], grad_scores))
    low_half = lane < HD
    parts = (
        jnp.concatenate(dq, 0).T,
        jnp.where(low_half, dk[0], dk[1]),
        jnp.where(low_half, dv[0], dv[1]),
    )
    for i, part in enumerate(parts):
        rounded = part.astype(BF)
        out_ref[:, i * 128 : (i + 1) * 128] = rounded
        sums_ref[0, :, i * 128 : (i + 1) * 128] = jnp.sum(
            rounded.astype(F32), 0, keepdims=True
        )


def attention_specs(packed, length):
    rows, wide = packed.shape
    pairs, seqs = wide // 384, rows // length
    block = lambda size: pl.BlockSpec((length, size), lambda s, p: (s, p))
    mask = pl.BlockSpec((1, length, 128), lambda s, p: (s, 0, 0))
    row = lambda count, size: pl.BlockSpec((1, count, size), lambda s, p: (s * pairs + p, 0, 0))
    return rows, pairs, seqs, block, mask, row


def attention_forward(packed, mask, length):
    rows, pairs, seqs, block, mask_spec, row = attention_specs(packed, length)
    return pl.pallas_call(
        forward_kernel,
        grid=(seqs, pairs),
        in_specs=[block(384), mask_spec],
        out_specs=[block(128), row(2, length)],
        out_shape=[
            jax.ShapeDtypeStruct((rows, pairs * 128), BF),
            jax.ShapeDtypeStruct((seqs * pairs, 2, length), F32),
        ],
        compiler_params=pltpu.CompilerParams(vmem_limit_bytes=48 * 2**20),
        name="attention_forward",
        cost_estimate=pl.CostEstimate(
            flops=16 * rows * length * pairs * 128,
            bytes_accessed=rows * pairs * 1024,
            transcendentals=2 * rows * length * pairs,
        ),
    )(packed, mask)


def attention_backward(packed, mask, logsum, grad, length):
    rows, pairs, seqs, block, mask_spec, row = attention_specs(packed, length)
    return pl.pallas_call(
        backward_kernel,
        grid=(seqs, pairs),
        in_specs=[block(384), mask_spec, row(2, length), block(128)],
        out_specs=[block(384), row(1, 384)],
        out_shape=[
            jax.ShapeDtypeStruct((rows, pairs * 384), BF),
            jax.ShapeDtypeStruct((seqs * pairs, 1, 384), F32),
        ],
        compiler_params=pltpu.CompilerParams(vmem_limit_bytes=48 * 2**20),
        name="attention_backward",
        cost_estimate=pl.CostEstimate(
            flops=28 * rows * length * pairs * 128,
            bytes_accessed=rows * pairs * 1792,
            transcendentals=2 * rows * length * pairs,
        ),
    )(packed, mask, logsum, grad)


def pair_major(block):
    lead = block.shape[:-1]
    return block.reshape(lead + (3, -1, 128)).swapaxes(-3, -2).reshape(block.shape)


def kind_major(block):
    lead = block.shape[:-1]
    return block.reshape(lead + (-1, 3, 128)).swapaxes(-3, -2).reshape(block.shape)


def feed_forward_kernel(step, x_ref, w_ref, b_ref, active_ref, slope_ref):
    x = x_ref[...]
    for start in range(0, w_ref.shape[1], step):
        part = slice(start, start + step)
        hidden = nn(x, w_ref[:, part]) + b_ref[:, part]
        bell = jnp.exp(hidden * hidden * -0.5)
        share = 0.5 * (1.0 + lax.erf(hidden * 0.7071067811865476))
        active_ref[:, part] = (hidden * share).astype(BF)
        slope_ref[:, part] = (share + hidden * bell * 0.3989422804014327).astype(BF)


def feed_forward(x, weight, bias):
    rows, width = x.shape
    inner = weight.shape[1]
    block = 256
    out = jax.ShapeDtypeStruct((rows, inner), BF)
    return pl.pallas_call(
        functools.partial(feed_forward_kernel, 512),
        grid=(rows // block,),
        in_specs=[
            pl.BlockSpec((block, width), lambda i: (i, 0)),
            pl.BlockSpec((width, inner), lambda i: (0, 0)),
            pl.BlockSpec((1, inner), lambda i: (0, 0)),
        ],
        out_specs=[pl.BlockSpec((block, inner), lambda i: (i, 0))] * 2,
        out_shape=[out, out],
        compiler_params=pltpu.CompilerParams(vmem_limit_bytes=48 * 2**20),
        name="feed_forward",
        cost_estimate=pl.CostEstimate(
            flops=2 * rows * width * inner,
            bytes_accessed=4 * rows * inner + 2 * width * inner,
            transcendentals=2 * rows * inner,
        ),
    )(x, weight, bias)


def second_norm_kernel(
    active_ref, weight_ref, first_ref, cot_ref, rows_ref, out_ref, grad_ref, low_ref, sums_ref
):
    bias, gain, shift = rows_ref[0:1, :], rows_ref[1:2, :], rows_ref[2:3, :]
    value = first_ref[...].astype(F32) + (nn(active_ref[...], weight_ref[...]) + bias)
    centered = value - jnp.mean(value, -1, keepdims=True)
    scale = lax.rsqrt(jnp.mean(centered * centered, -1, keepdims=True) + 1e-12)
    normal = centered * scale
    out_ref[...] = (normal * gain + shift).astype(BF)
    cot = cot_ref[...].astype(F32)
    scaled = cot * gain
    inner = jnp.mean(scaled * normal, -1, keepdims=True)
    grad = scale * (scaled - jnp.mean(scaled, -1, keepdims=True) - normal * inner)
    low = grad.astype(BF)
    grad_ref[...] = grad
    low_ref[...] = low

    @pl.when(pl.program_id(0) == 0)
    def _():
        sums_ref[...] = jnp.zeros_like(sums_ref)

    sums_ref[0:1, :] += jnp.sum(low.astype(F32), 0, keepdims=True)
    sums_ref[1:2, :] += jnp.sum(cot * normal, 0, keepdims=True)
    sums_ref[2:3, :] += jnp.sum(cot, 0, keepdims=True)


def second_norm(active, weight, first, cot, bias, gain, shift):
    rows, inner = active.shape
    width = weight.shape[1]
    block = 256
    side = jnp.stack([bias, gain, shift] + [jnp.zeros_like(bias)] * 5)
    tile = lambda size: pl.BlockSpec((block, size), lambda i: (i, 0))
    whole = lambda count: pl.BlockSpec((count, width), lambda i: (0, 0))
    return pl.pallas_call(
        second_norm_kernel,
        grid=(rows // block,),
        in_specs=[tile(inner), whole(inner), tile(width), tile(width), whole(8)],
        out_specs=[tile(width), tile(width), tile(width), whole(8)],
        out_shape=[
            jax.ShapeDtypeStruct((rows, width), BF),
            jax.ShapeDtypeStruct((rows, width), F32),
            jax.ShapeDtypeStruct((rows, width), BF),
            jax.ShapeDtypeStruct((8, width), F32),
        ],
        compiler_params=pltpu.CompilerParams(vmem_limit_bytes=48 * 2**20),
        name="second_norm",
        cost_estimate=pl.CostEstimate(
            flops=2 * rows * width * inner,
            bytes_accessed=2 * (rows * inner + inner * width) + 12 * rows * width,
            transcendentals=rows,
        ),
    )(active, weight, first, cot, side)


def swap(block, distance, devices):
    return lax.ppermute(block, BOTH, [(i, i ^ distance) for i in range(devices)])


def after(value, *done):
    return lax.optimization_barrier((value,) + done)[0]


def place_kernel(ids, counts, spans, me_ref, *refs):
    pieces, rest = refs[: len(counts)], refs[len(counts) :]
    outs, sems = rest[: len(spans)], rest[len(spans)]
    me = me_ref[0]
    copies = []
    at = 0
    for piece, count in zip(pieces, counts):
        for j in range(count):
            spot = me ^ ids[at]
            for out, (start, size) in zip(outs, spans):
                source = piece.at[j] if len(spans) == 1 else piece.at[j, :, pl.ds(start, size)]
                copy = pltpu.make_async_copy(source, out.at[spot], sems.at[len(copies)])
                copy.start()
                copies.append(copy)
            at += 1
    for copy in copies:
        copy.wait()


def place(pieces, ids, me, spans=None):
    counts = [p.shape[0] for p in pieces]
    total = sum(counts)
    tail = pieces[0].shape[1:]
    spans = spans or [(0, tail[-1])]
    any_space = pl.BlockSpec(memory_space=pl.ANY)
    moved = 2 * sum(p.size * p.dtype.itemsize for p in pieces)
    return pl.pallas_call(
        functools.partial(place_kernel, ids, counts, spans),
        in_specs=[pl.BlockSpec(memory_space=pltpu.SMEM)] + [any_space] * len(pieces),
        out_specs=[pl.BlockSpec(memory_space=pltpu.VMEM)] * len(spans),
        out_shape=[
            jax.ShapeDtypeStruct((total,) + tail[:-1] + (size,), pieces[0].dtype)
            for _, size in spans
        ],
        scratch_shapes=[pltpu.SemaphoreType.DMA((total * len(spans),))],
        compiler_params=pltpu.CompilerParams(vmem_limit_bytes=32 * 2**20),
        cost_estimate=pl.CostEstimate(flops=0, bytes_accessed=moved, transcendentals=0),
        name="place_blocks",
    )(me.reshape(1), *pieces)


def pack_rows(vectors, share):
    lead = vectors[0].shape[:-1]
    columns = []
    for at in range(0, len(vectors), share):
        rows = []
        for v in vectors[at : at + share]:
            rows.append(jnp.pad(v, [(0, 0)] * len(lead) + [(0, 128 - v.shape[-1])]))
        block = jnp.stack(rows, -2)
        columns.append(
            jnp.pad(block, [(0, 0)] * len(lead) + [(0, share - len(rows)), (0, 0)])
        )
    return columns[0] if len(columns) == 1 else jnp.concatenate(columns, -1)


def unpack_rows(block, sizes):
    share = block.shape[-2]
    out = []
    for i, size in enumerate(sizes):
        start = i // share * 128
        out.append(block[..., i % share, start : start + size])
    return out


def fence(holders, *values):
    arrays = [a for h in holders for a in h.arrays()]
    kept = lax.optimization_barrier(tuple(arrays) + values)
    at = 0
    for h in holders:
        count = len(h.arrays())
        h.put(list(kept[at : at + count]))
        at += count
    return kept[at:]


class Gather:
    def __init__(self, block, me, devices, plan):
        self.me, self.devices, self.plan = me, devices, plan
        self.held, self.ids = [block[None]], [[0]]

    def arrays(self):
        return self.held

    def put(self, arrays):
        self.held = arrays

    def swapped(self, block, distance):
        return swap(block, distance, self.devices)

    def along_z(self):
        own, own_ids = self.held[0], self.ids[0]
        distance = 32
        while distance < self.devices:
            own = jnp.concatenate([own, self.swapped(own, distance)])
            own_ids = own_ids + [i ^ distance for i in own_ids]
            distance *= 2
        self.held = [own] + [self.swapped(own, 8 * k) for k in (1, 2, 3)]
        self.ids = [[i ^ (8 * k) for i in own_ids] for k in range(4)]

    def grow(self, order):
        held, ids = [], []
        for block, block_ids, distance in zip(self.held, self.ids, order):
            held += [block, self.swapped(block, distance)]
            ids += [block_ids, [i ^ distance for i in block_ids]]
        self.held, self.ids = held, ids

    def join(self, pairs):
        self.held = [jnp.concatenate([self.held[i] for i in p]) for p in pairs]
        self.ids = [[i for j in p for i in self.ids[j]] for p in pairs]

    def first(self):
        if self.plan == "split":
            self.join([(0, 1), (2, 3)])
            self.grow((4, 2))
        else:
            self.join([(0, 1, 2, 3)])
            self.grow((4,) if self.plan == "xy" else (2,))

    def second(self):
        if self.plan == "split":
            self.join([(0, 1), (2, 3)])
            self.grow((2, 4))
        else:
            self.join([(0, 1)])
            self.grow((2,) if self.plan == "xy" else (4,))

    def core(self, which=None):
        for i in which or range(len(self.held)):
            self.held.append(self.swapped(self.held[i], 1))
            self.ids.append([j ^ 1 for j in self.ids[i]])

    def finish(self, spans=None):
        return place(self.held, [i for ids in self.ids for i in ids], self.me, spans)


def pick(block, axis, index):
    return lax.dynamic_index_in_dim(block, index, axis, keepdims=False)


def fold(block, axis, me, distance, devices):
    digit = (me // distance) % 2
    got = swap(pick(block, axis, 1 - digit), distance, devices)
    return (pick(block, axis, digit).astype(F32) + got.astype(F32)).astype(BF)


def core_sum(total, me, devices):
    tail = total.shape[1:]
    distance = devices // 2
    while distance >= 32:
        total = fold(total.reshape((2, distance) + tail), 0, me, distance, devices)
        distance //= 2
    return fold(total.reshape((16, 2) + tail), 1, me, 1, devices)


class Scatter:
    def __init__(self, total, me, devices, plan):
        self.me, self.devices, self.plan = me, devices, plan
        self.tail = total.shape[1:]
        self.held = [total]

    def arrays(self):
        return self.held

    def put(self, arrays):
        self.held = arrays

    def fold(self, block, axis, distance):
        return fold(block, axis, self.me, distance, self.devices)

    def first(self):
        total = self.held[0].reshape((4, 2, 2) + self.tail)
        if self.plan == "split":
            z = (self.me // 8) % 4
            halves = total.reshape((2, 2, 2, 2) + self.tail)
            self.held = [
                self.fold(pick(halves, 0, z // 2), 1, 4),
                self.fold(pick(halves, 0, 1 - z // 2), 2, 2),
            ]
        elif self.plan == "xy":
            self.held = [self.fold(total, 1, 4)]
        else:
            self.held = [self.fold(total, 2, 2)]

    def second(self):
        z = (self.me // 8) % 4
        if self.plan == "split":
            near = self.fold(self.held[0], 1, 2)
            away = self.fold(self.held[1], 1, 4)
            odd = z % 2
            self.held = [
                pick(near, 0, odd),
                pick(near, 0, 1 - odd),
                pick(away, 0, odd),
                pick(away, 0, 1 - odd),
            ]
        else:
            total = self.fold(self.held[0], 1, 2 if self.plan == "xy" else 4)
            self.held = [pick(total, 0, z ^ k) for k in range(4)]

    def along_z(self):
        sent = [swap(self.held[k], 8 * k, self.devices) for k in (1, 2, 3)]
        self.held = [self.held[0]] + sent

    def result(self):
        return sum(block.astype(F32) for block in self.held)


class ToSequences:
    def __init__(self, block, seat, members, devices):
        groups, count, width = block.shape
        parts = block.reshape(members, groups // members, count, width)
        self.devices = devices
        self.held = [pick(parts, 0, seat ^ k) for k in range(members)]

    def arrays(self):
        return self.held

    def put(self, arrays):
        self.held = arrays

    def send(self, k):
        self.held[k] = swap(self.held[k], k, self.devices)

    def finish(self):
        return jnp.stack(self.held, 1).reshape(-1, self.held[0].shape[-1])


class ToPositions:
    def __init__(self, block, members, devices):
        self.devices = devices
        self.held = [block[:, k][None] for k in range(members)]

    def arrays(self):
        return self.held

    def put(self, arrays):
        self.held = arrays

    def send(self, k):
        self.held[k] = swap(self.held[k], k, self.devices)

    def finish(self, seat):
        (placed,) = place(self.held, list(range(len(self.held))), seat)
        return placed.reshape((-1,) + placed.shape[2:])


def on_device(
    inputs,
    lengths,
    query_key_value_weight,
    query_bias,
    value_bias,
    output_weight,
    output_bias,
    norm1_gain,
    norm1_shift,
    in_weight,
    in_bias,
    down_weight,
    down_bias,
    norm2_gain,
    norm2_shift,
    cotangent,
):
    groups, local_len, width = inputs.shape
    rows = groups * local_len
    members = lax.axis_size("seq")
    devices = lax.axis_size("dp") * members
    kept = groups // members
    length = local_len * members
    seat = lax.axis_index("seq")
    me = lax.axis_index("dp") * members + seat
    share = query_key_value_weight.shape[0]
    inner_width = in_weight.shape[1]
    early = pack_rows([query_bias, value_bias], share)
    qkv_gather = Gather(
        jnp.concatenate([pair_major(query_key_value_weight), early], 1), me, devices, "split"
    )
    late_vectors = [
        output_bias,
        norm1_gain,
        norm1_shift,
        in_bias,
        down_bias,
        norm2_gain,
        norm2_shift,
    ]
    late = pack_rows(late_vectors, share)
    in_gather = Gather(
        jnp.concatenate([in_weight, output_weight, late], 1), me, devices, "split"
    )
    down_gather = Gather(down_weight, me, devices, "split")
    near, far = range(1, (members + 1) // 2), range((members + 1) // 2, members)
    flat = ToSequences(inputs, seat, members, devices)
    for k in range(1, members):
        flat.send(k)
    qkv_gather.along_z()
    fence([qkv_gather])
    qkv_gather.first()
    in_gather.put([after(a, qkv_gather.held[1]) for a in in_gather.arrays()])
    in_gather.along_z()
    in_gather.held[:2] = fence([qkv_gather, flat], *in_gather.held[:2])
    qkv_gather.second()
    fence([qkv_gather, in_gather])
    qkv_gather.core()
    fence([qkv_gather])
    in_gather.first()
    flat = flat.finish()
    wide_qkv, early = qkv_gather.finish([(0, 3 * width), (3 * width, early.shape[1])])
    (wide_qkv, early, flat) = fence([in_gather], wide_qkv, early, flat)
    in_gather.second()
    wide_qkv = wide_qkv.reshape(width, 3 * width)
    full_query_bias, full_value_bias = [
        v.reshape(-1).astype(F32) for v in unpack_rows(early, [share, share])
    ]
    bias_vector = jnp.concatenate([full_query_bias, jnp.zeros((width,), F32), full_value_bias])
    packed = jnp.dot(flat, wide_qkv, preferred_element_type=F32) + pair_major(bias_vector)
    packed = packed.astype(BF)
    (packed,) = fence([], packed)
    down_gather.put([after(a, packed) for a in down_gather.arrays()])
    down_gather.along_z()
    mine = lax.dynamic_slice(lengths, (seat * kept,), (kept,))
    slots = jnp.arange(length, dtype=jnp.int32)
    positions = ((slots // local_len) ^ seat) * local_len + slots % local_len
    mask = jnp.where(positions[None, :] < mine[:, None], 0.0, -1e30).astype(BF)
    mask = jnp.broadcast_to(mask[:, :, None], (kept, length, 128))
    mixed, logsum = attention_forward(packed, mask, length)
    (mixed, logsum, packed) = fence([in_gather, down_gather], mixed, logsum, packed)
    in_gather.core()
    down_gather.first()
    fence([in_gather])
    wide_in, wide_out, late = in_gather.finish(
        [(0, inner_width), (inner_width, width), (inner_width + width, late.shape[1])]
    )
    (wide_in, wide_out, late) = fence([down_gather], wide_in, wide_out, late)
    down_gather.second()
    down_gather.core((0, 2))
    wide_in = wide_in.reshape(width, inner_width)
    wide_out = wide_out.reshape(width, width)
    (
        full_out_bias,
        gain_one,
        shift_one,
        full_in_bias,
        full_down_bias,
        gain_two,
        shift_two,
    ) = [
        v.reshape(-1).astype(F32)
        for v in unpack_rows(late, [v.shape[0] for v in late_vectors])
    ]
    attention_branch = jnp.dot(mixed, wide_out, preferred_element_type=F32) + full_out_bias
    first, norm_one_pull = jax.vjp(
        layer_norm, flat.astype(F32) + attention_branch, gain_one, shift_one
    )
    first_low = first.astype(BF)
    (first_low,) = fence([down_gather], first_low)
    down_gather.core((1, 3))
    cot = ToSequences(after(cotangent, first_low), seat, members, devices)
    for k in range(1, members):
        cot.send(k)
    active_low, slope = feed_forward(first_low, wide_in, full_in_bias[None])
    (active_low, slope) = fence([down_gather, cot], active_low, slope)
    (wide_down,) = down_gather.finish()
    wide_down = wide_down.reshape(inner_width, width)
    outputs, grad_second, grad_branch_two, norm_sums = second_norm(
        active_low, wide_down, first_low, cot.finish(), full_down_bias, gain_two, shift_two
    )
    (outputs, grad_second, grad_branch_two, norm_sums) = fence(
        [], outputs, grad_second, grad_branch_two, norm_sums
    )
    outputs = outputs.reshape(kept, members, local_len, width)
    grad_down_bias, grad_gain_two, grad_shift_two = (norm_sums[i] for i in range(3))
    outputs = ToPositions(outputs, members, devices)
    for k in near:
        outputs.send(k)
    for k in far[:1]:
        outputs.send(k)
    grad_down = over_rows(active_low, grad_branch_two).astype(BF)
    (grad_down, grad_branch_two) = fence([outputs], grad_down, grad_branch_two)
    for k in far[1:]:
        outputs.send(k)
    down_scatter = Scatter(
        core_sum(grad_down.reshape(devices, -1, width), me, devices), me, devices, "split"
    )
    grad_hidden_low = (
        times_transposed(grad_branch_two, wide_down) * slope.astype(F32)
    ).astype(BF)
    grad_in_bias = jnp.sum(grad_hidden_low.astype(F32), 0)
    (grad_hidden_low, grad_in_bias) = fence([outputs, down_scatter], grad_hidden_low, grad_in_bias)
    down_scatter.first()
    grad_in = over_rows(first_low, grad_hidden_low).astype(BF)
    (grad_in, grad_hidden_low) = fence([down_scatter], grad_in, grad_hidden_low)
    down_scatter.second()
    in_core = core_sum(grad_in.reshape(devices, share, inner_width), me, devices)
    grad_first = times_transposed(grad_hidden_low, wide_in) + grad_second
    grad_residual, grad_gain_one, grad_shift_one = norm_one_pull(grad_first)
    grad_branch_one = grad_residual.astype(BF)
    grad_out_bias = jnp.sum(grad_branch_one.astype(F32), 0)
    grad_out = over_rows(mixed, grad_branch_one).astype(BF)
    late_sums = [
        grad_out_bias,
        grad_gain_one,
        grad_shift_one,
        grad_in_bias,
        grad_down_bias,
        grad_gain_two,
        grad_shift_two,
    ]
    late_block = pack_rows([v.reshape(devices, -1) for v in late_sums], share).astype(BF)
    out_core = core_sum(
        jnp.concatenate([grad_out.reshape(devices, share, width), late_block], 2), me, devices
    )
    grad_mixed = times_transposed(grad_branch_one, wide_out).astype(BF)
    in_scatter = Scatter(jnp.concatenate([in_core, out_core], 2), me, devices, "split")
    (grad_mixed, grad_residual) = fence([down_scatter, in_scatter], grad_mixed, grad_residual)
    in_scatter.first()
    down_scatter.along_z()
    grad_packed, column_sums = attention_backward(packed, mask, logsum, grad_mixed, length)
    (grad_packed, column_sums) = fence([in_scatter, down_scatter], grad_packed, column_sums)
    in_scatter.second()
    grad_qkv = over_rows(flat, grad_packed).astype(BF)
    column_sums = kind_major(column_sums.reshape(kept, 3 * width).sum(0))
    early_sums = [column_sums[:width], column_sums[2 * width :]]
    early_block = pack_rows([v.reshape(devices, -1) for v in early_sums], share).astype(BF)
    grad_qkv = jnp.concatenate([grad_qkv.reshape(devices, share, 3 * width), early_block], 2)
    (grad_qkv, grad_packed) = fence([], grad_qkv, grad_packed)
    qkv_scatter = Scatter(core_sum(grad_qkv, me, devices), me, devices, "split")
    grad_inputs = (times_transposed(grad_packed, wide_qkv) + grad_residual).astype(BF)
    (grad_inputs,) = fence([in_scatter, qkv_scatter], grad_inputs)
    grad_inputs = ToPositions(
        grad_inputs.reshape(kept, members, local_len, width), members, devices
    )
    for k in near:
        grad_inputs.send(k)
    for k in far[:1]:
        grad_inputs.send(k)
    qkv_scatter.first()
    in_scatter.along_z()
    fence([qkv_scatter, grad_inputs])
    qkv_scatter.second()
    fence([qkv_scatter, grad_inputs, in_scatter])
    for k in far[1:]:
        grad_inputs.send(k)
    qkv_scatter.along_z()
    outputs.put([after(a, *qkv_scatter.held[:1]) for a in outputs.arrays()])
    outputs = outputs.finish(seat)
    in_part = in_scatter.result()
    down_part = down_scatter.result()
    (in_part, outputs) = fence([qkv_scatter, grad_inputs], in_part, outputs)
    qkv_part = qkv_scatter.result()
    grad_inputs = grad_inputs.finish(seat)
    early_out = unpack_rows(qkv_part[:, 3 * width :], [share, share])
    late_out = unpack_rows(
        in_part[:, inner_width + width :], [v.shape[0] for v in late_vectors]
    )
    return (
        outputs,
        grad_inputs,
        kind_major(qkv_part[:, : 3 * width]),
        early_out[0],
        early_out[1],
        in_part[:, inner_width : inner_width + width],
        late_out[0],
        late_out[1],
        late_out[2],
        in_part[:, :inner_width],
        late_out[3],
        down_part,
        late_out[4],
        late_out[5],
        late_out[6],
    )


def solution(mesh):
    placed = (
        P("dp", "seq", None),
        P("dp"),
        P(("dp", "seq"), None),
        P(("dp", "seq")),
        P(("dp", "seq")),
        P(("dp", "seq"), None),
        P(("dp", "seq")),
        P(("dp", "seq")),
        P(("dp", "seq")),
        P(("dp", "seq"), None),
        P(("dp", "seq")),
        P(("dp", "seq"), None),
        P(("dp", "seq")),
        P(("dp", "seq")),
        P(("dp", "seq")),
        P("dp", "seq", None),
    )
    return jax.shard_map(
        on_device,
        mesh=mesh,
        in_specs=placed,
        out_specs=(
            P("dp", "seq", None),
            P("dp", "seq", None),
            P(("dp", "seq"), None),
            P(("dp", "seq")),
            P(("dp", "seq")),
            P(("dp", "seq"), None),
            P(("dp", "seq")),
            P(("dp", "seq")),
            P(("dp", "seq")),
            P(("dp", "seq"), None),
            P(("dp", "seq")),
            P(("dp", "seq"), None),
            P(("dp", "seq")),
            P(("dp", "seq")),
            P(("dp", "seq")),
        ),
        check_vma=False,
    )
```
